32 devices in a mesh: pipe: 4 (over y, x), ctx: 8 (over z, core).
Axes of the slice: x: 2, y: 2, z: 4, core: 2. Of those that a mesh axis runs over, the one named last changes fastest.
Arguments:
- queries: bfloat16 [4, 2048, 2048], P('pipe', 'ctx'), may hold values from -70 to 70
- key_rows: bfloat16 [4, 2048, 512], P('pipe', 'ctx'), may hold values from -6 to 6
- value_rows: bfloat16 [4, 2048, 512], P('pipe', 'ctx'), may hold values from -6 to 6
- out_grad: bfloat16 [4, 2048, 2048], P('pipe', 'ctx'), may hold values from -6 to 6
- doc_blocks: int32 [4, 16], P('pipe'), may hold values from 0 to 3, never falling along the last dimension, each value on 1 to 8 neighbouring positions
Outputs:
- attn_out: bfloat16 [4, 2048, 2048], P('pipe', 'ctx')
- grad_query: bfloat16 [4, 2048, 2048], P('pipe', 'ctx')
- grad_key: bfloat16 [4, 2048, 512], P('pipe', 'ctx')
- grad_value: bfloat16 [4, 2048, 512], P('pipe', 'ctx')
The draws below stay inside these ranges and needn't reach their ends.
Inputs may be any that keep to these rules, and one draw needn't show every extreme that they name: `doc_blocks`: each document is a run of 1 to 8 consecutive blocks; ids never fall along a section's sequence, and in each section some document has exactly 8 blocks.
All inputs are finite; a program needn't handle non-finite values.
Results may differ from the reference program's by a relative error of at most 0.014.
Values may be sent and summed in bfloat16 or wider, within the bound.
No kernel may reach another device: no remote copies, remote signals or barrier semaphores. Data moves between devices by JAX's collectives and lax.ppermute only.
A program may use at most 64 MiB of HBM per device.

```python
import math
import jax
import jax.numpy as jnp
import numpy as np
from jax import lax

HD = 128
H = 16
KVH = 4
BLK = 128
MOST_BLK = 8
TOK_DEV = 256
SECTIONS = 4
SEQ = 2048
NBLK = 16
REACH = 4


def joint_draw(base_key):
    query_source = jax.random.fold_in(base_key, 101)
    key_source = jax.random.fold_in(base_key, 202)
    group_size = H // KVH
    query_shape = (SECTIONS, SEQ, KVH, group_size, HD)
    key_shape = (SECTIONS, SEQ, KVH, HD)
    query_draw = jax.random.truncated_normal(query_source, -6.0, 6.0, query_shape, jnp.float32)
    key_draw = jax.random.truncated_normal(key_source, -6.0, 6.0, key_shape, jnp.float32)
    return (query_draw.reshape(SECTIONS, SEQ, H * HD), key_draw.reshape(SECTIONS, SEQ, KVH * HD))


def draw_queries(key, part):
    return joint_draw(key)[0].astype(jnp.bfloat16)


def draw_key_rows(key, part):
    return joint_draw(key)[1].astype(jnp.bfloat16)


def block_levels(own_key, extent, shards, least, top_value):
    level, own = 1.0, jax.random.fold_in(own_key, 6)
    for position, shards_of in shards:
        draws = jnp.exp(jax.random.uniform(jax.random.fold_in(own, position), (shards_of,), jnp.float32, least / len(shards), top_value / len(shards)))
        level = level * jnp.repeat(draws, extent[position] // shards_of).reshape([-1 if axis == position else 1 for axis in range(len(extent))])
    return level


def profile(number_of, total, limit, lean):
    weights = [(1 << 20) // math.isqrt(standing ** lean) + 1 for standing in range(2, number_of + 1)]
    spare, holding = total - limit - (number_of - 1), [1] * (number_of - 1)
    while spare > 0:
        movable = [i for i in range(number_of - 1) if holding[i] < limit]
        whole, budget = sum([weights[i] for i in movable]), spare
        for i in movable:
            more = min(limit - holding[i], max(1, budget * weights[i] // whole), spare)
            holding[i] = holding[i] + more
            spare = spare - more
    return np.array([limit] + holding)


def uneven_parts(own_key, amount, total, reach, lean):
    if amount == 2:
        one = jax.random.randint(own_key, (), max(1, total - reach), min(reach, total - 1) + 1)
        return jnp.stack([one, total - one])
    tallies = jnp.asarray(profile(amount, total, reach, lean), jnp.int32)
    couples = (amount - 1) // 2
    donor, receiver = tallies[1:1 + 2 * couples:2], tallies[2:2 + 2 * couples:2]
    slack = jnp.minimum(donor - 1, reach - receiver)
    passed = jax.random.randint(jax.random.fold_in(own_key, 1), (couples,), 0, 1 << 20) % (slack + 1)
    tallies = tallies.at[1:1 + 2 * couples:2].set(donor - passed).at[2:2 + 2 * couples:2].set(receiver + passed)
    return tallies[jax.random.permutation(jax.random.fold_in(own_key, 2), amount)]


def scatter_about(rng, shape, deviation, most, pieces=(), held_as=jnp.bfloat16):
    factor_of = block_levels(rng, shape, pieces, -0.22, 0.18) if pieces else 1.0
    array = jax.random.normal(rng, shape, jnp.float32) * deviation * factor_of
    return jnp.minimum(jnp.maximum(array, -most), most).astype(held_as)


def setup_inputs(seed: int = 0) -> dict:
    seeds = jax.random.split(jax.random.key(seed), 6)
    queries = draw_queries(jax.random.fold_in(seeds[5], 71), 0)
    key_rows = draw_key_rows(jax.random.fold_in(seeds[5], 71), 0)
    value_rows = scatter_about(seeds[2], (SECTIONS, SEQ, KVH * HD), 1.0, 6.0, ((0, 4), (1, 8)))
    out_grad = scatter_about(seeds[3], (SECTIONS, SEQ, H * HD), 1.0, 6.0, ((0, 4), (1, 8)))
    doc_blocks = jax.vmap(lambda own: jnp.searchsorted(jnp.cumsum(uneven_parts(own, NBLK // 4, NBLK, MOST_BLK, 1)), jnp.arange(NBLK), side="right"))(jax.random.split(seeds[4], SECTIONS)).reshape((SECTIONS, NBLK)).astype(jnp.int32)
    return dict(queries=queries, key_rows=key_rows, value_rows=value_rows, out_grad=out_grad, doc_blocks=doc_blocks)


def low_round(values_in):
    return lax.optimization_barrier(values_in.astype(jnp.bfloat16)).astype(jnp.float32)

def one_section(inputs):
    queries, key_rows, value_rows, out_grad, doc_row = inputs
    group_size = H // KVH
    window = MOST_BLK * BLK
    block_count = SEQ // BLK
    score_scale = 1.0 / math.sqrt(HD)
    query_full = queries.astype(jnp.float32).reshape(SEQ, KVH, group_size, HD)
    grad_full = out_grad.astype(jnp.float32).reshape(SEQ, KVH, group_size, HD)
    key_full = key_rows.astype(jnp.float32).reshape(SEQ, KVH, HD)
    value_full = value_rows.astype(jnp.float32).reshape(SEQ, KVH, HD)
    pad_rows = window - BLK
    key_pad = jnp.concatenate([jnp.zeros((pad_rows, KVH, HD), jnp.float32), key_full], 0)
    value_pad = jnp.concatenate([jnp.zeros((pad_rows, KVH, HD), jnp.float32), value_full], 0)
    doc_front = jnp.concatenate([jnp.full((MOST_BLK - 1,), -1, jnp.int32), doc_row.astype(jnp.int32)], 0)

    def query_block(block):
        offset = (block * BLK).astype(jnp.int32)
        query_here = lax.dynamic_slice_in_dim(query_full, offset, BLK, 0)
        grad_here = lax.dynamic_slice_in_dim(grad_full, offset, BLK, 0)
        key_window = lax.dynamic_slice_in_dim(key_pad, offset, window, 0)
        value_window = lax.dynamic_slice_in_dim(value_pad, offset, window, 0)
        key_doc = jnp.repeat(lax.dynamic_slice_in_dim(doc_front, block.astype(jnp.int32), MOST_BLK, 0), BLK)
        key_pos = offset - pad_rows + jnp.arange(window, dtype=jnp.int32)
        query_pos = offset + jnp.arange(BLK, dtype=jnp.int32)
        query_doc = lax.dynamic_slice_in_dim(doc_row.astype(jnp.int32), block.astype(jnp.int32), 1, 0)[0]
        visible = (key_doc[None, :] == query_doc) & (key_pos[None, :] <= query_pos[:, None])
        scores = jnp.einsum('tgcd,kgd->gctk', query_here, key_window) * score_scale
        masked = jnp.where(visible, scores, -1e+30)
        maxima = lax.optimization_barrier(jnp.max(masked, axis=-1))
        totals = lax.optimization_barrier(jnp.sum(jnp.where(visible, jnp.exp(masked - maxima[..., None]), 0.0), axis=-1))
        log_norm = maxima + jnp.log(totals)
        probs = jnp.where(visible, jnp.exp(scores - log_norm[..., None]), 0.0)
        probs_low = low_round(probs)
        output = jnp.einsum('gctk,kgd->tgcd', probs_low, value_window)
        out_low = output.astype(jnp.bfloat16)
        row_dots = jnp.einsum('tgcd,tgcd->gct', grad_here, lax.optimization_barrier(out_low).astype(jnp.float32))
        prob_grad = jnp.einsum('tgcd,kgd->gctk', grad_here, value_window)
        score_grad = low_round(probs * (prob_grad - row_dots[..., None]))
        query_grad = jnp.einsum('gctk,kgd->tgcd', score_grad, key_window) * score_scale
        return (out_low, query_grad.astype(jnp.bfloat16), log_norm, row_dots)
    out_blocks, query_blocks, norm_blocks, dot_blocks = lax.map(query_block, jnp.arange(block_count, dtype=jnp.int32))
    attn_out = out_blocks.reshape(SEQ, H * HD)
    query_grad = query_blocks.reshape(SEQ, H * HD)
    log_norm = norm_blocks.transpose(1, 2, 0, 3).reshape(KVH, group_size, SEQ)
    row_dots = dot_blocks.transpose(1, 2, 0, 3).reshape(KVH, group_size, SEQ)
    query_back = jnp.concatenate([query_full, jnp.zeros((pad_rows, KVH, group_size, HD), jnp.float32)], 0)
    grad_back = jnp.concatenate([grad_full, jnp.zeros((pad_rows, KVH, group_size, HD), jnp.float32)], 0)
    norm_back = jnp.concatenate([log_norm, jnp.zeros((KVH, group_size, pad_rows), jnp.float32)], 2)
    dots_back = jnp.concatenate([row_dots, jnp.zeros((KVH, group_size, pad_rows), jnp.float32)], 2)
    doc_back = jnp.concatenate([doc_row.astype(jnp.int32), jnp.full((MOST_BLK - 1,), -2, jnp.int32)], 0)

    def key_block(block):
        offset = (block * BLK).astype(jnp.int32)
        key_here = lax.dynamic_slice_in_dim(key_full, offset, BLK, 0)
        value_here = lax.dynamic_slice_in_dim(value_full, offset, BLK, 0)
        query_window = lax.dynamic_slice_in_dim(query_back, offset, window, 0)
        grad_window = lax.dynamic_slice_in_dim(grad_back, offset, window, 0)
        norm_window = lax.dynamic_slice_in_dim(norm_back, offset, window, 2)
        dots_window = lax.dynamic_slice_in_dim(dots_back, offset, window, 2)
        query_doc = jnp.repeat(lax.dynamic_slice_in_dim(doc_back, block.astype(jnp.int32), MOST_BLK, 0), BLK)
        key_doc = lax.dynamic_slice_in_dim(doc_row.astype(jnp.int32), block.astype(jnp.int32), 1, 0)[0]
        query_pos = offset + jnp.arange(window, dtype=jnp.int32)
        key_pos = offset + jnp.arange(BLK, dtype=jnp.int32)
        visible = (query_doc[:, None] == key_doc) & (key_pos[None, :] <= query_pos[:, None])
        scores = jnp.einsum('tgcd,kgd->gctk', query_window, key_here) * score_scale
        probs = jnp.where(visible, jnp.exp(scores - norm_window[..., None]), 0.0)
        probs_low = low_round(probs)
        prob_grad = jnp.einsum('tgcd,kgd->gctk', grad_window, value_here)
        score_grad = low_round(probs * (prob_grad - dots_window[..., None]))
        key_shard = offset // TOK_DEV
        query_shard = query_pos // TOK_DEV
        key_grad = jnp.zeros((BLK, KVH, HD), jnp.float32)
        value_grad = jnp.zeros((BLK, KVH, HD), jnp.float32)
        for distance in range(REACH + 1):
            pick = (query_shard == key_shard + distance)[None, None, :, None]
            key_term = jnp.einsum('gctk,tgcd->kgd', jnp.where(pick, score_grad, 0.0), query_window) * score_scale
            value_term = jnp.einsum('gctk,tgcd->kgd', jnp.where(pick, probs_low, 0.0), grad_window)
            if distance > 0:
                key_term = low_round(key_term)
                value_term = low_round(value_term)
            key_grad = key_grad + key_term
            value_grad = value_grad + value_term
        return (key_grad.astype(jnp.bfloat16), value_grad.astype(jnp.bfloat16))
    key_blocks, value_blocks = lax.map(key_block, jnp.arange(block_count, dtype=jnp.int32))
    key_grad = key_blocks.reshape(SEQ, KVH * HD)
    value_grad = value_blocks.reshape(SEQ, KVH * HD)
    return (attn_out, query_grad, key_grad, value_grad)

def to_previous(stacked):
    return jnp.concatenate([stacked[1:], jnp.zeros_like(stacked[:1])], 0)

def reference(queries, key_rows, value_rows, out_grad, doc_blocks):
    attn_out, query_grad, key_grad, value_grad = lax.map(one_section, (queries, key_rows, value_rows, out_grad, doc_blocks))
    return (attn_out, to_previous(query_grad), to_previous(key_grad), to_previous(value_grad))
```

```python
import functools
import math

import jax
import jax.numpy as jnp
from jax import lax
from jax.experimental import pallas as pl
from jax.experimental.pallas import tpu as pltpu
from jax.sharding import PartitionSpec as P

HD = 128
H = 16
KVH = 4
BLK = 128
MOST_BLK = 8

GROUP = H // KVH
HALF = KVH // 2
QW = GROUP * HD
KV2 = 2 * HD
SCALE = 1.0 / math.sqrt(HD)
LOG2E = math.log2(math.e)
CHUNKS = ((0,), (1,))

BF = jnp.bfloat16
F32 = jnp.float32
ANY = pl.BlockSpec(memory_space=pl.ANY)
VMEM = pl.BlockSpec(memory_space=pltpu.VMEM)
SMEM = pl.BlockSpec(memory_space=pltpu.SMEM)


def shape(rows, cols, dtype=BF):
    return jax.ShapeDtypeStruct((rows, cols), dtype)


def cols(start, size):
    return pl.ds(pl.multiple_of(start, HD), size)


def rows(start, size):
    return pl.ds(pl.multiple_of(start, BLK), size)


def pack_kv_kernel(k_ref, v_ref, *outs):
    core = lax.rem(lax.axis_index("ctx"), 2)
    for n, heads in enumerate(CHUNKS):
        for out, half in ((outs[2 * n], core), (outs[2 * n + 1], 1 - core)):
            for at, head in enumerate(heads):
                src = cols((half * HALF + head) * HD, HD)
                out[:, at * KV2:at * KV2 + HD] = k_ref[:, src]
                out[:, at * KV2 + HD:(at + 1) * KV2] = v_ref[:, src]


def pack_kv(keys, values):
    tokens = keys.shape[0]
    return pl.pallas_call(
        pack_kv_kernel,
        name="pack_kv",
        out_shape=[shape(tokens, len(heads) * KV2) for heads in CHUNKS for _ in range(2)],
        in_specs=[VMEM, VMEM],
        out_specs=[VMEM] * (2 * len(CHUNKS)),
        cost_estimate=pl.CostEstimate(flops=0, bytes_accessed=4 * keys.size * 2, transcendentals=0),
    )(keys, values)


def pack_pair_kernel(q_ref, g_ref, *rest):
    kv_refs, out, sems = rest[:-2], rest[-2], rest[-1]
    core = lax.rem(lax.axis_index("ctx"), 2)
    wide = HALF * QW
    src = cols((1 - core) * wide, wide)
    copies = [
        pltpu.make_async_copy(q_ref.at[:, src], out.at[:, pl.ds(0, wide)], sems.at[0]),
        pltpu.make_async_copy(g_ref.at[:, src], out.at[:, pl.ds(wide, wide)], sems.at[1]),
    ]
    at = 2 * wide
    for n, kv_ref in enumerate(kv_refs):
        width = kv_ref.shape[1]
        copies.append(pltpu.make_async_copy(kv_ref, out.at[:, pl.ds(at, width)], sems.at[2 + n]))
        at += width
    for copy in copies:
        copy.start()
    for copy in copies:
        copy.wait()


def pack_pair(queries, grads, kvs):
    tokens = queries.shape[0]
    width = 2 * HALF * QW + sum(kv.shape[1] for kv in kvs)
    return pl.pallas_call(
        pack_pair_kernel,
        name="pack_pair",
        out_shape=shape(tokens, width),
        in_specs=[ANY] * (2 + len(kvs)),
        out_specs=ANY,
        scratch_shapes=[pltpu.SemaphoreType.DMA((2 + len(kvs),))],
        cost_estimate=pl.CostEstimate(flops=0, bytes_accessed=4 * tokens * width, transcendentals=0),
    )(queries, grads, *kvs)


def relay_kernel(a_ref, b_ref, out):
    core = lax.rem(lax.axis_index("ctx"), 2)
    tokens = a_ref.shape[0]
    trim = tokens - BLK

    def lay(first, second):
        out[:trim, :] = first[BLK:, :]
        out[trim:, :] = second[...]

    pl.when(core == 0)(lambda: lay(a_ref, b_ref))
    pl.when(core == 1)(lambda: lay(b_ref, a_ref))


def relay(straight, crossed):
    tokens, width = straight.shape
    return pl.pallas_call(
        relay_kernel,
        name="relay",
        out_shape=shape(2 * tokens - BLK, width),
        in_specs=[VMEM, VMEM],
        out_specs=VMEM,
        cost_estimate=pl.CostEstimate(flops=0, bytes_accessed=8 * tokens * width, transcendentals=0),
    )(straight, crossed)


def add_middle_kernel(own_ref, got_ref, out):
    out[:BLK, :] = own_ref[:BLK, :].astype(BF)
    out[BLK:, :] = (own_ref[BLK:, :] + got_ref[...].astype(F32)).astype(BF)


def add_middle(own, got):
    return pl.pallas_call(
        add_middle_kernel,
        name="add_middle",
        out_shape=shape(*own.shape),
        in_specs=[VMEM, VMEM],
        out_specs=VMEM,
        cost_estimate=pl.CostEstimate(flops=own.size, bytes_accessed=8 * own.size, transcendentals=0),
    )(own, got)


def add_last_kernel(own_ref, got_ref, straight, crossed):
    core = lax.rem(lax.axis_index("ctx"), 2)
    tokens = straight.shape[0]
    for out, shard in ((straight, core), (crossed, 1 - core)):
        at = rows(shard * tokens, tokens)
        out[...] = (own_ref[at, :] + got_ref[at, :].astype(F32)).astype(BF)


def add_last(own, got):
    tokens, width = own.shape[0] // 2, own.shape[1]
    return pl.pallas_call(
        add_last_kernel,
        name="add_last",
        out_shape=[shape(tokens, width)] * 2,
        in_specs=[VMEM, VMEM],
        out_specs=[VMEM, VMEM],
        cost_estimate=pl.CostEstimate(flops=own.size, bytes_accessed=8 * own.size, transcendentals=0),
    )(own, got)


def lay_heads_kernel(*refs):
    parts, out, sems = refs[:-2], refs[-2], refs[-1]
    core = lax.rem(lax.axis_index("ctx"), 2)
    copies = []
    for n, heads in enumerate(CHUNKS):
        for m, half in ((0, core), (1, 1 - core)):
            src = parts[2 * n + m]
            dst = out.at[:, cols((half * HALF + heads[0]) * QW, len(heads) * QW)]
            copies.append(pltpu.make_async_copy(src, dst, sems.at[2 * n + m]))
    for copy in copies:
        copy.start()
    for copy in copies:
        copy.wait()


def lay_heads(parts):
    tokens = parts[0].shape[0]
    return pl.pallas_call(
        lay_heads_kernel,
        name="lay_heads",
        out_shape=shape(tokens, H * HD),
        in_specs=[ANY] * len(parts),
        out_specs=ANY,
        scratch_shapes=[pltpu.SemaphoreType.DMA((len(parts),))],
        cost_estimate=pl.CostEstimate(flops=0, bytes_accessed=4 * tokens * H * HD, transcendentals=0),
    )(*parts)


def lay_kv_kernel(*refs):
    parts, (key_out, value_out) = refs[:-2], refs[-2:]
    core = lax.rem(lax.axis_index("ctx"), 2)
    for n, heads in enumerate(CHUNKS):
        for m, half in ((0, core), (1, 1 - core)):
            src = parts[2 * n + m]
            for at, head in enumerate(heads):
                dst = cols((half * HALF + head) * HD, HD)
                key_out[:, dst] = src[:, at * KV2:at * KV2 + HD]
                value_out[:, dst] = src[:, at * KV2 + HD:(at + 1) * KV2]


def lay_kv(parts):
    tokens = parts[0].shape[0]
    return pl.pallas_call(
        lay_kv_kernel,
        name="lay_kv",
        out_shape=[shape(tokens, KVH * HD)] * 2,
        in_specs=[VMEM] * len(parts),
        out_specs=[VMEM, VMEM],
        cost_estimate=pl.CostEstimate(flops=0, bytes_accessed=8 * tokens * KVH * HD, transcendentals=0),
    )(*parts)


def fold8(op, value):
    return op(value.reshape(value.shape[0] // 8, 8, value.shape[1]), axis=0)


def core_kernel(chunk, tokens, doc_ref, q_ref, g_ref, pair_ref, own_ref, ra_ref, rb_ref, r2_ref,
                o_own, o_pair, dq_own, dq_pair, far_out, mid_out, near_out,
                q_s, g_s, kv_s, kvt_s, acc_s, s_s, e_s, d_s, o_s, dq_s, sems, out_sems):
    heads = CHUNKS[chunk]
    count = len(heads)
    me = lax.axis_index("ctx")
    chip, core = lax.div(me, 2), lax.rem(me, 2)
    far_rows = 2 * tokens - BLK
    near_at = far_rows + 2 * tokens
    kv_width = count * KV2
    wide = HALF * QW
    mine, other = rows(core * tokens, tokens), rows((1 - core) * tokens, tokens)
    q_src = cols((core * HALF + heads[0]) * QW, count * QW)
    pair_kv = 2 * wide + heads[0] * KV2
    moves = [
        (own_ref, kv_s.at[rows(near_at + core * tokens, tokens), :]),
        (pair_ref.at[:, pl.ds(pair_kv, kv_width)], kv_s.at[rows(near_at + (1 - core) * tokens, tokens), :]),
        (ra_ref, kv_s.at[rows(far_rows + core * tokens, tokens), :]),
        (rb_ref, kv_s.at[rows(far_rows + (1 - core) * tokens, tokens), :]),
        (r2_ref, kv_s.at[pl.ds(0, far_rows), :]),
        (q_ref.at[:, q_src], q_s.at[mine, :]),
        (pair_ref.at[:, pl.ds(heads[0] * QW, count * QW)], q_s.at[other, :]),
        (g_ref.at[:, q_src], g_s.at[mine, :]),
        (pair_ref.at[:, pl.ds(wide + heads[0] * QW, count * QW)], g_s.at[other, :]),
    ]
    copies = [pltpu.make_async_copy(src, dst, sems.at[n]) for n, (src, dst) in enumerate(moves)]
    for copy in copies:
        copy.start()
    acc_s[...] = jnp.zeros_like(acc_s)
    for copy in copies:
        copy.wait()
    blocks = kv_s.shape[0] // BLK
    for at in range(blocks):
        kvt_s[:, at * BLK:(at + 1) * BLK] = kv_s[at * BLK:(at + 1) * BLK, :].T

    def attend(block, at, many, seen):
        span = many * BLK
        base = (block + MOST_BLK - many) * BLK
        window = rows(base, span)
        tok = rows(block * BLK, BLK)
        key_cols = slice(at * KV2, at * KV2 + HD)
        value_cols = slice(at * KV2 + HD, (at + 1) * KV2)
        q_here, g_here = q_s[tok, at * QW:(at + 1) * QW], g_s[tok, at * QW:(at + 1) * QW]
        qt = jnp.concatenate([q_here[:, n * HD:(n + 1) * HD].T for n in range(GROUP)], axis=1)
        gt = jnp.concatenate([g_here[:, n * HD:(n + 1) * HD].T for n in range(GROUP)], axis=1)
        part = 2 * BLK
        ts = [slice(n * part, (n + 1) * part) for n in range(GROUP * BLK // part)]
        scale_rows = []
        edge = jnp.where(seen < many, F32(-1e30), F32(0.0))
        causal = (lax.broadcasted_iota(jnp.int32, (BLK, BLK), 0)
                  <= lax.broadcasted_iota(jnp.int32, (BLK, BLK), 1))
        causal = jnp.concatenate([causal] * (part // BLK), axis=1)
        for t in ts:
            tops = None
            for kb in range(many):
                k_here = kv_s[rows(base + kb * BLK, BLK), key_cols]
                s = jnp.dot(k_here, qt[:, t], preferred_element_type=F32)
                if kb == 0:
                    s = s + edge
                if kb == many - 1:
                    s = jnp.where(causal, s, F32(-1e30))
                s_s[kb * BLK:(kb + 1) * BLK, t] = s
                top = fold8(jnp.max, s)
                tops = top if tops is None else jnp.maximum(tops, top)
            top = jnp.max(tops, axis=0, keepdims=True) * F32(SCALE * LOG2E)
            sums = None
            for kb in range(many):
                e = jnp.exp2(s_s[kb * BLK:(kb + 1) * BLK, t] * F32(SCALE * LOG2E) - top)
                s_s[kb * BLK:(kb + 1) * BLK, t] = e
                e_s[kb * BLK:(kb + 1) * BLK, t] = e.astype(BF)
                total = fold8(jnp.sum, e)
                sums = total if sums is None else sums + total
            inv = 1.0 / jnp.sum(sums, axis=0, keepdims=True)
            scale_rows.append(inv)
            ot = jnp.dot(kvt_s[value_cols, cols(base, span)], e_s[:span, t],
                         preferred_element_type=F32) * inv
            ot_low = ot.astype(BF)
            dots = jnp.sum(gt[:, t].astype(F32) * ot_low.astype(F32), axis=0, keepdims=True)
            for kb in range(many):
                v_here = kv_s[rows(base + kb * BLK, BLK), value_cols]
                dp = jnp.dot(v_here, gt[:, t], preferred_element_type=F32)
                d_s[kb * BLK:(kb + 1) * BLK, t] = (s_s[kb * BLK:(kb + 1) * BLK, t] * (dp - dots)).astype(BF)
            dqt = jnp.dot(kvt_s[key_cols, cols(base, span)], d_s[:span, t],
                          preferred_element_type=F32) * (inv * F32(SCALE))
            dqt_low = dqt.astype(BF)
            for n in range(part // BLK):
                where = slice(at * QW + t.start + n * BLK, at * QW + t.start + (n + 1) * BLK)
                o_s[tok, where] = ot_low[:, n * BLK:(n + 1) * BLK].T
                dq_s[tok, where] = dqt_low[:, n * BLK:(n + 1) * BLK].T
        inv = jnp.concatenate(scale_rows, axis=1)
        gt_low = (gt.astype(F32) * inv).astype(BF)
        qt_low = (qt.astype(F32) * (inv * F32(SCALE))).astype(BF)
        last = (((1,), (1,)), ((), ()))
        acc_s[window, key_cols] += lax.dot_general(d_s[:span, :], qt_low, last, preferred_element_type=F32)
        acc_s[window, value_cols] += lax.dot_general(e_s[:span, :], gt_low, last, preferred_element_type=F32)

    def step(block, carry):
        place = chip * (2 * tokens // BLK) + block
        doc = doc_ref[0, place]
        seen = jnp.int32(0)
        for back in range(MOST_BLK):
            there = place - back
            same = (there >= 0) & (doc_ref[0, jnp.maximum(there, 0)] == doc)
            seen += same.astype(jnp.int32)
        for many in range(2, MOST_BLK + 1, 2):
            @pl.when((seen == many) | (seen == many - 1))
            def _():
                for at in range(count):
                    attend(block, at, many, seen)
        return carry

    lax.fori_loop(0, 2 * tokens // BLK, step, 0)
    far_out[...] = acc_s[:far_rows, :].astype(BF)
    mid_out[...] = acc_s[far_rows:near_at, :]
    near_out[...] = acc_s[near_at:, :]
    leaving = [(o_s, o_own, mine), (o_s, o_pair, other), (dq_s, dq_own, mine), (dq_s, dq_pair, other)]
    copies = [pltpu.make_async_copy(src.at[at, :], dst, out_sems.at[n])
              for n, (src, dst, at) in enumerate(leaving)]
    for copy in copies:
        copy.start()
    for copy in copies:
        copy.wait()


def attend_chunk(chunk, docs, queries, grads, pair, own_kv, straight, crossed, far):
    tokens = queries.shape[0]
    count = len(CHUNKS[chunk])
    kv_width, q_width = count * KV2, count * QW
    far_rows = 2 * tokens - BLK
    all_rows = far_rows + 4 * tokens
    most = MOST_BLK * BLK
    tiles = 2 * tokens // BLK * MOST_BLK * count * GROUP
    return pl.pallas_call(
        functools.partial(core_kernel, chunk, tokens),
        name="attend",
        out_shape=[shape(tokens, q_width)] * 4 + [
            shape(far_rows, kv_width),
            shape(2 * tokens, kv_width, F32),
            shape(2 * tokens, kv_width, F32),
        ],
        in_specs=[SMEM] + [ANY] * 7,
        out_specs=[ANY] * 4 + [VMEM] * 3,
        scratch_shapes=[
            pltpu.VMEM((2 * tokens, q_width), BF),
            pltpu.VMEM((2 * tokens, q_width), BF),
            pltpu.VMEM((all_rows, kv_width), BF),
            pltpu.VMEM((kv_width, all_rows), BF),
            pltpu.VMEM((all_rows, kv_width), F32),
            pltpu.VMEM((most, QW), F32),
            pltpu.VMEM((most, QW), BF),
            pltpu.VMEM((most, QW), BF),
            pltpu.VMEM((2 * tokens, q_width), BF),
            pltpu.VMEM((2 * tokens, q_width), BF),
            pltpu.SemaphoreType.DMA((9,)),
            pltpu.SemaphoreType.DMA((4,)),
        ],
        compiler_params=pltpu.CompilerParams(vmem_limit_bytes=40 * 1024 * 1024),
        cost_estimate=pl.CostEstimate(
            flops=10 * tiles * BLK * BLK * HD, bytes_accessed=6 * 1024 * 1024,
            transcendentals=tiles * BLK * BLK),
    )(docs, queries, grads, pair, own_kv, straight, crossed, far)


def shards(queries, key_rows, value_rows, out_grad, doc_blocks):
    peers = lax.axis_size("ctx")
    sections = lax.axis_size("pipe")

    def move(value, chips, cross):
        pairs = []
        for i in range(peers):
            to = (i // 2 + chips) * 2 + ((i % 2) ^ cross)
            if 0 <= to < peers:
                pairs.append((i, to))
        return lax.ppermute(value, "ctx", pairs)

    def move_back(value, cross):
        pairs = [(p * peers + i, (p - 1) * peers + (i ^ cross))
                 for p in range(1, sections) for i in range(peers)]
        return lax.ppermute(value, ("pipe", "ctx"), pairs)

    q, g = queries[0], out_grad[0]
    packed = pack_kv(key_rows[0], value_rows[0])
    straight, crossed = packed[0::2], packed[1::2]
    got_a = [move(kv, 1, 0) for kv in straight]
    got_b = [move(kv, 1, 1) for kv in crossed]
    pair = move(pack_pair(q, g, crossed), 0, 1)
    got_far = [move(relay(a, b), 1, 0) for a, b in zip(got_a, got_b)]
    outs, q_parts, kv_parts = [], [], []
    for n in range(len(CHUNKS)):
        o_own, o_pair, dq_own, dq_pair, far, mid, near = attend_chunk(
            n, doc_blocks, q, g, pair, straight[n], got_a[n], got_b[n], got_far[n])
        far_got = move(far, -1, 0)
        q_parts += [move_back(dq_own, 0), move_back(dq_pair, 1)]
        mid_got = move(add_middle(mid, far_got), -1, 0)
        outs += [o_own, move(o_pair, 0, 1)]
        ours, theirs = add_last(near, mid_got)
        kv_parts += [move_back(ours, 0), move_back(theirs, 1)]
    attn_out = lay_heads(outs)
    grad_query = lay_heads(q_parts)
    grad_key, grad_value = lay_kv(kv_parts)
    return attn_out[None], grad_query[None], grad_key[None], grad_value[None]


def solution(mesh):
    tokens = P("pipe", "ctx", None)
    return jax.shard_map(
        shards,
        mesh=mesh,
        in_specs=(tokens, tokens, tokens, tokens, P("pipe", None)),
        out_specs=(tokens, tokens, tokens, tokens),
        check_vma=False,
    )
```

```python
import functools
import math

import jax
import jax.numpy as jnp
from jax import lax
from jax.experimental import pallas as pl
from jax.experimental.pallas import tpu as pltpu
from jax.sharding import PartitionSpec as P

HD = 128
H = 16
KVH = 4
BLK = 128
MOST_BLK = 8

GROUP = H // KVH
HALF = KVH // 2
QW = GROUP * HD
KV2 = 2 * HD
SCALE = 1.0 / math.sqrt(HD)
LOG2E = math.log2(math.e)
CHUNKS = ((0,), (1,))
SMALL_BYTES = 4 * 1024 * 1024
FIRST_BYTES = 56 * 1024 * 1024
ATTEND_BYTES = 20 * 1024 * 1024

BF = jnp.bfloat16
F32 = jnp.float32
ANY = pl.BlockSpec(memory_space=pl.ANY)
VMEM = pl.BlockSpec(memory_space=pltpu.VMEM)
HBM = pl.BlockSpec(memory_space=pltpu.HBM)
SMEM = pl.BlockSpec(memory_space=pltpu.SMEM)


def shape(rows, cols, dtype=BF):
    return jax.ShapeDtypeStruct((rows, cols), dtype)


def cols(start, size):
    return pl.ds(pl.multiple_of(start, HD), size)


def rows(start, size):
    return pl.ds(pl.multiple_of(start, BLK), size)


def call(kernel, name, outs, args, scratch, in_specs=None, out_specs=None, limit=SMALL_BYTES):
    return pl.pallas_call(
        kernel,
        name=name,
        out_shape=outs,
        in_specs=in_specs or [ANY] * len(args),
        out_specs=out_specs or [ANY] * len(outs),
        scratch_shapes=scratch,
        compiler_params=pltpu.CompilerParams(vmem_limit_bytes=limit),
        cost_estimate=pl.CostEstimate(flops=1000, bytes_accessed=1000, transcendentals=0),
    )(*args)


def stage(moves, sems):
    copies = [pltpu.make_async_copy(src, dst, sems.at[n]) for n, (src, dst) in enumerate(moves)]
    for copy in copies:
        copy.start()
    return copies


def wait(copies):
    for copy in copies:
        copy.wait()


def pack_kernel(q_ref, g_ref, k_ref, v_ref, *rest):
    near, pair, kv_s, pair_s, in_sems, out_sems = rest[:-5], *rest[-5:]
    core = lax.rem(lax.axis_index("ctx"), 2)
    moves = []
    for n, heads in enumerate(CHUNKS):
        at = 0
        for half in range(2):
            for head in heads:
                src = pl.ds((half * HALF + head) * HD, HD)
                for ref in (k_ref, v_ref):
                    moves.append((ref.at[:, src], kv_s.at[n, :, pl.ds(at, HD)]))
                    at += HD
    each = len(moves) // len(near)
    wide = HALF * QW
    src = cols((1 - core) * wide, wide)
    moves += [(q_ref.at[:, src], pair_s.at[:, pl.ds(0, wide)]),
              (g_ref.at[:, src], pair_s.at[:, pl.ds(wide, wide)])]
    ins = stage(moves, in_sems)
    leaving = []
    for n, out in enumerate((*near, pair)):
        wait(ins[n * each:(n + 1) * each])
        src = kv_s.at[n] if n < len(near) else pair_s
        leaving.append(pltpu.make_async_copy(src, out, out_sems.at[n]))
        leaving[-1].start()
    wait(leaving)


def pack(queries, grads, keys, values):
    tokens = queries.shape[0]
    width = 2 * len(CHUNKS[0]) * KV2
    outs = call(
        pack_kernel, "pack",
        [shape(tokens, width)] * len(CHUNKS) + [shape(tokens, 2 * HALF * QW)],
        (queries, grads, keys, values),
        [pltpu.VMEM((len(CHUNKS), tokens, width), BF),
         pltpu.VMEM((tokens, 2 * HALF * QW), BF),
         pltpu.SemaphoreType.DMA((4 * HALF + 2,)),
         pltpu.SemaphoreType.DMA((len(CHUNKS) + 1,))],
        [HBM] * 4,
        limit=FIRST_BYTES)
    return list(outs[:-1]), outs[-1]


def add_last_kernel(near_ref, mid_ref, far_ref, straight, crossed):
    core = lax.rem(lax.axis_index("ctx"), 2)
    tokens = straight.shape[0]
    trim = near_ref.shape[0] - far_ref.shape[0]

    def half(out, shard):
        at = slice(shard * tokens, (shard + 1) * tokens)
        total = near_ref[at, :] + mid_ref[at, :].astype(F32)
        if shard == 0:
            out[:trim, :] = total[:trim, :].astype(BF)
            out[trim:, :] = (total[trim:, :] + far_ref[:tokens - trim, :].astype(F32)).astype(BF)
        else:
            out[...] = (total + far_ref[tokens - trim:, :].astype(F32)).astype(BF)

    @pl.when(core == 0)
    def _():
        half(straight, 0)
        half(crossed, 1)

    @pl.when(core == 1)
    def _():
        half(straight, 1)
        half(crossed, 0)


def add_last(near, mid, far):
    tokens, width = near.shape[0] // 2, near.shape[1]
    return call(add_last_kernel, "add_last", [shape(tokens, width)] * 2, (near, mid, far), [],
                [VMEM] * 3, [VMEM] * 2)


def lay_heads_kernel(*refs):
    parts, (out, held, in_sems, out_sems) = refs[:-4], refs[-4:]
    core = lax.rem(lax.axis_index("ctx"), 2)
    moves = []
    for n, heads in enumerate(CHUNKS):
        for m, half in ((0, core), (1, 1 - core)):
            moves.append((parts[2 * n + m],
                          held.at[:, cols((half * HALF + heads[0]) * QW, len(heads) * QW)]))
    wait(stage(moves, in_sems))
    wait(stage([(held, out)], out_sems))


def lay_heads(parts):
    tokens = parts[0].shape[0]
    return call(
        lay_heads_kernel, "lay_heads", [shape(tokens, H * HD)], parts,
        [pltpu.VMEM((tokens, H * HD), BF),
         pltpu.SemaphoreType.DMA((len(parts),)),
         pltpu.SemaphoreType.DMA((1,))])[0]


def lay_kv_kernel(*refs):
    parts, (key_out, value_out, held, in_sems, out_sems) = refs[:-5], refs[-5:]
    core = lax.rem(lax.axis_index("ctx"), 2)
    moves = []
    for n, heads in enumerate(CHUNKS):
        for m, half in ((0, core), (1, 1 - core)):
            for at, head in enumerate(heads):
                dst = cols((half * HALF + head) * HD, HD)
                for side in range(2):
                    src = parts[2 * n + m].at[:, pl.ds(at * KV2 + side * HD, HD)]
                    moves.append((src, held.at[side, :, dst]))
    wait(stage(moves, in_sems))
    wait(stage([(held.at[0], key_out), (held.at[1], value_out)], out_sems))


def lay_kv(parts):
    tokens = parts[0].shape[0]
    return call(
        lay_kv_kernel, "lay_kv", [shape(tokens, KVH * HD)] * 2, parts,
        [pltpu.VMEM((2, tokens, KVH * HD), BF),
         pltpu.SemaphoreType.DMA((4 * HALF,)),
         pltpu.SemaphoreType.DMA((2,))])


def fold8(op, value):
    return op(value.reshape(value.shape[0] // 8, 8, value.shape[1]), axis=0)


def core_kernel(chunk, tokens, doc_ref, q_ref, g_ref, pair_ref, *rest):
    (kv_refs, (o_own, o_pair, dq_own, dq_pair, far_out, mid_out, near_out,
               q_s, g_s, kv_s, kvt_s, acc_s, s_s, e_s, d_s, o_s, dq_s, sems, out_sems)) = rest[:6], rest[6:]
    heads = CHUNKS[chunk]
    count = len(heads)
    me = lax.axis_index("ctx")
    chip, core = lax.div(me, 2), lax.rem(me, 2)
    near_at = 4 * tokens
    kv_width = count * KV2
    wide = HALF * QW
    mine, other = rows(core * tokens, tokens), rows((1 - core) * tokens, tokens)
    q_src = cols((core * HALF + heads[0]) * QW, count * QW)
    kv_src = cols(core * kv_width, kv_width)
    moves = [
        (q_ref.at[:, q_src], q_s.at[mine, :]),
        (pair_ref.at[:, pl.ds(heads[0] * QW, count * QW)], q_s.at[other, :]),
        (g_ref.at[:, q_src], g_s.at[mine, :]),
        (pair_ref.at[:, pl.ds(wide + heads[0] * QW, count * QW)], g_s.at[other, :]),
    ]
    for n in range(3):
        for m, shard in ((0, core), (1, 1 - core)):
            moves.append((kv_refs[2 * n + m].at[:, kv_src],
                          kv_s.at[rows((4 - 2 * n + shard) * tokens, tokens), :]))
    copies = [pltpu.make_async_copy(src, dst, sems.at[n]) for n, (src, dst) in enumerate(moves)]
    for copy in copies:
        copy.start()
    acc_s[...] = jnp.zeros_like(acc_s)
    for copy in copies:
        copy.wait()
    blocks = kv_s.shape[0] // BLK
    for at in range(blocks):
        kvt_s[:, at * BLK:(at + 1) * BLK] = kv_s[at * BLK:(at + 1) * BLK, :].T

    def attend(block, at, many, seen):
        span = many * BLK
        base = (block + MOST_BLK + 1 - many) * BLK
        window = rows(base, span)
        tok = rows(block * BLK, BLK)
        key_cols = slice(at * KV2, at * KV2 + HD)
        value_cols = slice(at * KV2 + HD, (at + 1) * KV2)
        q_here, g_here = q_s[tok, at * QW:(at + 1) * QW], g_s[tok, at * QW:(at + 1) * QW]
        qt = jnp.concatenate([q_here[:, n * HD:(n + 1) * HD].T for n in range(GROUP)], axis=1)
        gt = jnp.concatenate([g_here[:, n * HD:(n + 1) * HD].T for n in range(GROUP)], axis=1)
        part = 2 * BLK
        ts = [slice(n * part, (n + 1) * part) for n in range(GROUP * BLK // part)]
        scale_rows = []
        edge = jnp.where(seen < many, F32(-1e30), F32(0.0))
        causal = (lax.broadcasted_iota(jnp.int32, (BLK, BLK), 0)
                  <= lax.broadcasted_iota(jnp.int32, (BLK, BLK), 1))
        causal = jnp.concatenate([causal] * (part // BLK), axis=1)
        for t in ts:
            tops = None
            for kb in range(many):
                k_here = kv_s[rows(base + kb * BLK, BLK), key_cols]
                s = jnp.dot(k_here, qt[:, t], preferred_element_type=F32)
                if kb == 0:
                    s = s + edge
                if kb == many - 1:
                    s = jnp.where(causal, s, F32(-1e30))
                s_s[kb * BLK:(kb + 1) * BLK, t] = s
                top = fold8(jnp.max, s)
                tops = top if tops is None else jnp.maximum(tops, top)
            top = jnp.max(tops, axis=0, keepdims=True) * F32(SCALE * LOG2E)
            sums = None
            for kb in range(many):
                e = jnp.exp2(s_s[kb * BLK:(kb + 1) * BLK, t] * F32(SCALE * LOG2E) - top)
                s_s[kb * BLK:(kb + 1) * BLK, t] = e
                e_s[kb * BLK:(kb + 1) * BLK, t] = e.astype(BF)
                total = fold8(jnp.sum, e)
                sums = total if sums is None else sums + total
            inv = 1.0 / jnp.sum(sums, axis=0, keepdims=True)
            scale_rows.append(inv)
            ot = jnp.dot(kvt_s[value_cols, cols(base, span)], e_s[:span, t],
                         preferred_element_type=F32) * inv
            ot_low = ot.astype(BF)
            dots = jnp.sum(gt[:, t].astype(F32) * ot_low.astype(F32), axis=0, keepdims=True)
            for kb in range(many):
                v_here = kv_s[rows(base + kb * BLK, BLK), value_cols]
                dp = jnp.dot(v_here, gt[:, t], preferred_element_type=F32)
                d_s[kb * BLK:(kb + 1) * BLK, t] = (s_s[kb * BLK:(kb + 1) * BLK, t] * (dp - dots)).astype(BF)
            dqt = jnp.dot(kvt_s[key_cols, cols(base, span)], d_s[:span, t],
                          preferred_element_type=F32) * (inv * F32(SCALE))
            dqt_low = dqt.astype(BF)
            for n in range(part // BLK):
                where = slice(at * QW + t.start + n * BLK, at * QW + t.start + (n + 1) * BLK)
                o_s[tok, where] = ot_low[:, n * BLK:(n + 1) * BLK].T
                dq_s[tok, where] = dqt_low[:, n * BLK:(n + 1) * BLK].T
        inv = jnp.concatenate(scale_rows, axis=1)
        gt_low = (gt.astype(F32) * inv).astype(BF)
        qt_low = (qt.astype(F32) * (inv * F32(SCALE))).astype(BF)
        last = (((1,), (1,)), ((), ()))
        acc_s[window, key_cols] += lax.dot_general(d_s[:span, :], qt_low, last, preferred_element_type=F32)
        acc_s[window, value_cols] += lax.dot_general(e_s[:span, :], gt_low, last, preferred_element_type=F32)

    def step(block, carry):
        place = chip * (2 * tokens // BLK) + block
        doc = doc_ref[0, place]
        seen = jnp.int32(0)
        for back in range(MOST_BLK):
            there = place - back
            same = (there >= 0) & (doc_ref[0, jnp.maximum(there, 0)] == doc)
            seen += same.astype(jnp.int32)
        for many in range(2, MOST_BLK + 1, 2):
            @pl.when((seen == many) | (seen == many - 1))
            def _():
                for at in range(count):
                    attend(block, at, many, seen)
        return carry

    lax.fori_loop(0, 2 * tokens // BLK, step, 0)
    far_out[...] = acc_s[BLK:2 * tokens, :].astype(BF)
    mid_out[...] = acc_s[2 * tokens:near_at, :].astype(BF)
    near_out[...] = acc_s[near_at:, :]
    leaving = [(o_s, o_own, mine), (o_s, o_pair, other), (dq_s, dq_own, mine), (dq_s, dq_pair, other)]
    copies = [pltpu.make_async_copy(src.at[at, :], dst, out_sems.at[n])
              for n, (src, dst, at) in enumerate(leaving)]
    for copy in copies:
        copy.start()
    for copy in copies:
        copy.wait()


def attend_chunk(chunk, docs, queries, grads, pair, kvs):
    tokens = queries.shape[0]
    count = len(CHUNKS[chunk])
    kv_width, q_width = count * KV2, count * QW
    all_rows = 6 * tokens
    most = MOST_BLK * BLK
    return call(
        functools.partial(core_kernel, chunk, tokens),
        "attend",
        [shape(tokens, q_width)] * 4 + [
            shape(2 * tokens - BLK, kv_width),
            shape(2 * tokens, kv_width),
            shape(2 * tokens, kv_width, F32),
        ],
        (docs, queries, grads, pair, *kvs),
        [
            pltpu.VMEM((2 * tokens, q_width), BF),
            pltpu.VMEM((2 * tokens, q_width), BF),
            pltpu.VMEM((all_rows, kv_width), BF),
            pltpu.VMEM((kv_width, all_rows), BF),
            pltpu.VMEM((all_rows, kv_width), F32),
            pltpu.VMEM((most, QW), F32),
            pltpu.VMEM((most, QW), BF),
            pltpu.VMEM((most, QW), BF),
            pltpu.VMEM((2 * tokens, q_width), BF),
            pltpu.VMEM((2 * tokens, q_width), BF),
            pltpu.SemaphoreType.DMA((10,)),
            pltpu.SemaphoreType.DMA((4,)),
        ],
        [SMEM] + [HBM] * 2 + [ANY] * 7,
        [ANY] * 4 + [VMEM] * 3,
        ATTEND_BYTES)


def shards(queries, key_rows, value_rows, out_grad, doc_blocks):
    peers = lax.axis_size("ctx")
    sections = lax.axis_size("pipe")

    def move(value, chips, cross):
        pairs = []
        for i in range(peers):
            to = (i // 2 + chips) * 2 + ((i % 2) ^ cross)
            if 0 <= to < peers:
                pairs.append((i, to))
        return lax.ppermute(value, "ctx", pairs)

    def move_back(value, cross):
        pairs = [(p * peers + i, (p - 1) * peers + (i ^ cross))
                 for p in range(1, sections) for i in range(peers)]
        return lax.ppermute(value, ("pipe", "ctx"), pairs)

    q, g = queries[0], out_grad[0]
    near, pair = pack(q, g, key_rows[0], value_rows[0])
    mid = [move(kv, 1, 0) for kv in near]
    pair = move(pair, 0, 1)
    far = [move(kv, 1, 0) for kv in mid]
    outs, q_parts, kv_parts = [], [], []
    far_got = mid_got = None
    for n in range(len(CHUNKS)):
        kvs = []
        if n:
            near[n], mid[n], far[n], _ = lax.optimization_barrier((near[n], mid[n], far[n], near_part))
        for kv in (near[n], mid[n], far[n]):
            kvs += [kv, move(kv, 0, 1)]
        o_own, o_pair, dq_own, dq_pair, far_part, mid_part, near_part = attend_chunk(
            n, doc_blocks, q, g, pair, kvs)
        if n:
            far_part, mid_part, far_got, mid_got = lax.optimization_barrier(
                (far_part, mid_part, far_got, mid_got))
            dq_own, dq_pair, *q_parts = lax.optimization_barrier((dq_own, dq_pair, *q_parts))
        far_got = move(far_part, -2, 0)
        mid_got = move(mid_part, -1, 0)
        q_parts += [move_back(dq_own, 0), move_back(dq_pair, 1)]
        outs += [o_own, move(o_pair, 0, 1)]
        ours, theirs = add_last(near_part, mid_got, far_got)
        kv_parts += [move_back(ours, 0), move_back(theirs, 1)]
    attn_out = lay_heads(outs)
    grad_query = lay_heads(q_parts)
    grad_key, grad_value = lay_kv(kv_parts)
    return attn_out[None], grad_query[None], grad_key[None], grad_value[None]


def solution(mesh):
    tokens = P("pipe", "ctx", None)
    return jax.shard_map(
        shards,
        mesh=mesh,
        in_specs=(tokens, tokens, tokens, tokens, P("pipe", None)),
        out_specs=(tokens, tokens, tokens, tokens),
        check_vma=False,
    )
```

```python
import functools
import math

import jax
import jax.numpy as jnp
from jax import lax
from jax.experimental import pallas as pl
from jax.experimental.pallas import tpu as pltpu
from jax.sharding import PartitionSpec as P

HD = 128
H = 16
KVH = 4
BLK = 128
MOST_BLK = 8

GROUP = H // KVH
HALF = KVH // 2
QW = GROUP * HD
KV2 = 2 * HD
SCALE = 1.0 / math.sqrt(HD)
LOG2E = math.log2(math.e)
CHUNKS = ((0,), (1,))
SMALL_BYTES = 4 * 1024 * 1024
FIRST_BYTES = 56 * 1024 * 1024
ATTEND_BYTES = 20 * 1024 * 1024

BF = jnp.bfloat16
F32 = jnp.float32
ANY = pl.BlockSpec(memory_space=pl.ANY)
VMEM = pl.BlockSpec(memory_space=pltpu.VMEM)
HBM = pl.BlockSpec(memory_space=pltpu.HBM)
SMEM = pl.BlockSpec(memory_space=pltpu.SMEM)


def shape(rows, cols, dtype=BF):
    return jax.ShapeDtypeStruct((rows, cols), dtype)


def cols(start, size):
    return pl.ds(pl.multiple_of(start, HD), size)


def rows(start, size):
    return pl.ds(pl.multiple_of(start, BLK), size)


def call(kernel, name, outs, args, scratch, in_specs=None, out_specs=None, limit=SMALL_BYTES):
    return pl.pallas_call(
        kernel,
        name=name,
        out_shape=outs,
        in_specs=in_specs or [ANY] * len(args),
        out_specs=out_specs or [ANY] * len(outs),
        scratch_shapes=scratch,
        compiler_params=pltpu.CompilerParams(vmem_limit_bytes=limit),
        cost_estimate=pl.CostEstimate(flops=1000, bytes_accessed=1000, transcendentals=0),
    )(*args)


def stage(moves, sems):
    copies = [pltpu.make_async_copy(src, dst, sems.at[n]) for n, (src, dst) in enumerate(moves)]
    for copy in copies:
        copy.start()
    return copies


def wait(copies):
    for copy in copies:
        copy.wait()


def pack_kernel(q_ref, g_ref, k_ref, v_ref, *rest):
    near, pair, kv_s, pair_s, in_sems, out_sems = rest
    core = lax.rem(lax.axis_index("ctx"), 2)
    moves = []
    for n, heads in enumerate(CHUNKS):
        at = 0
        for half in range(2):
            for head in heads:
                src = pl.ds((half * HALF + head) * HD, HD)
                for ref in (k_ref, v_ref):
                    moves.append((ref.at[:, src], kv_s.at[n, :, pl.ds(at, HD)]))
                    at += HD
    kv_moves = len(moves)
    wide = HALF * QW
    src = cols((1 - core) * wide, wide)
    moves += [(q_ref.at[:, src], pair_s.at[:, pl.ds(0, wide)]),
              (g_ref.at[:, src], pair_s.at[:, pl.ds(wide, wide)])]
    ins = stage(moves, in_sems)
    wait(ins[:kv_moves])
    leaving = [pltpu.make_async_copy(kv_s, near, out_sems.at[0])]
    leaving[0].start()
    wait(ins[kv_moves:])
    leaving.append(pltpu.make_async_copy(pair_s, pair, out_sems.at[1]))
    leaving[1].start()
    wait(leaving)


def pack(queries, grads, keys, values):
    tokens = queries.shape[0]
    kv_shape = (len(CHUNKS), tokens, 2 * len(CHUNKS[0]) * KV2)
    return call(
        pack_kernel, "pack",
        [jax.ShapeDtypeStruct(kv_shape, BF), shape(tokens, 2 * HALF * QW)],
        (queries, grads, keys, values),
        [pltpu.VMEM(kv_shape, BF),
         pltpu.VMEM((tokens, 2 * HALF * QW), BF),
         pltpu.SemaphoreType.DMA((4 * HALF + 2,)),
         pltpu.SemaphoreType.DMA((2,))],
        [HBM] * 4,
        limit=FIRST_BYTES)


def sum_shards(near_ref, mid_ref, far_ref, straight, crossed, at=0):
    core = lax.rem(lax.axis_index("ctx"), 2)
    tokens = straight.shape[0]
    trim = near_ref.shape[0] - far_ref.shape[0]
    to = slice(at, at + near_ref.shape[1])

    def half(out, shard):
        rows_here = slice(shard * tokens, (shard + 1) * tokens)
        total = near_ref[rows_here, :] + mid_ref[rows_here, :].astype(F32)
        if shard == 0:
            out[:trim, to] = total[:trim, :].astype(BF)
            out[trim:, to] = (total[trim:, :] + far_ref[:tokens - trim, :].astype(F32)).astype(BF)
        else:
            out[:, to] = (total + far_ref[tokens - trim:, :].astype(F32)).astype(BF)

    @pl.when(core == 0)
    def _():
        half(straight, 0)
        half(crossed, 1)

    @pl.when(core == 1)
    def _():
        half(straight, 1)
        half(crossed, 0)


def add_last(near, mid, far):
    tokens, width = near.shape[0] // 2, near.shape[1]
    return call(sum_shards, "add_last", [shape(tokens, width)] * 2, (near, mid, far), [],
                [VMEM] * 3, [VMEM] * 2)


def join_kernel(near_ref, mid_ref, far_ref, own_ref, pair_ref, straight, crossed, sems):
    width = own_ref.shape[1]
    copies = stage([(own_ref, straight.at[:, pl.ds(0, width)]),
                    (pair_ref, crossed.at[:, pl.ds(0, width)])], sems)
    sum_shards(near_ref, mid_ref, far_ref, straight, crossed, width)
    wait(copies)


def join(near, mid, far, own, pair):
    tokens, width = own.shape
    return call(join_kernel, "join", [shape(tokens, width + near.shape[1])] * 2,
                (near, mid, far, own, pair), [pltpu.SemaphoreType.DMA((2,))],
                [VMEM] * 3 + [ANY] * 2, [VMEM] * 2)


def lay_heads_kernel(*refs):
    parts, (out, held, in_sems, out_sems) = refs[:-4], refs[-4:]
    core = lax.rem(lax.axis_index("ctx"), 2)
    moves = []
    for n, heads in enumerate(CHUNKS):
        for m, half in ((0, core), (1, 1 - core)):
            width = len(heads) * QW
            moves.append((parts[2 * n + m].at[:, pl.ds(0, width)],
                          held.at[:, cols((half * HALF + heads[0]) * QW, width)]))
    wait(stage(moves, in_sems))
    wait(stage([(held, out)], out_sems))


def lay_heads(parts):
    tokens = parts[0].shape[0]
    return call(
        lay_heads_kernel, "lay_heads", [shape(tokens, H * HD)], parts,
        [pltpu.VMEM((tokens, H * HD), BF),
         pltpu.SemaphoreType.DMA((len(parts),)),
         pltpu.SemaphoreType.DMA((1,))])[0]


def lay_kv_kernel(*refs):
    parts, (key_out, value_out, held, in_sems, out_sems) = refs[:-5], refs[-5:]
    core = lax.rem(lax.axis_index("ctx"), 2)
    moves = []
    for n, heads in enumerate(CHUNKS):
        for m, half in ((0, core), (1, 1 - core)):
            part = parts[2 * n + m]
            first = part.shape[1] - len(heads) * KV2
            for at, head in enumerate(heads):
                dst = cols((half * HALF + head) * HD, HD)
                for side in range(2):
                    src = part.at[:, pl.ds(first + at * KV2 + side * HD, HD)]
                    moves.append((src, held.at[side, :, dst]))
    wait(stage(moves, in_sems))
    wait(stage([(held.at[0], key_out), (held.at[1], value_out)], out_sems))


def lay_kv(parts):
    tokens = parts[0].shape[0]
    return call(
        lay_kv_kernel, "lay_kv", [shape(tokens, KVH * HD)] * 2, parts,
        [pltpu.VMEM((2, tokens, KVH * HD), BF),
         pltpu.SemaphoreType.DMA((4 * HALF,)),
         pltpu.SemaphoreType.DMA((2,))])


def fold8(op, value):
    return op(value.reshape(value.shape[0] // 8, 8, value.shape[1]), axis=0)


def core_kernel(chunk, tokens, doc_ref, q_ref, g_ref, pair_ref, *rest):
    (kv_refs, (o_own, o_pair, dq_own, dq_pair, far_out, mid_out, near_out,
               q_s, g_s, kv_s, kvt_s, acc_s, s_s, e_s, d_s, o_s, dq_s, sems, out_sems)) = rest[:6], rest[6:]
    heads = CHUNKS[chunk]
    count = len(heads)
    me = lax.axis_index("ctx")
    chip, core = lax.div(me, 2), lax.rem(me, 2)
    near_at = 4 * tokens
    kv_width = count * KV2
    wide = HALF * QW
    mine, other = rows(core * tokens, tokens), rows((1 - core) * tokens, tokens)
    q_src = cols((core * HALF + heads[0]) * QW, count * QW)
    kv_src = cols(core * kv_width, kv_width)
    moves = [
        (q_ref.at[:, q_src], q_s.at[mine, :]),
        (pair_ref.at[:, pl.ds(heads[0] * QW, count * QW)], q_s.at[other, :]),
        (g_ref.at[:, q_src], g_s.at[mine, :]),
        (pair_ref.at[:, pl.ds(wide + heads[0] * QW, count * QW)], g_s.at[other, :]),
    ]
    for n in range(3):
        for m, shard in ((0, core), (1, 1 - core)):
            kv_ref = kv_refs[2 * n + m]
            kv_ref = kv_ref.at[chunk] if n < 2 else kv_ref
            moves.append((kv_ref.at[:, kv_src],
                          kv_s.at[rows((4 - 2 * n + shard) * tokens, tokens), :]))
    copies = [pltpu.make_async_copy(src, dst, sems.at[n]) for n, (src, dst) in enumerate(moves)]
    for copy in copies:
        copy.start()
    acc_s[...] = jnp.zeros_like(acc_s)
    for copy in copies:
        copy.wait()
    blocks = kv_s.shape[0] // BLK
    for at in range(blocks):
        kvt_s[:, at * BLK:(at + 1) * BLK] = kv_s[at * BLK:(at + 1) * BLK, :].T

    def attend(block, at, many, seen):
        span = many * BLK
        base = (block + MOST_BLK + 1 - many) * BLK
        window = rows(base, span)
        tok = rows(block * BLK, BLK)
        key_cols = slice(at * KV2, at * KV2 + HD)
        value_cols = slice(at * KV2 + HD, (at + 1) * KV2)
        q_here, g_here = q_s[tok, at * QW:(at + 1) * QW], g_s[tok, at * QW:(at + 1) * QW]
        qt = jnp.concatenate([q_here[:, n * HD:(n + 1) * HD].T for n in range(GROUP)], axis=1)
        gt = jnp.concatenate([g_here[:, n * HD:(n + 1) * HD].T for n in range(GROUP)], axis=1)
        part = 2 * BLK
        ts = [slice(n * part, (n + 1) * part) for n in range(GROUP * BLK // part)]
        scale_rows = []
        edge = jnp.where(seen < many, F32(-1e30), F32(0.0))
        causal = (lax.broadcasted_iota(jnp.int32, (BLK, BLK), 0)
                  <= lax.broadcasted_iota(jnp.int32, (BLK, BLK), 1))
        causal = jnp.concatenate([causal] * (part // BLK), axis=1)
        for t in ts:
            tops = None
            for kb in range(many):
                k_here = kv_s[rows(base + kb * BLK, BLK), key_cols]
                s = jnp.dot(k_here, qt[:, t], preferred_element_type=F32)
                if kb == 0:
                    s = s + edge
                if kb == many - 1:
                    s = jnp.where(causal, s, F32(-1e30))
                s_s[kb * BLK:(kb + 1) * BLK, t] = s
                top = fold8(jnp.max, s)
                tops = top if tops is None else jnp.maximum(tops, top)
            top = jnp.max(tops, axis=0, keepdims=True) * F32(SCALE * LOG2E)
            sums = None
            for kb in range(many):
                e = jnp.exp2(s_s[kb * BLK:(kb + 1) * BLK, t] * F32(SCALE * LOG2E) - top)
                s_s[kb * BLK:(kb + 1) * BLK, t] = e
                e_s[kb * BLK:(kb + 1) * BLK, t] = e.astype(BF)
                total = fold8(jnp.sum, e)
                sums = total if sums is None else sums + total
            inv = 1.0 / jnp.sum(sums, axis=0, keepdims=True)
            scale_rows.append(inv)
            ot = jnp.dot(kvt_s[value_cols, cols(base, span)], e_s[:span, t],
                         preferred_element_type=F32) * inv
            ot_low = ot.astype(BF)
            dots = jnp.sum(gt[:, t].astype(F32) * ot_low.astype(F32), axis=0, keepdims=True)
            for kb in range(many):
                v_here = kv_s[rows(base + kb * BLK, BLK), value_cols]
                dp = jnp.dot(v_here, gt[:, t], preferred_element_type=F32)
                d_s[kb * BLK:(kb + 1) * BLK, t] = (s_s[kb * BLK:(kb + 1) * BLK, t] * (dp - dots)).astype(BF)
            dqt = jnp.dot(kvt_s[key_cols, cols(base, span)], d_s[:span, t],
                          preferred_element_type=F32) * (inv * F32(SCALE))
            dqt_low = dqt.astype(BF)
            for n in range(part // BLK):
                where = slice(at * QW + t.start + n * BLK, at * QW + t.start + (n + 1) * BLK)
                o_s[tok, where] = ot_low[:, n * BLK:(n + 1) * BLK].T
                dq_s[tok, where] = dqt_low[:, n * BLK:(n + 1) * BLK].T
        inv = jnp.concatenate(scale_rows, axis=1)
        gt_low = (gt.astype(F32) * inv).astype(BF)
        qt_low = (qt.astype(F32) * (inv * F32(SCALE))).astype(BF)
        last = (((1,), (1,)), ((), ()))
        acc_s[window, key_cols] += lax.dot_general(d_s[:span, :], qt_low, last, preferred_element_type=F32)
        acc_s[window, value_cols] += lax.dot_general(e_s[:span, :], gt_low, last, preferred_element_type=F32)

    def step(block, carry):
        place = chip * (2 * tokens // BLK) + block
        doc = doc_ref[0, place]
        seen = jnp.int32(0)
        for back in range(MOST_BLK):
            there = place - back
            same = (there >= 0) & (doc_ref[0, jnp.maximum(there, 0)] == doc)
            seen += same.astype(jnp.int32)
        for many in range(2, MOST_BLK + 1, 2):
            @pl.when((seen == many) | (seen == many - 1))
            def _():
                for at in range(count):
                    attend(block, at, many, seen)
        return carry

    lax.fori_loop(0, 2 * tokens // BLK, step, 0)
    far_out[...] = acc_s[BLK:2 * tokens, :].astype(BF)
    mid_out[...] = acc_s[2 * tokens:near_at, :].astype(BF)
    near_out[...] = acc_s[near_at:, :]
    leaving = [(o_s, o_own, mine), (o_s, o_pair, other), (dq_s, dq_own, mine), (dq_s, dq_pair, other)]
    copies = [pltpu.make_async_copy(src.at[at, :], dst, out_sems.at[n])
              for n, (src, dst, at) in enumerate(leaving)]
    for copy in copies:
        copy.start()
    for copy in copies:
        copy.wait()


def attend_chunk(chunk, docs, queries, grads, pair, kvs):
    tokens = queries.shape[0]
    count = len(CHUNKS[chunk])
    kv_width, q_width = count * KV2, count * QW
    all_rows = 6 * tokens
    most = MOST_BLK * BLK
    return call(
        functools.partial(core_kernel, chunk, tokens),
        "attend",
        [shape(tokens, q_width)] * 4 + [
            shape(2 * tokens - BLK, kv_width),
            shape(2 * tokens, kv_width),
            shape(2 * tokens, kv_width, F32),
        ],
        (docs, queries, grads, pair, *kvs),
        [
            pltpu.VMEM((2 * tokens, q_width), BF),
            pltpu.VMEM((2 * tokens, q_width), BF),
            pltpu.VMEM((all_rows, kv_width), BF),
            pltpu.VMEM((kv_width, all_rows), BF),
            pltpu.VMEM((all_rows, kv_width), F32),
            pltpu.VMEM((most, QW), F32),
            pltpu.VMEM((most, QW), BF),
            pltpu.VMEM((most, QW), BF),
            pltpu.VMEM((2 * tokens, q_width), BF),
            pltpu.VMEM((2 * tokens, q_width), BF),
            pltpu.SemaphoreType.DMA((10,)),
            pltpu.SemaphoreType.DMA((4,)),
        ],
        [SMEM] + [HBM] * 2 + [ANY] * 7,
        [ANY] * 4 + [VMEM] * 3,
        ATTEND_BYTES)


def shards(queries, key_rows, value_rows, out_grad, doc_blocks):
    peers = lax.axis_size("ctx")
    sections = lax.axis_size("pipe")

    def move(value, chips, cross):
        pairs = []
        for i in range(peers):
            to = (i // 2 + chips) * 2 + ((i % 2) ^ cross)
            if 0 <= to < peers:
                pairs.append((i, to))
        return lax.ppermute(value, "ctx", pairs)

    def move_back(value, cross):
        pairs = [(p * peers + i, (p - 1) * peers + (i ^ cross))
                 for p in range(1, sections) for i in range(peers)]
        return lax.ppermute(value, ("pipe", "ctx"), pairs)

    q, g = queries[0], out_grad[0]
    near, pair = pack(q, g, key_rows[0], value_rows[0])
    mid = move(near, 1, 0)
    pair, near_pair = move(pair, 0, 1), move(near, 0, 1)
    mid_pair = move(mid, 0, 1)
    far = [move(mid[n], 1, 0) for n in range(len(CHUNKS))]
    outs, q_parts, kv_parts, back = [], [], [], None
    for n in range(len(CHUNKS)):
        if n:
            far[n], _ = lax.optimization_barrier((far[n], near_part))
        o_own, o_pair, dq_own, dq_pair, far_part, mid_part, near_here = attend_chunk(
            n, doc_blocks, q, g, pair, (near, near_pair, mid, mid_pair, far[n], move(far[n], 0, 1)))
        if n:
            far_part, mid_part, *back = lax.optimization_barrier((far_part, mid_part, *back))
            dq_own, dq_pair = join(near_part, *back, dq_own, dq_pair)
            dq_own, dq_pair, *q_parts = lax.optimization_barrier((dq_own, dq_pair, *q_parts))
        near_part = near_here
        back = [move(mid_part, -1, 0), move(far_part, -2, 0)]
        q_parts += [move_back(dq_own, 0), move_back(dq_pair, 1)]
        outs += [o_own, move(o_pair, 0, 1)]
    ours, theirs = add_last(near_part, *back)
    kv_parts = q_parts[2:] + [move_back(ours, 0), move_back(theirs, 1)]
    attn_out = lay_heads(outs)
    grad_query = lay_heads(q_parts)
    grad_key, grad_value = lay_kv(kv_parts)
    return attn_out[None], grad_query[None], grad_key[None], grad_value[None]


def solution(mesh):
    tokens = P("pipe", "ctx", None)
    return jax.shard_map(
        shards,
        mesh=mesh,
        in_specs=(tokens, tokens, tokens, tokens, P("pipe", None)),
        out_specs=(tokens, tokens, tokens, tokens),
        check_vma=False,
    )
```

```python
import functools
import math

import jax
import jax.numpy as jnp
from jax import lax
from jax.experimental import pallas as pl
from jax.experimental.pallas import tpu as pltpu
from jax.sharding import PartitionSpec as P

HD = 128
H = 16
KVH = 4
BLK = 128
MOST_BLK = 8

GROUP = H // KVH
HALF = KVH // 2
QW = GROUP * HD
KV2 = 2 * HD
SCALE = 1.0 / math.sqrt(HD)
LOG2E = math.log2(math.e)
CHUNKS = ((0,), (1,))
SMALL_BYTES = 4 * 1024 * 1024
ATTEND_BYTES = 20 * 1024 * 1024

BF = jnp.bfloat16
F32 = jnp.float32
ANY = pl.BlockSpec(memory_space=pl.ANY)
VMEM = pl.BlockSpec(memory_space=pltpu.VMEM)
SMEM = pl.BlockSpec(memory_space=pltpu.SMEM)


def shape(rows, cols, dtype=BF):
    return jax.ShapeDtypeStruct((rows, cols), dtype)


def cols(start, size):
    return pl.ds(pl.multiple_of(start, HD), size)


def rows(start, size):
    return pl.ds(pl.multiple_of(start, BLK), size)


def call(kernel, name, outs, args, scratch, in_specs=None, out_specs=None, limit=SMALL_BYTES):
    return pl.pallas_call(
        kernel,
        name=name,
        out_shape=outs,
        in_specs=in_specs or [ANY] * len(args),
        out_specs=out_specs or [ANY] * len(outs),
        scratch_shapes=scratch,
        compiler_params=pltpu.CompilerParams(vmem_limit_bytes=limit),
        cost_estimate=pl.CostEstimate(flops=1000, bytes_accessed=1000, transcendentals=0),
    )(*args)


def stage(moves, sems):
    copies = [pltpu.make_async_copy(src, dst, sems.at[n]) for n, (src, dst) in enumerate(moves)]
    for copy in copies:
        copy.start()
    return copies


def wait(copies):
    for copy in copies:
        copy.wait()


def sum_shards(near_ref, mid_ref, far_ref, straight, crossed, at=0):
    core = lax.rem(lax.axis_index("ctx"), 2)
    tokens = straight.shape[0]
    trim = near_ref.shape[0] - far_ref.shape[0]
    to = slice(at, at + near_ref.shape[1])

    def half(out, shard):
        rows_here = slice(shard * tokens, (shard + 1) * tokens)
        total = near_ref[rows_here, :] + mid_ref[rows_here, :].astype(F32)
        if shard == 0:
            out[:trim, to] = total[:trim, :].astype(BF)
            out[trim:, to] = (total[trim:, :] + far_ref[:tokens - trim, :].astype(F32)).astype(BF)
        else:
            out[:, to] = (total + far_ref[tokens - trim:, :].astype(F32)).astype(BF)

    @pl.when(core == 0)
    def _():
        half(straight, 0)
        half(crossed, 1)

    @pl.when(core == 1)
    def _():
        half(straight, 1)
        half(crossed, 0)


def add_last(near, mid, far):
    tokens, width = near.shape[0] // 2, near.shape[1]
    return call(sum_shards, "add_last", [shape(tokens, width)] * 2, (near, mid, far), [],
                [VMEM] * 3, [VMEM] * 2)


def join_kernel(near_ref, mid_ref, far_ref, own_ref, pair_ref, straight, crossed, sems):
    width = own_ref.shape[1]
    copies = stage([(own_ref, straight.at[:, pl.ds(0, width)]),
                    (pair_ref, crossed.at[:, pl.ds(0, width)])], sems)
    sum_shards(near_ref, mid_ref, far_ref, straight, crossed, width)
    wait(copies)


def join(near, mid, far, own, pair):
    tokens, width = own.shape
    return call(join_kernel, "join", [shape(tokens, width + near.shape[1])] * 2,
                (near, mid, far, own, pair), [pltpu.SemaphoreType.DMA((2,))],
                [VMEM] * 3 + [ANY] * 2, [VMEM] * 2)


def lay_heads_kernel(*refs):
    parts, (out, held, in_sems, out_sems) = refs[:-4], refs[-4:]
    core = lax.rem(lax.axis_index("ctx"), 2)
    moves = []
    for n, heads in enumerate(CHUNKS):
        for m, half in ((0, core), (1, 1 - core)):
            width = len(heads) * QW
            moves.append((parts[2 * n + m].at[:, pl.ds(0, width)],
                          held.at[:, cols((half * HALF + heads[0]) * QW, width)]))
    wait(stage(moves, in_sems))
    wait(stage([(held, out)], out_sems))


def lay_heads(parts):
    tokens = parts[0].shape[0]
    return call(
        lay_heads_kernel, "lay_heads", [shape(tokens, H * HD)], parts,
        [pltpu.VMEM((tokens, H * HD), BF),
         pltpu.SemaphoreType.DMA((len(parts),)),
         pltpu.SemaphoreType.DMA((1,))])[0]


def lay_kv_kernel(*refs):
    parts, (key_out, value_out, held, in_sems, out_sems) = refs[:-5], refs[-5:]
    core = lax.rem(lax.axis_index("ctx"), 2)
    moves = []
    for n, heads in enumerate(CHUNKS):
        for m, half in ((0, core), (1, 1 - core)):
            part = parts[2 * n + m]
            first = part.shape[1] - len(heads) * KV2
            for at, head in enumerate(heads):
                dst = cols((half * HALF + head) * HD, HD)
                for side in range(2):
                    src = part.at[:, pl.ds(first + at * KV2 + side * HD, HD)]
                    moves.append((src, held.at[side, :, dst]))
    wait(stage(moves, in_sems))
    wait(stage([(held.at[0], key_out), (held.at[1], value_out)], out_sems))


def lay_kv(parts):
    tokens = parts[0].shape[0]
    return call(
        lay_kv_kernel, "lay_kv", [shape(tokens, KVH * HD)] * 2, parts,
        [pltpu.VMEM((2, tokens, KVH * HD), BF),
         pltpu.SemaphoreType.DMA((4 * HALF,)),
         pltpu.SemaphoreType.DMA((2,))])


def fold8(op, value):
    return op(value.reshape(value.shape[0] // 8, 8, value.shape[1]), axis=0)


def core_kernel(chunk, tokens, doc_ref, q_ref, g_ref, q_pair, g_pair, *rest):
    (kv_refs, (o_own, o_pair, dq_own, dq_pair, far_out, mid_out, near_out,
               q_s, g_s, kv_s, kvt_s, acc_s, s_s, p_s, e_s, d_s, o_s, dq_s, sems, out_sems)) = rest[:12], rest[12:]
    heads = CHUNKS[chunk]
    count = len(heads)
    me = lax.axis_index("ctx")
    chip, core = lax.div(me, 2), lax.rem(me, 2)
    near_at = 4 * tokens
    kv_width = count * KV2
    mine, other = rows(core * tokens, tokens), rows((1 - core) * tokens, tokens)
    q_src = cols((core * HALF + heads[0]) * QW, count * QW)
    moves = [
        (q_ref.at[:, q_src], q_s.at[mine, :]),
        (q_pair.at[:, q_src], q_s.at[other, :]),
        (g_ref.at[:, q_src], g_s.at[mine, :]),
        (g_pair.at[:, q_src], g_s.at[other, :]),
    ]
    for n in range(3):
        for m, shard in ((0, core), (1, 1 - core)):
            at = rows((4 - 2 * n + shard) * tokens, tokens)
            for side in range(2):
                for j, head in enumerate(heads):
                    moves.append((kv_refs[4 * n + 2 * m + side].at[:, cols((core * HALF + head) * HD, HD)],
                                  kv_s.at[at, pl.ds(j * KV2 + side * HD, HD)]))
    copies = [pltpu.make_async_copy(src, dst, sems.at[n]) for n, (src, dst) in enumerate(moves)]
    for copy in copies:
        copy.start()
    acc_s[...] = jnp.zeros_like(acc_s)
    for copy in copies:
        copy.wait()
    blocks = kv_s.shape[0] // BLK
    for at in range(blocks):
        kvt_s[:, at * BLK:(at + 1) * BLK] = kv_s[at * BLK:(at + 1) * BLK, :].T

    def attend(block, at, many, seen):
        span = many * BLK
        base = (block + MOST_BLK + 1 - many) * BLK
        window = rows(base, span)
        tok = rows(block * BLK, BLK)
        key_cols = slice(at * KV2, at * KV2 + HD)
        value_cols = slice(at * KV2 + HD, (at + 1) * KV2)
        q_here, g_here = q_s[tok, at * QW:(at + 1) * QW], g_s[tok, at * QW:(at + 1) * QW]
        qt = jnp.concatenate([q_here[:, n * HD:(n + 1) * HD].T for n in range(GROUP)], axis=1)
        gt = jnp.concatenate([g_here[:, n * HD:(n + 1) * HD].T for n in range(GROUP)], axis=1)
        part = 2 * BLK
        ts = [slice(n * part, (n + 1) * part) for n in range(GROUP * BLK // part)]
        scale_rows = []
        edge = jnp.where(seen < many, F32(-1e30), F32(0.0))
        causal = (lax.broadcasted_iota(jnp.int32, (BLK, BLK), 0)
                  <= lax.broadcasted_iota(jnp.int32, (BLK, BLK), 1))
        causal = jnp.concatenate([causal] * (part // BLK), axis=1)
        keys, values = kv_s[window, key_cols], kv_s[window, value_cols]
        here = [slice(kb * BLK, (kb + 1) * BLK) for kb in range(many)]
        tops = []
        for t in ts:
            s_all = jnp.dot(keys, qt[:, t], preferred_element_type=F32)
            most = None
            for kb in range(many):
                s = s_all[here[kb], :]
                if kb == 0:
                    s = s + edge
                if kb == many - 1:
                    s = jnp.where(causal, s, F32(-1e30))
                s_s[here[kb], t] = s
                top = fold8(jnp.max, s)
                most = top if most is None else jnp.maximum(most, top)
            tops.append(jnp.max(most, axis=0, keepdims=True) * F32(SCALE * LOG2E))
        for t in ts:
            p_s[:span, t] = jnp.dot(values, gt[:, t], preferred_element_type=F32)
        for t, top in zip(ts, tops):
            sums = None
            for kb in range(many):
                e = jnp.exp2(s_s[here[kb], t] * F32(SCALE * LOG2E) - top)
                e_s[here[kb], t] = e.astype(BF)
                total = fold8(jnp.sum, e)
                sums = total if sums is None else sums + total
            scale_rows.append(1.0 / jnp.sum(sums, axis=0, keepdims=True))
        dots = []
        for t, inv in zip(ts, scale_rows):
            ot = jnp.dot(kvt_s[value_cols, cols(base, span)], e_s[:span, t],
                         preferred_element_type=F32) * inv
            ot_low = ot.astype(BF)
            dots.append(jnp.sum(gt[:, t].astype(F32) * ot_low.astype(F32), axis=0, keepdims=True))
            for n in range(part // BLK):
                where = slice(at * QW + t.start + n * BLK, at * QW + t.start + (n + 1) * BLK)
                o_s[tok, where] = ot_low[:, n * BLK:(n + 1) * BLK].T
        for t, inv, dot in zip(ts, scale_rows, dots):
            for kb in range(many):
                d_s[here[kb], t] = e_s[here[kb], t] * (p_s[here[kb], t] - dot).astype(BF)
            dqt = jnp.dot(kvt_s[key_cols, cols(base, span)], d_s[:span, t],
                          preferred_element_type=F32) * (inv * F32(SCALE))
            dqt_low = dqt.astype(BF)
            for n in range(part // BLK):
                where = slice(at * QW + t.start + n * BLK, at * QW + t.start + (n + 1) * BLK)
                dq_s[tok, where] = dqt_low[:, n * BLK:(n + 1) * BLK].T
        inv = jnp.concatenate(scale_rows, axis=1)
        gt_low = (gt.astype(F32) * inv).astype(BF)
        qt_low = (qt.astype(F32) * (inv * F32(SCALE))).astype(BF)
        last = (((1,), (1,)), ((), ()))
        acc_s[window, value_cols] += lax.dot_general(e_s[:span, :], gt_low, last, preferred_element_type=F32)
        acc_s[window, key_cols] += lax.dot_general(d_s[:span, :], qt_low, last, preferred_element_type=F32)

    def step(block, carry):
        place = chip * (2 * tokens // BLK) + block
        doc = doc_ref[0, place]
        seen = jnp.int32(0)
        for back in range(MOST_BLK):
            there = place - back
            same = (there >= 0) & (doc_ref[0, jnp.maximum(there, 0)] == doc)
            seen += same.astype(jnp.int32)
        for many in range(2, MOST_BLK + 1, 2):
            @pl.when((seen == many) | (seen == many - 1))
            def _():
                for at in range(count):
                    attend(block, at, many, seen)
        return carry

    lax.fori_loop(0, 2 * tokens // BLK, step, 0)
    far_out[...] = acc_s[BLK:2 * tokens, :].astype(BF)
    mid_out[...] = acc_s[2 * tokens:near_at, :].astype(BF)
    near_out[...] = acc_s[near_at:, :]
    leaving = [(o_s, o_own, mine), (o_s, o_pair, other), (dq_s, dq_own, mine), (dq_s, dq_pair, other)]
    copies = [pltpu.make_async_copy(src.at[at, :], dst, out_sems.at[n])
              for n, (src, dst, at) in enumerate(leaving)]
    for copy in copies:
        copy.start()
    for copy in copies:
        copy.wait()


def attend_chunk(chunk, docs, heads, kvs):
    tokens = heads[0].shape[0]
    count = len(CHUNKS[chunk])
    kv_width, q_width = count * KV2, count * QW
    all_rows = 6 * tokens
    most = MOST_BLK * BLK
    return call(
        functools.partial(core_kernel, chunk, tokens),
        "attend",
        [shape(tokens, q_width)] * 4 + [
            shape(2 * tokens - BLK, kv_width),
            shape(2 * tokens, kv_width),
            shape(2 * tokens, kv_width, F32),
        ],
        (docs, *heads, *kvs),
        [
            pltpu.VMEM((2 * tokens, q_width), BF),
            pltpu.VMEM((2 * tokens, q_width), BF),
            pltpu.VMEM((all_rows, kv_width), BF),
            pltpu.VMEM((kv_width, all_rows), BF),
            pltpu.VMEM((all_rows, kv_width), F32),
            pltpu.VMEM((most, QW), F32),
            pltpu.VMEM((most, QW), F32),
            pltpu.VMEM((most, QW), BF),
            pltpu.VMEM((most, QW), BF),
            pltpu.VMEM((2 * tokens, q_width), BF),
            pltpu.VMEM((2 * tokens, q_width), BF),
            pltpu.SemaphoreType.DMA((16,)),
            pltpu.SemaphoreType.DMA((4,)),
        ],
        [SMEM] + [ANY] * 16,
        [ANY] * 4 + [VMEM] * 3,
        ATTEND_BYTES)


def shards(queries, key_rows, value_rows, out_grad, doc_blocks):
    peers = lax.axis_size("ctx")
    sections = lax.axis_size("pipe")

    def move(value, chips, cross):
        pairs = []
        for i in range(peers):
            to = (i // 2 + chips) * 2 + ((i % 2) ^ cross)
            if 0 <= to < peers:
                pairs.append((i, to))
        return lax.ppermute(value, "ctx", pairs)

    def move_back(value, cross):
        pairs = [(p * peers + i, (p - 1) * peers + (i ^ cross))
                 for p in range(1, sections) for i in range(peers)]
        return lax.ppermute(value, ("pipe", "ctx"), pairs)

    q, g = queries[0], out_grad[0]
    near = [key_rows[0], value_rows[0]]
    mid = [move(kv, 1, 0) for kv in near]
    near_pair = [move(kv, 0, 1) for kv in near]
    far = [move(kv, 1, 0) for kv in mid]
    q_pair, g_pair = move(q, 0, 1), move(g, 0, 1)
    kvs = near + near_pair
    for both in (mid, far):
        kvs += both + [move(kv, 0, 1) for kv in both]
    outs, q_parts, kv_parts, back = [], [], [], None
    for n in range(len(CHUNKS)):
        o_own, o_pair, dq_own, dq_pair, far_part, mid_part, near_here = attend_chunk(
            n, doc_blocks, (q, g, q_pair, g_pair), kvs)
        if n:
            far_part, mid_part, *back = lax.optimization_barrier((far_part, mid_part, *back))
            dq_own, dq_pair = join(near_part, *back, dq_own, dq_pair)
            dq_own, dq_pair, *q_parts = lax.optimization_barrier((dq_own, dq_pair, *q_parts))
        near_part = near_here
        back = [move(mid_part, -1, 0), move(far_part, -2, 0)]
        q_parts += [move_back(dq_own, 0), move_back(dq_pair, 1)]
        outs += [o_own, move(o_pair, 0, 1)]
    ours, theirs = add_last(near_part, *back)
    kv_parts = q_parts[2:] + [move_back(ours, 0), move_back(theirs, 1)]
    attn_out = lay_heads(outs)
    grad_query = lay_heads(q_parts)
    grad_key, grad_value = lay_kv(kv_parts)
    return attn_out[None], grad_query[None], grad_key[None], grad_value[None]


def solution(mesh):
    tokens = P("pipe", "ctx", None)
    return jax.shard_map(
        shards,
        mesh=mesh,
        in_specs=(tokens, tokens, tokens, tokens, P("pipe", None)),
        out_specs=(tokens, tokens, tokens, tokens),
        check_vma=False,
    )
```

```python
import functools
import math

import jax
import jax.numpy as jnp
from jax import lax
from jax.experimental import pallas as pl
from jax.experimental.pallas import tpu as pltpu
from jax.sharding import PartitionSpec as P

HD = 128
H = 16
KVH = 4
BLK = 128
MOST_BLK = 8

GROUP = H // KVH
HALF = KVH // 2
QW = GROUP * HD
KV2 = 2 * HD
SCALE = 1.0 / math.sqrt(HD)
LOG2E = math.log2(math.e)
CHUNKS = ((0,), (1,))
SMALL_BYTES = 4 * 1024 * 1024
ATTEND_BYTES = 20 * 1024 * 1024

BF = jnp.bfloat16
F32 = jnp.float32
ANY = pl.BlockSpec(memory_space=pl.ANY)
VMEM = pl.BlockSpec(memory_space=pltpu.VMEM)
SMEM = pl.BlockSpec(memory_space=pltpu.SMEM)


def shape(rows, cols, dtype=BF):
    return jax.ShapeDtypeStruct((rows, cols), dtype)


def cols(start, size):
    return pl.ds(pl.multiple_of(start, HD), size)


def rows(start, size):
    return pl.ds(pl.multiple_of(start, BLK), size)


def call(kernel, name, outs, args, scratch, in_specs=None, out_specs=None, limit=SMALL_BYTES):
    return pl.pallas_call(
        kernel,
        name=name,
        out_shape=outs,
        in_specs=in_specs or [ANY] * len(args),
        out_specs=out_specs or [ANY] * len(outs),
        scratch_shapes=scratch,
        compiler_params=pltpu.CompilerParams(vmem_limit_bytes=limit),
        cost_estimate=pl.CostEstimate(flops=1000, bytes_accessed=1000, transcendentals=0),
    )(*args)


def stage(moves, sems):
    copies = [pltpu.make_async_copy(src, dst, sems.at[n]) for n, (src, dst) in enumerate(moves)]
    for copy in copies:
        copy.start()
    return copies


def wait(copies):
    for copy in copies:
        copy.wait()


def sum_shards(near_ref, mid_ref, far_ref, straight, crossed, at=0):
    core = lax.rem(lax.axis_index("ctx"), 2)
    tokens = straight.shape[0]
    trim = near_ref.shape[0] - far_ref.shape[0]
    to = slice(at, at + near_ref.shape[1])

    def half(out, shard):
        rows_here = slice(shard * tokens, (shard + 1) * tokens)
        total = near_ref[rows_here, :] + mid_ref[rows_here, :].astype(F32)
        if shard == 0:
            out[:trim, to] = total[:trim, :].astype(BF)
            out[trim:, to] = (total[trim:, :] + far_ref[:tokens - trim, :].astype(F32)).astype(BF)
        else:
            out[:, to] = (total + far_ref[tokens - trim:, :].astype(F32)).astype(BF)

    @pl.when(core == 0)
    def _():
        half(straight, 0)
        half(crossed, 1)

    @pl.when(core == 1)
    def _():
        half(straight, 1)
        half(crossed, 0)


def add_last(near, mid, far):
    tokens, width = near.shape[0] // 2, near.shape[1]
    return call(sum_shards, "add_last", [shape(tokens, width)] * 2, (near, mid, far), [],
                [VMEM] * 3, [VMEM] * 2)


def join_kernel(near_ref, mid_ref, far_ref, own_ref, pair_ref, straight, crossed, sems):
    width = own_ref.shape[1]
    copies = stage([(own_ref, straight.at[:, pl.ds(0, width)]),
                    (pair_ref, crossed.at[:, pl.ds(0, width)])], sems)
    sum_shards(near_ref, mid_ref, far_ref, straight, crossed, width)
    wait(copies)


def join(near, mid, far, own, pair):
    tokens, width = own.shape
    return call(join_kernel, "join", [shape(tokens, width + near.shape[1])] * 2,
                (near, mid, far, own, pair), [pltpu.SemaphoreType.DMA((2,))],
                [VMEM] * 3 + [ANY] * 2, [VMEM] * 2)


def lay_heads_kernel(*refs):
    parts, (out, held, in_sems, out_sems) = refs[:-4], refs[-4:]
    core = lax.rem(lax.axis_index("ctx"), 2)
    moves = []
    for n, heads in enumerate(CHUNKS):
        for m, half in ((0, core), (1, 1 - core)):
            width = len(heads) * QW
            moves.append((parts[2 * n + m].at[:, pl.ds(0, width)],
                          held.at[:, cols((half * HALF + heads[0]) * QW, width)]))
    wait(stage(moves, in_sems))
    wait(stage([(held, out)], out_sems))


def lay_heads(parts):
    tokens = parts[0].shape[0]
    return call(
        lay_heads_kernel, "lay_heads", [shape(tokens, H * HD)], parts,
        [pltpu.VMEM((tokens, H * HD), BF),
         pltpu.SemaphoreType.DMA((len(parts),)),
         pltpu.SemaphoreType.DMA((1,))])[0]


def lay_kv_kernel(*refs):
    parts, (key_out, value_out, held, in_sems, out_sems) = refs[:-5], refs[-5:]
    core = lax.rem(lax.axis_index("ctx"), 2)
    moves = []
    for n, heads in enumerate(CHUNKS):
        for m, half in ((0, core), (1, 1 - core)):
            part = parts[2 * n + m]
            first = part.shape[1] - len(heads) * KV2
            for at, head in enumerate(heads):
                dst = cols((half * HALF + head) * HD, HD)
                for side in range(2):
                    src = part.at[:, pl.ds(first + at * KV2 + side * HD, HD)]
                    moves.append((src, held.at[side, :, dst]))
    wait(stage(moves, in_sems))
    wait(stage([(held.at[0], key_out), (held.at[1], value_out)], out_sems))


def lay_kv(parts):
    tokens = parts[0].shape[0]
    return call(
        lay_kv_kernel, "lay_kv", [shape(tokens, KVH * HD)] * 2, parts,
        [pltpu.VMEM((2, tokens, KVH * HD), BF),
         pltpu.SemaphoreType.DMA((4 * HALF,)),
         pltpu.SemaphoreType.DMA((2,))])


def fold8(op, value):
    return op(value.reshape(value.shape[0] // 8, 8, value.shape[1]), axis=0)


def core_kernel(chunk, tokens, doc_ref, q_own, g_own, q_pair, g_pair, *rest):
    q_refs, g_refs = (q_own, q_pair), (g_own, g_pair)
    (kv_refs, (o_own, o_pair, dq_own, dq_pair, far_out, mid_out, near_out,
               q_s, g_s, kv_s, kvt_s, acc_s, s_s, p_s, e_s, d_s, o_s, dq_s, out_sems)) = rest[:12], rest[12:]
    heads = CHUNKS[chunk]
    count = len(heads)
    me = lax.axis_index("ctx")
    chip, core = lax.div(me, 2), lax.rem(me, 2)
    near_at = 4 * tokens
    kv_width = count * KV2
    def lay(core):
        other = 1 - core
        for to, sources in ((q_s, q_refs), (g_s, g_refs)):
            for shard, ref, half in ((core, sources[0], 0), (other, sources[1], core)):
                src = slice((half * HALF + heads[0]) * QW, (half * HALF + heads[0] + count) * QW)
                to[shard * tokens:(shard + 1) * tokens, :] = ref[:, src]
        for n in range(3):
            for m, shard in ((0, core), (1, other)):
                at = (4 - 2 * n + shard) * tokens
                half = 0 if n + m == 0 else core
                for side in range(2):
                    for j, head in enumerate(heads):
                        lane = (half * HALF + head) * HD
                        to = j * KV2 + side * HD
                        here = kv_refs[4 * n + 2 * m + side][:, lane:lane + HD]
                        kv_s[at:at + tokens, to:to + HD] = here
                        kvt_s[to:to + HD, at:at + tokens] = here.T

    pl.when(core == 0)(lambda: lay(0))
    pl.when(core == 1)(lambda: lay(1))
    acc_s[...] = jnp.zeros_like(acc_s)

    def attend(block, at, many, seen):
        span = many * BLK
        base = (block + MOST_BLK + 1 - many) * BLK
        window = rows(base, span)
        tok = rows(block * BLK, BLK)
        key_cols = slice(at * KV2, at * KV2 + HD)
        value_cols = slice(at * KV2 + HD, (at + 1) * KV2)
        q_here, g_here = q_s[tok, at * QW:(at + 1) * QW], g_s[tok, at * QW:(at + 1) * QW]
        qt = jnp.concatenate([q_here[:, n * HD:(n + 1) * HD].T for n in range(GROUP)], axis=1)
        gt = jnp.concatenate([g_here[:, n * HD:(n + 1) * HD].T for n in range(GROUP)], axis=1)
        part = 2 * BLK
        ts = [slice(n * part, (n + 1) * part) for n in range(GROUP * BLK // part)]
        scale_rows = []
        edge = jnp.where(seen < many, F32(-1e30), F32(0.0))
        causal = (lax.broadcasted_iota(jnp.int32, (BLK, BLK), 0)
                  <= lax.broadcasted_iota(jnp.int32, (BLK, BLK), 1))
        causal = jnp.concatenate([causal] * (part // BLK), axis=1)
        keys, values = kv_s[window, key_cols], kv_s[window, value_cols]
        here = [slice(kb * BLK, (kb + 1) * BLK) for kb in range(many)]
        tops = []
        for t in ts:
            s_all = jnp.dot(keys, qt[:, t], preferred_element_type=F32)
            most = None
            for kb in range(many):
                s = s_all[here[kb], :]
                if kb == 0:
                    s = s + edge
                if kb == many - 1:
                    s = jnp.where(causal, s, F32(-1e30))
                s_s[here[kb], t] = s
                top = fold8(jnp.max, s)
                most = top if most is None else jnp.maximum(most, top)
            tops.append(jnp.max(most, axis=0, keepdims=True) * F32(SCALE * LOG2E))
        for t in ts:
            p_s[:span, t] = jnp.dot(values, gt[:, t], preferred_element_type=F32)
        for t, top in zip(ts, tops):
            sums = None
            for kb in range(many):
                e = jnp.exp2(s_s[here[kb], t] * F32(SCALE * LOG2E) - top)
                e_s[here[kb], t] = e.astype(BF)
                total = fold8(jnp.sum, e)
                sums = total if sums is None else sums + total
            scale_rows.append(1.0 / jnp.sum(sums, axis=0, keepdims=True))
        dots = []
        for t, inv in zip(ts, scale_rows):
            ot = jnp.dot(kvt_s[value_cols, cols(base, span)], e_s[:span, t],
                         preferred_element_type=F32) * inv
            ot_low = ot.astype(BF)
            dots.append(jnp.sum(gt[:, t].astype(F32) * ot_low.astype(F32), axis=0, keepdims=True))
            for n in range(part // BLK):
                where = slice(at * QW + t.start + n * BLK, at * QW + t.start + (n + 1) * BLK)
                o_s[tok, where] = ot_low[:, n * BLK:(n + 1) * BLK].T
        for t, inv, dot in zip(ts, scale_rows, dots):
            for kb in range(many):
                d_s[here[kb], t] = e_s[here[kb], t] * (p_s[here[kb], t] - dot).astype(BF)
            dqt = jnp.dot(kvt_s[key_cols, cols(base, span)], d_s[:span, t],
                          preferred_element_type=F32) * (inv * F32(SCALE))
            dqt_low = dqt.astype(BF)
            for n in range(part // BLK):
                where = slice(at * QW + t.start + n * BLK, at * QW + t.start + (n + 1) * BLK)
                dq_s[tok, where] = dqt_low[:, n * BLK:(n + 1) * BLK].T
        inv = jnp.concatenate(scale_rows, axis=1)
        gt_low = (gt.astype(F32) * inv).astype(BF)
        qt_low = (qt.astype(F32) * (inv * F32(SCALE))).astype(BF)
        last = (((1,), (1,)), ((), ()))
        acc_s[window, value_cols] += lax.dot_general(e_s[:span, :], gt_low, last, preferred_element_type=F32)
        acc_s[window, key_cols] += lax.dot_general(d_s[:span, :], qt_low, last, preferred_element_type=F32)

    def step(block, carry):
        place = chip * (2 * tokens // BLK) + block
        doc = doc_ref[0, place]
        seen = jnp.int32(0)
        for back in range(MOST_BLK):
            there = place - back
            same = (there >= 0) & (doc_ref[0, jnp.maximum(there, 0)] == doc)
            seen += same.astype(jnp.int32)
        for many in range(2, MOST_BLK + 1, 2):
            @pl.when((seen == many) | (seen == many - 1))
            def _():
                for at in range(count):
                    attend(block, at, many, seen)
        shard, inner = lax.div(block, tokens // BLK), lax.rem(block, tokens // BLK)
        for mine, (o_to, dq_to) in ((True, (o_own, dq_own)), (False, (o_pair, dq_pair))):
            @pl.when((shard == core) == mine)
            def _():
                for copy in leave(block, inner, o_to, dq_to):
                    copy.start()
        return carry

    def leave(block, inner, o_to, dq_to):
        src, dst = rows(block * BLK, BLK), rows(inner * BLK, BLK)
        return (pltpu.make_async_copy(o_s.at[src, :], o_to.at[dst, :], out_sems.at[block, 0]),
                pltpu.make_async_copy(dq_s.at[src, :], dq_to.at[dst, :], out_sems.at[block, 1]))

    lax.fori_loop(0, 2 * tokens // BLK, step, 0)
    far_out[...] = acc_s[BLK:2 * tokens, :].astype(BF)
    mid_out[...] = acc_s[2 * tokens:near_at, :].astype(BF)
    near_out[...] = acc_s[near_at:, :]
    for block in range(2 * tokens // BLK):
        wait(leave(block, block % (tokens // BLK), o_own, dq_own))


def attend_chunk(chunk, docs, heads, kvs):
    tokens = heads[0].shape[0]
    count = len(CHUNKS[chunk])
    kv_width, q_width = count * KV2, count * QW
    all_rows = 6 * tokens
    most = MOST_BLK * BLK
    return call(
        functools.partial(core_kernel, chunk, tokens),
        "attend",
        [shape(tokens, q_width)] * 4 + [
            shape(2 * tokens - BLK, kv_width),
            shape(2 * tokens, kv_width),
            shape(2 * tokens, kv_width, F32),
        ],
        (docs, *heads, *kvs),
        [
            pltpu.VMEM((2 * tokens, q_width), BF),
            pltpu.VMEM((2 * tokens, q_width), BF),
            pltpu.VMEM((all_rows, kv_width), BF),
            pltpu.VMEM((kv_width, all_rows), BF),
            pltpu.VMEM((all_rows, kv_width), F32),
            pltpu.VMEM((most, QW), F32),
            pltpu.VMEM((most, QW), F32),
            pltpu.VMEM((most, QW), BF),
            pltpu.VMEM((most, QW), BF),
            pltpu.VMEM((2 * tokens, q_width), BF),
            pltpu.VMEM((2 * tokens, q_width), BF),
            pltpu.SemaphoreType.DMA((2 * tokens // BLK, 2)),
        ],
        [SMEM] + [VMEM] * 16,
        [ANY] * 4 + [VMEM] * 3,
        ATTEND_BYTES)


def shards(queries, key_rows, value_rows, out_grad, doc_blocks):
    peers = lax.axis_size("ctx")
    sections = lax.axis_size("pipe")

    def move(value, chips, cross):
        pairs = []
        for i in range(peers):
            to = (i // 2 + chips) * 2 + ((i % 2) ^ cross)
            if 0 <= to < peers:
                pairs.append((i, to))
        return lax.ppermute(value, "ctx", pairs)

    def move_back(value, cross):
        pairs = [(p * peers + i, (p - 1) * peers + (i ^ cross))
                 for p in range(1, sections) for i in range(peers)]
        return lax.ppermute(value, ("pipe", "ctx"), pairs)

    q, g = queries[0], out_grad[0]
    near = [key_rows[0], value_rows[0]]
    mid = [move(kv, 1, 0) for kv in near]
    near_pair = [move(kv, 0, 1) for kv in near]
    far = [move(kv, 1, 0) for kv in mid]
    q_pair, g_pair = move(q, 0, 1), move(g, 0, 1)
    core = lax.rem(lax.axis_index("ctx"), 2)

    def own_half(value):
        width = value.shape[1] // 2
        return lax.dynamic_slice(value, (0, core * width), (value.shape[0], width))

    kvs = [own_half(kv) for kv in near] + near_pair
    for both in (mid, far):
        kvs += both + [move(kv, 0, 1) for kv in both]
    outs, q_parts, kv_parts, back = [], [], [], None
    for n in range(len(CHUNKS)):
        o_own, o_pair, dq_own, dq_pair, far_part, mid_part, near_here = attend_chunk(
            n, doc_blocks, (own_half(q), own_half(g), q_pair, g_pair), kvs)
        if n:
            far_part, mid_part, *back = lax.optimization_barrier((far_part, mid_part, *back))
            dq_own, dq_pair = join(near_part, *back, dq_own, dq_pair)
            dq_own, dq_pair, *q_parts = lax.optimization_barrier((dq_own, dq_pair, *q_parts))
        near_part = near_here
        back = [move(mid_part, -1, 0), move(far_part, -2, 0)]
        q_parts += [move_back(dq_own, 0), move_back(dq_pair, 1)]
        outs += [o_own, move(o_pair, 0, 1)]
    ours, theirs = add_last(near_part, *back)
    kv_parts = q_parts[2:] + [move_back(ours, 0), move_back(theirs, 1)]
    attn_out = lay_heads(outs)
    grad_query = lay_heads(q_parts)
    grad_key, grad_value = lay_kv(kv_parts)
    return attn_out[None], grad_query[None], grad_key[None], grad_value[None]


def solution(mesh):
    tokens = P("pipe", "ctx", None)
    return jax.shard_map(
        shards,
        mesh=mesh,
        in_specs=(tokens, tokens, tokens, tokens, P("pipe", None)),
        out_specs=(tokens, tokens, tokens, tokens),
        check_vma=False,
    )
```

```python
import functools
import math

import jax
import jax.numpy as jnp
from jax import lax
from jax.experimental import pallas as pl
from jax.experimental.pallas import tpu as pltpu
from jax.sharding import PartitionSpec as P

HD = 128
H = 16
KVH = 4
BLK = 128
MOST_BLK = 8

GROUP = H // KVH
HALF = KVH // 2
QW = GROUP * HD
KV2 = 2 * HD
SCALE = 1.0 / math.sqrt(HD)
LOG2E = math.log2(math.e)
CHUNKS = ((0,), (1,))
SMALL_BYTES = 4 * 1024 * 1024
ATTEND_BYTES = 20 * 1024 * 1024

BF = jnp.bfloat16
F32 = jnp.float32
ANY = pl.BlockSpec(memory_space=pl.ANY)
VMEM = pl.BlockSpec(memory_space=pltpu.VMEM)
SMEM = pl.BlockSpec(memory_space=pltpu.SMEM)


def shape(rows, cols, dtype=BF):
    return jax.ShapeDtypeStruct((rows, cols), dtype)


def cols(start, size):
    return pl.ds(pl.multiple_of(start, HD), size)


def rows(start, size):
    return pl.ds(pl.multiple_of(start, BLK), size)


def call(kernel, name, outs, args, scratch, in_specs=None, out_specs=None, limit=SMALL_BYTES):
    return pl.pallas_call(
        kernel,
        name=name,
        out_shape=outs,
        in_specs=in_specs or [ANY] * len(args),
        out_specs=out_specs or [ANY] * len(outs),
        scratch_shapes=scratch,
        compiler_params=pltpu.CompilerParams(vmem_limit_bytes=limit),
        cost_estimate=pl.CostEstimate(flops=1000, bytes_accessed=1000, transcendentals=0),
    )(*args)


def stage(moves, sems):
    copies = [pltpu.make_async_copy(src, dst, sems.at[n]) for n, (src, dst) in enumerate(moves)]
    for copy in copies:
        copy.start()
    return copies


def wait(copies):
    for copy in copies:
        copy.wait()


def sum_shards(near_ref, mid_ref, far_ref, straight, crossed, at=0):
    core = lax.rem(lax.axis_index("ctx"), 2)
    tokens = straight.shape[0]
    trim = near_ref.shape[0] - far_ref.shape[0]
    to = slice(at, at + near_ref.shape[1])

    def half(out, shard):
        rows_here = slice(shard * tokens, (shard + 1) * tokens)
        total = near_ref[rows_here, :] + mid_ref[rows_here, :].astype(F32)
        if shard == 0:
            out[:trim, to] = total[:trim, :].astype(BF)
            out[trim:, to] = (total[trim:, :] + far_ref[:tokens - trim, :].astype(F32)).astype(BF)
        else:
            out[:, to] = (total + far_ref[tokens - trim:, :].astype(F32)).astype(BF)

    @pl.when(core == 0)
    def _():
        half(straight, 0)
        half(crossed, 1)

    @pl.when(core == 1)
    def _():
        half(straight, 1)
        half(crossed, 0)


def add_last(near, mid, far):
    tokens, width = near.shape[0] // 2, near.shape[1]
    return call(sum_shards, "add_last", [shape(tokens, width)] * 2, (near, mid, far), [],
                [VMEM] * 3, [VMEM] * 2)


def lay_heads_kernel(*refs):
    parts, (out, held, in_sems, out_sems) = refs[:-4], refs[-4:]
    core = lax.rem(lax.axis_index("ctx"), 2)
    moves = []
    for n, heads in enumerate(CHUNKS):
        for m, half in ((0, core), (1, 1 - core)):
            width = len(heads) * QW
            moves.append((parts[2 * n + m].at[:, pl.ds(0, width)],
                          held.at[:, cols((half * HALF + heads[0]) * QW, width)]))
    wait(stage(moves, in_sems))
    wait(stage([(held, out)], out_sems))


def lay_heads(parts):
    tokens = parts[0].shape[0]
    return call(
        lay_heads_kernel, "lay_heads", [shape(tokens, H * HD)], parts,
        [pltpu.VMEM((tokens, H * HD), BF),
         pltpu.SemaphoreType.DMA((len(parts),)),
         pltpu.SemaphoreType.DMA((1,))])[0]


def lay_kv_kernel(*refs):
    parts, (key_out, value_out, held, in_sems, out_sems) = refs[:-5], refs[-5:]
    core = lax.rem(lax.axis_index("ctx"), 2)
    moves = []
    for n, heads in enumerate(CHUNKS):
        for m, half in ((0, core), (1, 1 - core)):
            part = parts[2 * n + m]
            first = part.shape[1] - len(heads) * KV2
            for at, head in enumerate(heads):
                dst = cols((half * HALF + head) * HD, HD)
                for side in range(2):
                    src = part.at[:, pl.ds(first + at * KV2 + side * HD, HD)]
                    moves.append((src, held.at[side, :, dst]))
    wait(stage(moves, in_sems))
    wait(stage([(held.at[0], key_out), (held.at[1], value_out)], out_sems))


def lay_kv(parts):
    tokens = parts[0].shape[0]
    return call(
        lay_kv_kernel, "lay_kv", [shape(tokens, KVH * HD)] * 2, parts,
        [pltpu.VMEM((2, tokens, KVH * HD), BF),
         pltpu.SemaphoreType.DMA((4 * HALF,)),
         pltpu.SemaphoreType.DMA((2,))])


def fold8(op, value):
    return op(value.reshape(value.shape[0] // 8, 8, value.shape[1]), axis=0)


def core_kernel(chunk, tokens, doc_ref, q_own, g_own, q_pair, g_pair, *rest):
    q_refs, g_refs = (q_own, q_pair), (g_own, g_pair)
    (kv_refs, (o_own, o_pair, dq_own, dq_pair, far_out, mid_out, near_out,
               q_s, g_s, kv_s, kvt_s, acc_s, s_s, p_s, e_s, d_s, o_s, dq_s, sems, out_sems)) = rest[:12], rest[12:]
    heads = CHUNKS[chunk]
    count = len(heads)
    me = lax.axis_index("ctx")
    chip, core = lax.div(me, 2), lax.rem(me, 2)
    near_at = 4 * tokens
    q_src = cols((core * HALF + heads[0]) * QW, count * QW)
    own_src = pl.ds(heads[0] * QW, count * QW)
    moves = []
    for to, (own, pair) in ((q_s, q_refs), (g_s, g_refs)):
        moves += [(own.at[:, own_src], to.at[rows(core * tokens, tokens), :]),
                  (pair.at[:, q_src], to.at[rows((1 - core) * tokens, tokens), :])]
    for n in range(3):
        for m, shard in ((0, core), (1, 1 - core)):
            at = rows((4 - 2 * n + shard) * tokens, tokens)
            half = 0 if n + m == 0 else core
            for side in range(2):
                for j, head in enumerate(heads):
                    moves.append((kv_refs[4 * n + 2 * m + side].at[:, cols((half * HALF + head) * HD, HD)],
                                  kv_s.at[at, pl.ds(j * KV2 + side * HD, HD)]))
    copies = stage(moves, sems)
    acc_s[...] = jnp.zeros_like(acc_s)
    wait(copies)
    for at in range(kv_s.shape[0] // BLK):
        kvt_s[:, at * BLK:(at + 1) * BLK] = kv_s[at * BLK:(at + 1) * BLK, :].T

    def attend(block, at, many, seen):
        span = many * BLK
        base = (block + MOST_BLK + 1 - many) * BLK
        window = rows(base, span)
        tok = rows(block * BLK, BLK)
        key_cols = slice(at * KV2, at * KV2 + HD)
        value_cols = slice(at * KV2 + HD, (at + 1) * KV2)
        q_here, g_here = q_s[tok, at * QW:(at + 1) * QW], g_s[tok, at * QW:(at + 1) * QW]
        qt = jnp.concatenate([q_here[:, n * HD:(n + 1) * HD].T for n in range(GROUP)], axis=1)
        gt = jnp.concatenate([g_here[:, n * HD:(n + 1) * HD].T for n in range(GROUP)], axis=1)
        part = 2 * BLK
        ts = [slice(n * part, (n + 1) * part) for n in range(GROUP * BLK // part)]
        scale_rows = []
        edge = jnp.where(seen < many, F32(-1e30), F32(0.0))
        causal = (lax.broadcasted_iota(jnp.int32, (BLK, BLK), 0)
                  <= lax.broadcasted_iota(jnp.int32, (BLK, BLK), 1))
        causal = jnp.concatenate([causal] * (part // BLK), axis=1)
        keys, values = kv_s[window, key_cols], kv_s[window, value_cols]
        here = [slice(kb * BLK, (kb + 1) * BLK) for kb in range(many)]
        tops = []
        for t in ts:
            s_all = jnp.dot(keys, qt[:, t], preferred_element_type=F32)
            most = None
            for kb in range(many):
                s = s_all[here[kb], :]
                if kb == 0:
                    s = s + edge
                if kb == many - 1:
                    s = jnp.where(causal, s, F32(-1e30))
                s_s[here[kb], t] = s
                top = fold8(jnp.max, s)
                most = top if most is None else jnp.maximum(most, top)
            tops.append(jnp.max(most, axis=0, keepdims=True) * F32(SCALE * LOG2E))
        for t in ts:
            p_s[:span, t] = jnp.dot(values, gt[:, t], preferred_element_type=F32)
        for t, top in zip(ts, tops):
            sums = None
            for kb in range(many):
                e = jnp.exp2(s_s[here[kb], t] * F32(SCALE * LOG2E) - top)
                e_s[here[kb], t] = e.astype(BF)
                total = fold8(jnp.sum, e)
                sums = total if sums is None else sums + total
            scale_rows.append(1.0 / jnp.sum(sums, axis=0, keepdims=True))
        dots = []
        for t, inv in zip(ts, scale_rows):
            ot = jnp.dot(kvt_s[value_cols, cols(base, span)], e_s[:span, t],
                         preferred_element_type=F32) * inv
            ot_low = ot.astype(BF)
            dots.append(jnp.sum(gt[:, t].astype(F32) * ot_low.astype(F32), axis=0, keepdims=True))
            for n in range(part // BLK):
                where = slice(at * QW + t.start + n * BLK, at * QW + t.start + (n + 1) * BLK)
                o_s[tok, where] = ot_low[:, n * BLK:(n + 1) * BLK].T
        inv = jnp.concatenate(scale_rows, axis=1)
        gt_low = (gt.astype(F32) * inv).astype(BF)
        qt_low = (qt.astype(F32) * (inv * F32(SCALE))).astype(BF)
        last = (((1,), (1,)), ((), ()))
        acc_s[window, value_cols] += lax.dot_general(e_s[:span, :], gt_low, last, preferred_element_type=F32)
        for t, inv, dot in zip(ts, scale_rows, dots):
            for kb in range(many):
                d_s[here[kb], t] = e_s[here[kb], t] * (p_s[here[kb], t] - dot).astype(BF)
            dqt = jnp.dot(kvt_s[key_cols, cols(base, span)], d_s[:span, t],
                          preferred_element_type=F32) * (inv * F32(SCALE))
            dqt_low = dqt.astype(BF)
            for n in range(part // BLK):
                where = slice(at * QW + t.start + n * BLK, at * QW + t.start + (n + 1) * BLK)
                dq_s[tok, where] = dqt_low[:, n * BLK:(n + 1) * BLK].T
        acc_s[window, key_cols] += lax.dot_general(d_s[:span, :], qt_low, last, preferred_element_type=F32)

    def step(block, carry):
        place = chip * (2 * tokens // BLK) + block
        doc = doc_ref[0, place]
        seen = jnp.int32(0)
        for back in range(MOST_BLK):
            there = place - back
            same = (there >= 0) & (doc_ref[0, jnp.maximum(there, 0)] == doc)
            seen += same.astype(jnp.int32)
        for many in range(2, MOST_BLK + 1, 2):
            @pl.when((seen == many) | (seen == many - 1))
            def _():
                for at in range(count):
                    attend(block, at, many, seen)
        shard, inner = lax.div(block, tokens // BLK), lax.rem(block, tokens // BLK)
        for mine, (o_to, dq_to) in ((True, (o_own, dq_own)), (False, (o_pair, dq_pair))):
            @pl.when((shard == core) == mine)
            def _():
                for copy in leave(block, inner, o_to, dq_to):
                    copy.start()
        return carry

    def leave(block, inner, o_to, dq_to):
        src, dst = rows(block * BLK, BLK), rows(inner * BLK, BLK)
        return (pltpu.make_async_copy(o_s.at[src, :], o_to.at[dst, :], out_sems.at[block, 0]),
                pltpu.make_async_copy(dq_s.at[src, :], dq_to.at[dst, :], out_sems.at[block, 1]))

    lax.fori_loop(0, 2 * tokens // BLK, step, 0)
    far_out[...] = acc_s[BLK:2 * tokens, :].astype(BF)
    mid_out[...] = acc_s[2 * tokens:near_at, :].astype(BF)
    near_out[...] = acc_s[near_at:, :]
    for block in range(2 * tokens // BLK):
        wait(leave(block, block % (tokens // BLK), o_own, dq_own))


def attend_chunk(chunk, docs, heads, kvs):
    tokens = heads[0].shape[0]
    count = len(CHUNKS[chunk])
    kv_width, q_width = count * KV2, count * QW
    all_rows = 6 * tokens
    most = MOST_BLK * BLK
    return call(
        functools.partial(core_kernel, chunk, tokens),
        "attend",
        [shape(tokens, q_width)] * 4 + [
            shape(2 * tokens - BLK, kv_width),
            shape(2 * tokens, kv_width),
            shape(2 * tokens, kv_width, F32),
        ],
        (docs, *heads, *kvs),
        [
            pltpu.VMEM((2 * tokens, q_width), BF),
            pltpu.VMEM((2 * tokens, q_width), BF),
            pltpu.VMEM((all_rows, kv_width), BF),
            pltpu.VMEM((kv_width, all_rows), BF),
            pltpu.VMEM((all_rows, kv_width), F32),
            pltpu.VMEM((most, QW), F32),
            pltpu.VMEM((most, QW), F32),
            pltpu.VMEM((most, QW), BF),
            pltpu.VMEM((most, QW), BF),
            pltpu.VMEM((2 * tokens, q_width), BF),
            pltpu.VMEM((2 * tokens, q_width), BF),
            pltpu.SemaphoreType.DMA((16,)),
            pltpu.SemaphoreType.DMA((2 * tokens // BLK, 2)),
        ],
        [SMEM] + [ANY] * 16,
        [ANY] * 4 + [VMEM] * 3,
        ATTEND_BYTES)


def shards(queries, key_rows, value_rows, out_grad, doc_blocks):
    peers = lax.axis_size("ctx")
    sections = lax.axis_size("pipe")

    def move(value, chips, cross):
        pairs = []
        for i in range(peers):
            to = (i // 2 + chips) * 2 + ((i % 2) ^ cross)
            if 0 <= to < peers:
                pairs.append((i, to))
        return lax.ppermute(value, "ctx", pairs)

    def move_back(value, cross):
        pairs = [(p * peers + i, (p - 1) * peers + (i ^ cross))
                 for p in range(1, sections) for i in range(peers)]
        return lax.ppermute(value, ("pipe", "ctx"), pairs)

    q, g = queries[0], out_grad[0]
    core = lax.rem(lax.axis_index("ctx"), 2)

    def own_half(value):
        width = value.shape[1] // 2
        return lax.dynamic_slice(value, (0, core * width), (value.shape[0], width))

    near = [key_rows[0], value_rows[0]]
    mid = [move(kv, 1, 0) for kv in near]
    near_pair = [move(kv, 0, 1) for kv in near]
    q_pair, g_pair = move(q, 0, 1), move(g, 0, 1)
    own = [own_half(value) for value in (q, g, *near)]
    mid[1], *own = lax.optimization_barrier((mid[1], *own))
    far = [move(kv, 1, 0) for kv in mid]
    kvs = own[2:] + near_pair
    for both in (mid, far):
        kvs += both + [move(kv, 0, 1) for kv in both]
    outs, q_parts, kv_parts, back = [], [], [], None
    for n in range(len(CHUNKS)):
        o_own, o_pair, dq_own, dq_pair, far_part, mid_part, near_part = attend_chunk(
            n, doc_blocks, (*own[:2], q_pair, g_pair), kvs)
        if n:
            near_before, near_part, *q_parts = lax.optimization_barrier((near_before, near_part, *q_parts))
            ours, theirs = add_last(near_before, *back)
            kv_parts += [move_back(ours, 0), move_back(theirs, 1)]
        near_before = near_part
        q_parts += [move_back(dq_own, 0), move_back(dq_pair, 1)]
        back = [move(mid_part, -1, 0), move(far_part, -2, 0)]
        outs += [o_own, move(o_pair, 0, 1)]
    *gone, near_part = lax.optimization_barrier((*q_parts[2:], *kv_parts, near_part))
    q_parts[2:], kv_parts = gone[:2], gone[2:]
    ours, theirs = add_last(near_part, *back)
    kv_parts += [move_back(ours, 0), move_back(theirs, 1)]
    attn_out = lay_heads(outs)
    grad_query = lay_heads(q_parts)
    grad_key, grad_value = lay_kv(kv_parts)
    return attn_out[None], grad_query[None], grad_key[None], grad_value[None]


def solution(mesh):
    tokens = P("pipe", "ctx", None)
    return jax.shard_map(
        shards,
        mesh=mesh,
        in_specs=(tokens, tokens, tokens, tokens, P("pipe", None)),
        out_specs=(tokens, tokens, tokens, tokens),
        check_vma=False,
    )
```

```python
import functools
import math

import jax
import jax.numpy as jnp
from jax import lax
from jax.experimental import pallas as pl
from jax.experimental.pallas import tpu as pltpu
from jax.sharding import PartitionSpec as P

HD = 128
H = 16
KVH = 4
BLK = 128
MOST_BLK = 8

GROUP = H // KVH
HALF = KVH // 2
QW = GROUP * HD
KV2 = 2 * HD
SCALE = 1.0 / math.sqrt(HD)
LOG2E = math.log2(math.e)
SMALL_BYTES = 4 * 1024 * 1024
FIRST_BYTES = 56 * 1024 * 1024
ATTEND_BYTES = 20 * 1024 * 1024

BF = jnp.bfloat16
F32 = jnp.float32
ANY = pl.BlockSpec(memory_space=pl.ANY)
VMEM = pl.BlockSpec(memory_space=pltpu.VMEM)
SMEM = pl.BlockSpec(memory_space=pltpu.SMEM)


def shape(rows, cols, dtype=BF):
    return jax.ShapeDtypeStruct((rows, cols), dtype)


def cols(start, size):
    return pl.ds(pl.multiple_of(start, HD), size)


def rows(start, size):
    return pl.ds(pl.multiple_of(start, BLK), size)


def call(kernel, name, outs, args, scratch, in_specs=None, out_specs=None, limit=SMALL_BYTES):
    return pl.pallas_call(
        kernel,
        name=name,
        out_shape=outs,
        in_specs=in_specs or [ANY] * len(args),
        out_specs=out_specs or [ANY] * len(outs),
        scratch_shapes=scratch,
        compiler_params=pltpu.CompilerParams(vmem_limit_bytes=limit),
        cost_estimate=pl.CostEstimate(flops=1000, bytes_accessed=1000, transcendentals=0),
    )(*args)


def stage(moves, sems):
    copies = [pltpu.make_async_copy(src, dst, sems.at[n]) for n, (src, dst) in enumerate(moves)]
    for copy in copies:
        copy.start()
    return copies


def wait(copies):
    for copy in copies:
        copy.wait()


def pack_kernel(k_ref, v_ref, q_ref, g_ref, *rest):
    outs, (kv_s, qg_s, in_sems, out_sems) = rest[:4], rest[4:]
    moves = []
    for refs, held in (((k_ref, v_ref), kv_s), ((q_ref, g_ref), qg_s)):
        width = refs[0].shape[1] // 2
        for half in (1, 0):
            for side, ref in enumerate(refs):
                moves.append((ref.at[:, pl.ds(half * width, width)],
                              held.at[half, :, pl.ds(side * width, width)]))
    ins = stage(moves, in_sems)
    leaving = []
    for n, src in enumerate((kv_s.at[1], kv_s.at[0], qg_s.at[1], qg_s.at[0])):
        wait(ins[2 * n:2 * n + 2])
        leaving.append(pltpu.make_async_copy(src, outs[n], out_sems.at[n]))
        leaving[-1].start()
    wait(leaving)


def pack(keys, values, queries, grads):
    kv, qg = keys.shape, queries.shape
    return call(
        pack_kernel, "pack", [shape(*kv)] * 2 + [shape(*qg)] * 2, (keys, values, queries, grads),
        [pltpu.VMEM((2, *kv), BF), pltpu.VMEM((2, *qg), BF),
         pltpu.SemaphoreType.DMA((8,)), pltpu.SemaphoreType.DMA((4,))],
        limit=FIRST_BYTES)


def sum_shards(near_ref, mid_ref, far_ref, straight, crossed, at=0):
    core = lax.rem(lax.axis_index("ctx"), 2)
    tokens = straight.shape[0]
    trim = near_ref.shape[0] - far_ref.shape[0]
    to = slice(at, at + near_ref.shape[1])

    def half(out, shard):
        rows_here = slice(shard * tokens, (shard + 1) * tokens)
        total = near_ref[rows_here, :] + mid_ref[rows_here, :].astype(F32)
        if shard == 0:
            out[:trim, to] = total[:trim, :].astype(BF)
            out[trim:, to] = (total[trim:, :] + far_ref[:tokens - trim, :].astype(F32)).astype(BF)
        else:
            out[:, to] = (total + far_ref[tokens - trim:, :].astype(F32)).astype(BF)

    @pl.when(core == 0)
    def _():
        half(straight, 0)
        half(crossed, 1)

    @pl.when(core == 1)
    def _():
        half(straight, 1)
        half(crossed, 0)


def add_last(near, mid, far):
    tokens, width = near.shape[0] // 2, near.shape[1]
    return call(sum_shards, "add_last", [shape(tokens, width)] * 2, (near, mid, far), [],
                [VMEM] * 3, [VMEM] * 2)


def lay_heads_kernel(blank_last, *refs):
    parts, (out, held, in_sems, out_sems) = refs[:-4], refs[-4:]
    core = lax.rem(lax.axis_index("ctx"), 2)
    moves = []
    for n, part in enumerate(parts):
        half = core if n % 2 == 0 else 1 - core
        moves.append((part, held.at[:, cols((n // 2 * HALF + half) * QW, QW)]))
    wait(stage(moves, in_sems))
    if blank_last:
        @pl.when(lax.axis_index("pipe") == lax.axis_size("pipe") - 1)
        def _():
            held[...] = jnp.zeros_like(held)
    wait(stage([(held, out)], out_sems))


def lay_heads(parts, blank_last):
    tokens = parts[0].shape[0]
    return call(
        functools.partial(lay_heads_kernel, blank_last), "lay_heads", [shape(tokens, H * HD)], parts,
        [pltpu.VMEM((tokens, H * HD), BF),
         pltpu.SemaphoreType.DMA((len(parts),)),
         pltpu.SemaphoreType.DMA((1,))])[0]


def lay_kv_kernel(*refs):
    parts, (key_out, value_out, held, in_sems, out_sems) = refs[:-5], refs[-5:]
    core = lax.rem(lax.axis_index("ctx"), 2)
    moves = []
    for n, part in enumerate(parts):
        half = core if n % 2 == 0 else 1 - core
        dst = cols((n // 2 * HALF + half) * HD, HD)
        for side in range(2):
            moves.append((part.at[:, pl.ds(side * HD, HD)], held.at[side, :, dst]))
    wait(stage(moves, in_sems))

    @pl.when(lax.axis_index("pipe") == lax.axis_size("pipe") - 1)
    def _():
        held[...] = jnp.zeros_like(held)

    wait(stage([(held.at[0], key_out), (held.at[1], value_out)], out_sems))


def lay_kv(parts):
    tokens = parts[0].shape[0]
    return call(
        lay_kv_kernel, "lay_kv", [shape(tokens, KVH * HD)] * 2, parts,
        [pltpu.VMEM((2, tokens, KVH * HD), BF),
         pltpu.SemaphoreType.DMA((2 * KVH,)),
         pltpu.SemaphoreType.DMA((2,))])


def fold8(op, value):
    return op(value.reshape(value.shape[0] // 8, 8, value.shape[1]), axis=0)


def core_kernel(tokens, doc_ref, qg_own, qg_pair, *rest):
    (kv_refs, (o_own, o_pair, dq_own, dq_pair, far_out, mid_out, near_out,
               q_s, g_s, kv_s, kvt_s, acc_s, s_s, p_s, e_s, d_s, o_s, dq_s, sems, out_sems)) = rest[:6], rest[6:]
    me = lax.axis_index("ctx")
    chip, core = lax.div(me, 2), lax.rem(me, 2)
    near_at = 4 * tokens
    mine, other = rows(core * tokens, tokens), rows((1 - core) * tokens, tokens)
    moves = []
    for ref, at in ((qg_own, mine), (qg_pair, other)):
        for side, to in enumerate((q_s, g_s)):
            moves.append((ref.at[:, cols((side * HALF + core) * QW, QW)], to.at[at, :]))
    for n in range(3):
        for m, shard in ((0, core), (1, 1 - core)):
            at = rows((4 - 2 * n + shard) * tokens, tokens)
            for side in range(2):
                moves.append((kv_refs[2 * n + m].at[:, cols((side * HALF + core) * HD, HD)],
                              kv_s.at[at, pl.ds(side * HD, HD)]))
    copies = [pltpu.make_async_copy(src, dst, sems.at[n]) for n, (src, dst) in enumerate(moves)]
    for copy in copies:
        copy.start()
    acc_s[...] = jnp.zeros_like(acc_s)
    for copy in copies:
        copy.wait()
    blocks = kv_s.shape[0] // BLK
    for at in range(blocks):
        kvt_s[:, at * BLK:(at + 1) * BLK] = kv_s[at * BLK:(at + 1) * BLK, :].T

    def attend(block, at, many, seen):
        span = many * BLK
        base = (block + MOST_BLK + 1 - many) * BLK
        window = rows(base, span)
        tok = rows(block * BLK, BLK)
        key_cols = slice(at * KV2, at * KV2 + HD)
        value_cols = slice(at * KV2 + HD, (at + 1) * KV2)
        q_here, g_here = q_s[tok, at * QW:(at + 1) * QW], g_s[tok, at * QW:(at + 1) * QW]
        qt = jnp.concatenate([q_here[:, n * HD:(n + 1) * HD].T for n in range(GROUP)], axis=1)
        gt = jnp.concatenate([g_here[:, n * HD:(n + 1) * HD].T for n in range(GROUP)], axis=1)
        part = 2 * BLK
        ts = [slice(n * part, (n + 1) * part) for n in range(GROUP * BLK // part)]
        scale_rows = []
        edge = jnp.where(seen < many, F32(-1e30), F32(0.0))
        causal = (lax.broadcasted_iota(jnp.int32, (BLK, BLK), 0)
                  <= lax.broadcasted_iota(jnp.int32, (BLK, BLK), 1))
        causal = jnp.concatenate([causal] * (part // BLK), axis=1)
        keys, values = kv_s[window, key_cols], kv_s[window, value_cols]
        here = [slice(kb * BLK, (kb + 1) * BLK) for kb in range(many)]
        tops = []
        for t in ts:
            s_all = jnp.dot(keys, qt[:, t], preferred_element_type=F32)
            most = None
            for kb in range(many):
                s = s_all[here[kb], :]
                if kb == 0:
                    s = s + edge
                if kb == many - 1:
                    s = jnp.where(causal, s, F32(-1e30))
                s_s[here[kb], t] = s
                top = fold8(jnp.max, s)
                most = top if most is None else jnp.maximum(most, top)
            tops.append(jnp.max(most, axis=0, keepdims=True) * F32(SCALE * LOG2E))
        for t in ts:
            p_s[:span, t] = jnp.dot(values, gt[:, t], preferred_element_type=F32)
        for t, top in zip(ts, tops):
            sums = None
            for kb in range(many):
                e = jnp.exp2(s_s[here[kb], t] * F32(SCALE * LOG2E) - top)
                e_s[here[kb], t] = e.astype(BF)
                total = fold8(jnp.sum, e)
                sums = total if sums is None else sums + total
            scale_rows.append(1.0 / jnp.sum(sums, axis=0, keepdims=True))
        dots = []
        for t, inv in zip(ts, scale_rows):
            ot = jnp.dot(kvt_s[value_cols, cols(base, span)], e_s[:span, t],
                         preferred_element_type=F32) * inv
            ot_low = ot.astype(BF)
            dots.append(jnp.sum(gt[:, t].astype(F32) * ot_low.astype(F32), axis=0, keepdims=True))
            for n in range(part // BLK):
                where = slice(at * QW + t.start + n * BLK, at * QW + t.start + (n + 1) * BLK)
                o_s[tok, where] = ot_low[:, n * BLK:(n + 1) * BLK].T
        for t, inv, dot in zip(ts, scale_rows, dots):
            for kb in range(many):
                d_s[here[kb], t] = e_s[here[kb], t] * (p_s[here[kb], t] - dot).astype(BF)
            dqt = jnp.dot(kvt_s[key_cols, cols(base, span)], d_s[:span, t],
                          preferred_element_type=F32) * (inv * F32(SCALE))
            dqt_low = dqt.astype(BF)
            for n in range(part // BLK):
                where = slice(at * QW + t.start + n * BLK, at * QW + t.start + (n + 1) * BLK)
                dq_s[tok, where] = dqt_low[:, n * BLK:(n + 1) * BLK].T
        inv = jnp.concatenate(scale_rows, axis=1)
        gt_low = (gt.astype(F32) * inv).astype(BF)
        qt_low = (qt.astype(F32) * (inv * F32(SCALE))).astype(BF)
        last = (((1,), (1,)), ((), ()))
        acc_s[window, value_cols] += lax.dot_general(e_s[:span, :], gt_low, last, preferred_element_type=F32)
        acc_s[window, key_cols] += lax.dot_general(d_s[:span, :], qt_low, last, preferred_element_type=F32)

    def step(block, carry):
        place = chip * (2 * tokens // BLK) + block
        doc = doc_ref[0, place]
        seen = jnp.int32(0)
        for back in range(MOST_BLK):
            there = place - back
            same = (there >= 0) & (doc_ref[0, jnp.maximum(there, 0)] == doc)
            seen += same.astype(jnp.int32)
        for many in range(2, MOST_BLK + 1, 2):
            @pl.when((seen == many) | (seen == many - 1))
            def _():
                attend(block, 0, many, seen)
        return carry

    lax.fori_loop(0, 2 * tokens // BLK, step, 0)
    far_out[...] = acc_s[BLK:2 * tokens, :].astype(BF)
    mid_out[...] = acc_s[2 * tokens:near_at, :].astype(BF)
    near_out[...] = acc_s[near_at:, :]
    leaving = [(o_s, o_own, mine), (o_s, o_pair, other), (dq_s, dq_own, mine), (dq_s, dq_pair, other)]
    copies = [pltpu.make_async_copy(src.at[at, :], dst, out_sems.at[n])
              for n, (src, dst, at) in enumerate(leaving)]
    for copy in copies:
        copy.start()
    for copy in copies:
        copy.wait()


def attend_half(docs, qg_own, qg_pair, kvs):
    tokens = qg_own.shape[0]
    all_rows = 6 * tokens
    most = MOST_BLK * BLK
    return call(
        functools.partial(core_kernel, tokens),
        "attend",
        [shape(tokens, QW)] * 4 + [
            shape(2 * tokens - BLK, KV2),
            shape(2 * tokens, KV2),
            shape(2 * tokens, KV2, F32),
        ],
        (docs, qg_own, qg_pair, *kvs),
        [
            pltpu.VMEM((2 * tokens, QW), BF),
            pltpu.VMEM((2 * tokens, QW), BF),
            pltpu.VMEM((all_rows, KV2), BF),
            pltpu.VMEM((KV2, all_rows), BF),
            pltpu.VMEM((all_rows, KV2), F32),
            pltpu.VMEM((most, QW), F32),
            pltpu.VMEM((most, QW), F32),
            pltpu.VMEM((most, QW), BF),
            pltpu.VMEM((most, QW), BF),
            pltpu.VMEM((2 * tokens, QW), BF),
            pltpu.VMEM((2 * tokens, QW), BF),
            pltpu.SemaphoreType.DMA((16,)),
            pltpu.SemaphoreType.DMA((4,)),
        ],
        [SMEM] + [ANY] * 8,
        [ANY] * 4 + [VMEM] * 3,
        ATTEND_BYTES)


def shards(queries, key_rows, value_rows, out_grad, doc_blocks):
    peers = lax.axis_size("ctx")
    sections = lax.axis_size("pipe")

    def move(value, chips, cross):
        pairs = []
        for i in range(peers):
            to = (i // 2 + chips) * 2 + ((i % 2) ^ cross)
            if 0 <= to < peers:
                pairs.append((i, to))
        return lax.ppermute(value, "ctx", pairs)

    def pass_on(value, by, cross, ring):
        pairs = [(p * peers + i, (p + by) % sections * peers + (i ^ cross))
                 for p in range(sections) for i in range(peers) if ring or 0 <= p + by < sections]
        return lax.ppermute(value, ("pipe", "ctx"), pairs)

    q, g, k, v = queries[0], out_grad[0], key_rows[0], value_rows[0]

    kv_next, kv_here, qg_next, qg_here = pack(k, v, q, g)
    kv_next = pass_on(kv_next, -1, 0, True)
    docs_next = pass_on(doc_blocks, -1, 0, True)
    def with_pair(kv):
        return [kv, move(kv, 0, 1)]

    mid_here = move(kv_here, 1, 0)
    kv_next, mid_here, docs_next, qg_next = lax.optimization_barrier((kv_next, mid_here, docs_next, qg_next))
    qg_next = pass_on(qg_next, -1, 0, True)
    mid_next = move(kv_next, 1, 0)
    kvs = with_pair(kv_here) + with_pair(mid_here) + with_pair(move(mid_here, 1, 0))
    far_next = move(mid_next, 1, 0)
    kvs_next = with_pair(kv_next) + with_pair(mid_next) + with_pair(far_next)
    *kvs, kvs_next[-1] = lax.optimization_barrier((*kvs, kvs_next[-1]))
    o_own, o_pair, dq_own, dq_pair, far, mid, near = attend_half(
        doc_blocks, *with_pair(qg_here), kvs)
    qg_next, near = lax.optimization_barrier((qg_next, near))
    back = [move(mid, -1, 0), move(far, -2, 0)]
    q_parts = [pass_on(dq_own, -1, 0, False), pass_on(dq_pair, -1, 1, False)]
    outs = [o_own, move(o_pair, 0, 1)]
    o_own, o_pair, dq_own, dq_pair, far, mid, near_next = attend_half(
        docs_next, *with_pair(qg_next), kvs_next)
    near, near_next, *q_parts = lax.optimization_barrier((near, near_next, *q_parts))
    back_next = [move(mid, -1, 0), move(far, -2, 0)]
    outs += [pass_on(o_own, 1, 0, True), pass_on(o_pair, 1, 1, True)]
    q_parts += [dq_own, move(dq_pair, 0, 1)]
    ours, theirs = add_last(near, *back)
    kv_parts = [pass_on(ours, -1, 0, False), pass_on(theirs, -1, 1, False)]
    attn_out = lay_heads(outs, False)
    ours, theirs = add_last(near_next, *back_next)
    kv_parts += [ours, move(theirs, 0, 1)]
    grad_query = lay_heads(q_parts, True)
    grad_key, grad_value = lay_kv(kv_parts)
    return attn_out[None], grad_query[None], grad_key[None], grad_value[None]


def solution(mesh):
    tokens = P("pipe", "ctx", None)
    return jax.shard_map(
        shards,
        mesh=mesh,
        in_specs=(tokens, tokens, tokens, tokens, P("pipe", None)),
        out_specs=(tokens, tokens, tokens, tokens),
        check_vma=False,
    )
```

```python
import functools
import math

import jax
import jax.numpy as jnp
from jax import lax
from jax.experimental import pallas as pl
from jax.experimental.pallas import tpu as pltpu
from jax.sharding import PartitionSpec as P

HD = 128
H = 16
KVH = 4
BLK = 128
MOST_BLK = 8

GROUP = H // KVH
HALF = KVH // 2
QW = GROUP * HD
KV2 = 2 * HD
SCALE = 1.0 / math.sqrt(HD)
LOG2E = math.log2(math.e)
SMALL_BYTES = 4 * 1024 * 1024
FIRST_BYTES = 56 * 1024 * 1024
ATTEND_BYTES = 20 * 1024 * 1024

BF = jnp.bfloat16
F32 = jnp.float32
ANY = pl.BlockSpec(memory_space=pl.ANY)
VMEM = pl.BlockSpec(memory_space=pltpu.VMEM)
SMEM = pl.BlockSpec(memory_space=pltpu.SMEM)


def shape(rows, cols, dtype=BF):
    return jax.ShapeDtypeStruct((rows, cols), dtype)


def cols(start, size):
    return pl.ds(pl.multiple_of(start, HD), size)


def rows(start, size):
    return pl.ds(pl.multiple_of(start, BLK), size)


def call(kernel, name, outs, args, scratch, in_specs=None, out_specs=None, limit=SMALL_BYTES):
    return pl.pallas_call(
        kernel,
        name=name,
        out_shape=outs,
        in_specs=in_specs or [ANY] * len(args),
        out_specs=out_specs or [ANY] * len(outs),
        scratch_shapes=scratch,
        compiler_params=pltpu.CompilerParams(vmem_limit_bytes=limit),
        cost_estimate=pl.CostEstimate(flops=1000, bytes_accessed=1000, transcendentals=0),
    )(*args)


def stage(moves, sems):
    copies = [pltpu.make_async_copy(src, dst, sems.at[n]) for n, (src, dst) in enumerate(moves)]
    for copy in copies:
        copy.start()
    return copies


def wait(copies):
    for copy in copies:
        copy.wait()


def pack_kernel(k_ref, v_ref, q_ref, g_ref, *rest):
    outs, (kv_s, qg_s, in_sems, out_sems) = rest[:4], rest[4:]
    moves = []
    for refs, held in (((k_ref, v_ref), kv_s), ((q_ref, g_ref), qg_s)):
        width = refs[0].shape[1] // 2
        for half in (1, 0):
            for side, ref in enumerate(refs):
                moves.append((ref.at[:, pl.ds(half * width, width)],
                              held.at[half, :, pl.ds(side * width, width)]))
    ins = stage(moves, in_sems)
    leaving = []
    for n, src in enumerate((kv_s.at[1], kv_s.at[0], qg_s.at[1], qg_s.at[0])):
        wait(ins[2 * n:2 * n + 2])
        leaving.append(pltpu.make_async_copy(src, outs[n], out_sems.at[n]))
        leaving[-1].start()
    wait(leaving)


def pack(keys, values, queries, grads):
    kv, qg = keys.shape, queries.shape
    return call(
        pack_kernel, "pack", [shape(*kv)] * 2 + [shape(*qg)] * 2, (keys, values, queries, grads),
        [pltpu.VMEM((2, *kv), BF), pltpu.VMEM((2, *qg), BF),
         pltpu.SemaphoreType.DMA((8,)), pltpu.SemaphoreType.DMA((4,))],
        limit=FIRST_BYTES)


def sum_shards(near_ref, mid_ref, far_ref, straight, crossed, at=0):
    core = lax.rem(lax.axis_index("ctx"), 2)
    tokens = straight.shape[0]
    trim = near_ref.shape[0] - far_ref.shape[0]
    to = slice(at, at + near_ref.shape[1])

    def half(out, shard):
        rows_here = slice(shard * tokens, (shard + 1) * tokens)
        total = near_ref[rows_here, :] + mid_ref[rows_here, :].astype(F32)
        if shard == 0:
            out[:trim, to] = total[:trim, :].astype(BF)
            out[trim:, to] = (total[trim:, :] + far_ref[:tokens - trim, :].astype(F32)).astype(BF)
        else:
            out[:, to] = (total + far_ref[tokens - trim:, :].astype(F32)).astype(BF)

    @pl.when(core == 0)
    def _():
        half(straight, 0)
        half(crossed, 1)

    @pl.when(core == 1)
    def _():
        half(straight, 1)
        half(crossed, 0)


def add_last(near, mid, far):
    tokens, width = near.shape[0] // 2, near.shape[1]
    return call(sum_shards, "add_last", [shape(tokens, width)] * 2, (near, mid, far), [],
                [VMEM] * 3, [VMEM] * 2)


def lay_heads_kernel(blank_last, *refs):
    parts, (out, held, in_sems, out_sems) = refs[:-4], refs[-4:]
    core = lax.rem(lax.axis_index("ctx"), 2)
    moves = []
    for n, part in enumerate(parts):
        half = core if n % 2 == 0 else 1 - core
        moves.append((part, held.at[:, cols((n // 2 * HALF + half) * QW, QW)]))
    wait(stage(moves, in_sems))
    if blank_last:
        @pl.when(lax.axis_index("pipe") == lax.axis_size("pipe") - 1)
        def _():
            held[...] = jnp.zeros_like(held)
    wait(stage([(held, out)], out_sems))


def lay_heads(parts, blank_last):
    tokens = parts[0].shape[0]
    return call(
        functools.partial(lay_heads_kernel, blank_last), "lay_heads", [shape(tokens, H * HD)], parts,
        [pltpu.VMEM((tokens, H * HD), BF),
         pltpu.SemaphoreType.DMA((len(parts),)),
         pltpu.SemaphoreType.DMA((1,))])[0]


def lay_kv_kernel(*refs):
    parts, (key_out, value_out, held, in_sems, out_sems) = refs[:-5], refs[-5:]
    core = lax.rem(lax.axis_index("ctx"), 2)
    moves = []
    for n, part in enumerate(parts):
        half = core if n % 2 == 0 else 1 - core
        dst = cols((n // 2 * HALF + half) * HD, HD)
        for side in range(2):
            moves.append((part.at[:, pl.ds(side * HD, HD)], held.at[side, :, dst]))
    wait(stage(moves, in_sems))

    @pl.when(lax.axis_index("pipe") == lax.axis_size("pipe") - 1)
    def _():
        held[...] = jnp.zeros_like(held)

    wait(stage([(held.at[0], key_out), (held.at[1], value_out)], out_sems))


def lay_kv(parts):
    tokens = parts[0].shape[0]
    return call(
        lay_kv_kernel, "lay_kv", [shape(tokens, KVH * HD)] * 2, parts,
        [pltpu.VMEM((2, tokens, KVH * HD), BF),
         pltpu.SemaphoreType.DMA((2 * KVH,)),
         pltpu.SemaphoreType.DMA((2,))])


def fold8(op, value):
    return op(value.reshape(value.shape[0] // 8, 8, value.shape[1]), axis=0)


def core_kernel(tokens, doc_ref, qg_own, qg_pair, *rest):
    (kv_refs, (o_own, o_pair, dq_own, dq_pair, far_out, mid_out, near_out,
               q_s, g_s, kv_s, kvt_s, acc_s, s_s, p_s, e_s, d_s, o_s, dq_s, sems, out_sems)) = rest[:6], rest[6:]
    me = lax.axis_index("ctx")
    chip, core = lax.div(me, 2), lax.rem(me, 2)
    near_at = 4 * tokens
    mine, other = rows(core * tokens, tokens), rows((1 - core) * tokens, tokens)
    moves = []
    for ref, at in ((qg_own, mine), (qg_pair, other)):
        for side, to in enumerate((q_s, g_s)):
            moves.append((ref.at[:, cols((side * HALF + core) * QW, QW)], to.at[at, :]))
    for n in range(3):
        for m, shard in ((0, core), (1, 1 - core)):
            at = rows((4 - 2 * n + shard) * tokens, tokens)
            for side in range(2):
                moves.append((kv_refs[2 * n + m].at[:, cols((side * HALF + core) * HD, HD)],
                              kv_s.at[at, pl.ds(side * HD, HD)]))
    copies = [pltpu.make_async_copy(src, dst, sems.at[n]) for n, (src, dst) in enumerate(moves)]
    for copy in copies:
        copy.start()
    acc_s[...] = jnp.zeros_like(acc_s)
    for copy in copies:
        copy.wait()
    blocks = kv_s.shape[0] // BLK
    for at in range(blocks):
        kvt_s[:, at * BLK:(at + 1) * BLK] = kv_s[at * BLK:(at + 1) * BLK, :].T

    def attend(block, at, many, seen):
        span = many * BLK
        base = (block + MOST_BLK + 1 - many) * BLK
        window = rows(base, span)
        tok = rows(block * BLK, BLK)
        key_cols = slice(at * KV2, at * KV2 + HD)
        value_cols = slice(at * KV2 + HD, (at + 1) * KV2)
        q_here, g_here = q_s[tok, at * QW:(at + 1) * QW], g_s[tok, at * QW:(at + 1) * QW]
        qt = jnp.concatenate([q_here[:, n * HD:(n + 1) * HD].T for n in range(GROUP)], axis=1)
        gt = jnp.concatenate([g_here[:, n * HD:(n + 1) * HD].T for n in range(GROUP)], axis=1)
        part = 2 * BLK
        ts = [slice(n * part, (n + 1) * part) for n in range(GROUP * BLK // part)]
        scale_rows = []
        edge = jnp.where(seen < many, F32(-1e30), F32(0.0))
        causal = (lax.broadcasted_iota(jnp.int32, (BLK, BLK), 0)
                  <= lax.broadcasted_iota(jnp.int32, (BLK, BLK), 1))
        causal = jnp.concatenate([causal] * (part // BLK), axis=1)
        keys, values = kv_s[window, key_cols], kv_s[window, value_cols]
        here = [slice(kb * BLK, (kb + 1) * BLK) for kb in range(many)]
        tops = []
        for t in ts:
            s_all = jnp.dot(keys, qt[:, t], preferred_element_type=F32)
            most = None
            for kb in range(many):
                s = s_all[here[kb], :]
                if kb == 0:
                    s = s + edge
                if kb == many - 1:
                    s = jnp.where(causal, s, F32(-1e30))
                s_s[here[kb], t] = s
                top = fold8(jnp.max, s)
                most = top if most is None else jnp.maximum(most, top)
            tops.append(jnp.max(most, axis=0, keepdims=True) * F32(SCALE * LOG2E))
        for t in ts:
            p_s[:span, t] = jnp.dot(values, gt[:, t], preferred_element_type=F32)
        for t, top in zip(ts, tops):
            sums = None
            for kb in range(many):
                e = jnp.exp2(s_s[here[kb], t] * F32(SCALE * LOG2E) - top)
                e_s[here[kb], t] = e.astype(BF)
                total = fold8(jnp.sum, e)
                sums = total if sums is None else sums + total
            scale_rows.append(1.0 / jnp.sum(sums, axis=0, keepdims=True))
        dots = []
        for t, inv in zip(ts, scale_rows):
            ot = jnp.dot(kvt_s[value_cols, cols(base, span)], e_s[:span, t],
                         preferred_element_type=F32) * inv
            ot_low = ot.astype(BF)
            dots.append(jnp.sum(gt[:, t].astype(F32) * ot_low.astype(F32), axis=0, keepdims=True))
            for n in range(part // BLK):
                where = slice(at * QW + t.start + n * BLK, at * QW + t.start + (n + 1) * BLK)
                o_s[tok, where] = ot_low[:, n * BLK:(n + 1) * BLK].T
        for t, inv, dot in zip(ts, scale_rows, dots):
            for kb in range(many):
                d_s[here[kb], t] = e_s[here[kb], t] * (p_s[here[kb], t] - dot).astype(BF)
            dqt = jnp.dot(kvt_s[key_cols, cols(base, span)], d_s[:span, t],
                          preferred_element_type=F32) * (inv * F32(SCALE))
            dqt_low = dqt.astype(BF)
            for n in range(part // BLK):
                where = slice(at * QW + t.start + n * BLK, at * QW + t.start + (n + 1) * BLK)
                dq_s[tok, where] = dqt_low[:, n * BLK:(n + 1) * BLK].T
        inv = jnp.concatenate(scale_rows, axis=1)
        gt_low = (gt.astype(F32) * inv).astype(BF)
        qt_low = (qt.astype(F32) * (inv * F32(SCALE))).astype(BF)
        last = (((1,), (1,)), ((), ()))
        acc_s[window, value_cols] += lax.dot_general(e_s[:span, :], gt_low, last, preferred_element_type=F32)
        acc_s[window, key_cols] += lax.dot_general(d_s[:span, :], qt_low, last, preferred_element_type=F32)

    def step(block, carry):
        place = chip * (2 * tokens // BLK) + block
        doc = doc_ref[0, place]
        seen = jnp.int32(0)
        for back in range(MOST_BLK):
            there = place - back
            same = (there >= 0) & (doc_ref[0, jnp.maximum(there, 0)] == doc)
            seen += same.astype(jnp.int32)
        for many in range(2, MOST_BLK + 1, 2):
            @pl.when((seen == many) | (seen == many - 1))
            def _():
                attend(block, 0, many, seen)
        return carry

    lax.fori_loop(0, 2 * tokens // BLK, step, 0)
    far_out[...] = acc_s[BLK:2 * tokens, :].astype(BF)
    mid_out[...] = acc_s[2 * tokens:near_at, :].astype(BF)
    near_out[...] = acc_s[near_at:, :]
    leaving = [(o_s, o_own, mine), (o_s, o_pair, other), (dq_s, dq_own, mine), (dq_s, dq_pair, other)]
    copies = [pltpu.make_async_copy(src.at[at, :], dst, out_sems.at[n])
              for n, (src, dst, at) in enumerate(leaving)]
    for copy in copies:
        copy.start()
    for copy in copies:
        copy.wait()


def attend_half(docs, qg_own, qg_pair, kvs):
    tokens = qg_own.shape[0]
    all_rows = 6 * tokens
    most = MOST_BLK * BLK
    return call(
        functools.partial(core_kernel, tokens),
        "attend",
        [shape(tokens, QW)] * 4 + [
            shape(2 * tokens - BLK, KV2),
            shape(2 * tokens, KV2),
            shape(2 * tokens, KV2, F32),
        ],
        (docs, qg_own, qg_pair, *kvs),
        [
            pltpu.VMEM((2 * tokens, QW), BF),
            pltpu.VMEM((2 * tokens, QW), BF),
            pltpu.VMEM((all_rows, KV2), BF),
            pltpu.VMEM((KV2, all_rows), BF),
            pltpu.VMEM((all_rows, KV2), F32),
            pltpu.VMEM((most, QW), F32),
            pltpu.VMEM((most, QW), F32),
            pltpu.VMEM((most, QW), BF),
            pltpu.VMEM((most, QW), BF),
            pltpu.VMEM((2 * tokens, QW), BF),
            pltpu.VMEM((2 * tokens, QW), BF),
            pltpu.SemaphoreType.DMA((16,)),
            pltpu.SemaphoreType.DMA((4,)),
        ],
        [SMEM] + [ANY] * 8,
        [ANY] * 4 + [VMEM] * 3,
        ATTEND_BYTES)


def shards(queries, key_rows, value_rows, out_grad, doc_blocks):
    peers = lax.axis_size("ctx")
    sections = lax.axis_size("pipe")

    def move(value, chips, cross):
        pairs = [(i, (i // 2 + chips) % (peers // 2) * 2 + ((i % 2) ^ cross)) for i in range(peers)]
        return lax.ppermute(value, "ctx", pairs)

    def pass_on(value, by, cross):
        pairs = [(p * peers + i, (p + by) % sections * peers + (i ^ cross))
                 for p in range(sections) for i in range(peers)]
        return lax.ppermute(value, ("pipe", "ctx"), pairs)

    q, g, k, v = queries[0], out_grad[0], key_rows[0], value_rows[0]

    kv_next, kv_here, qg_next, qg_here = pack(k, v, q, g)
    kv_next = pass_on(kv_next, -1, 0)
    docs_next = pass_on(doc_blocks, -1, 0)
    def with_pair(kv):
        return [kv, move(kv, 0, 1)]

    mid_here = move(kv_here, 1, 0)
    kv_next, mid_here, docs_next, qg_next = lax.optimization_barrier((kv_next, mid_here, docs_next, qg_next))
    qg_next = pass_on(qg_next, -1, 0)
    mid_next = move(kv_next, 1, 0)
    kvs = with_pair(kv_here) + with_pair(mid_here) + with_pair(move(mid_here, 1, 0))
    far_next = move(mid_next, 1, 0)
    kvs_next = with_pair(kv_next) + with_pair(mid_next) + with_pair(far_next)
    *kvs, kvs_next[-1] = lax.optimization_barrier((*kvs, kvs_next[-1]))
    o_own, o_pair, dq_own, dq_pair, far, mid, near = attend_half(
        doc_blocks, *with_pair(qg_here), kvs)
    qg_next, near = lax.optimization_barrier((qg_next, near))
    back = [move(mid, -1, 0), move(far, -2, 0)]
    q_parts = [pass_on(dq_own, -1, 0), pass_on(dq_pair, -1, 1)]
    outs = [o_own, move(o_pair, 0, 1)]
    o_own, o_pair, dq_own, dq_pair, far, mid, near_next = attend_half(
        docs_next, *with_pair(qg_next), kvs_next)
    near, near_next, *q_parts = lax.optimization_barrier((near, near_next, *q_parts))
    back_next = [move(mid, -1, 0), move(far, -2, 0)]
    outs += [pass_on(o_own, 1, 0), pass_on(o_pair, 1, 1)]
    q_parts += [dq_own, move(dq_pair, 0, 1)]
    ours, theirs = add_last(near, *back)
    kv_parts = [pass_on(ours, -1, 0), pass_on(theirs, -1, 1)]
    attn_out = lay_heads(outs, False)
    ours, theirs = add_last(near_next, *back_next)
    kv_parts += [ours, move(theirs, 0, 1)]
    grad_query = lay_heads(q_parts, True)
    grad_key, grad_value = lay_kv(kv_parts)
    return attn_out[None], grad_query[None], grad_key[None], grad_value[None]


def solution(mesh):
    tokens = P("pipe", "ctx", None)
    return jax.shard_map(
        shards,
        mesh=mesh,
        in_specs=(tokens, tokens, tokens, tokens, P("pipe", None)),
        out_specs=(tokens, tokens, tokens, tokens),
        check_vma=False,
    )
```

```python
import functools
import math

import jax
import jax.numpy as jnp
from jax import lax
from jax.experimental import pallas as pl
from jax.experimental.pallas import tpu as pltpu
from jax.sharding import PartitionSpec as P

HD = 128
H = 16
KVH = 4
BLK = 128
MOST_BLK = 8

GROUP = H // KVH
HALF = KVH // 2
QW = GROUP * HD
KV2 = 2 * HD
SCALE = 1.0 / math.sqrt(HD)
LOG2E = math.log2(math.e)
SMALL_BYTES = 4 * 1024 * 1024
FIRST_BYTES = 56 * 1024 * 1024
ATTEND_BYTES = 20 * 1024 * 1024
ATTEND_FLOPS = 8 * 10 ** 9

BF = jnp.bfloat16
F32 = jnp.float32
ANY = pl.BlockSpec(memory_space=pl.ANY)
VMEM = pl.BlockSpec(memory_space=pltpu.VMEM)
SMEM = pl.BlockSpec(memory_space=pltpu.SMEM)


def shape(rows, cols, dtype=BF):
    return jax.ShapeDtypeStruct((rows, cols), dtype)


def cols(start, size):
    return pl.ds(pl.multiple_of(start, HD), size)


def rows(start, size):
    return pl.ds(pl.multiple_of(start, BLK), size)


def call(kernel, name, outs, args, scratch, in_specs=None, out_specs=None, limit=SMALL_BYTES, flops=1000):
    return pl.pallas_call(
        kernel,
        name=name,
        out_shape=outs,
        in_specs=in_specs or [ANY] * len(args),
        out_specs=out_specs or [ANY] * len(outs),
        scratch_shapes=scratch,
        compiler_params=pltpu.CompilerParams(vmem_limit_bytes=limit),
        cost_estimate=pl.CostEstimate(flops=flops, bytes_accessed=1000, transcendentals=0),
    )(*args)


def stage(moves, sems):
    copies = [pltpu.make_async_copy(src, dst, sems.at[n]) for n, (src, dst) in enumerate(moves)]
    for copy in copies:
        copy.start()
    return copies


def wait(copies):
    for copy in copies:
        copy.wait()


def pack_kernel(k_ref, v_ref, q_ref, g_ref, *rest):
    outs, (kv_s, qg_s, in_sems, out_sems) = rest[:3], rest[3:]
    moves = []
    for refs, held, half in (((k_ref, v_ref), kv_s.at[1], 1), ((k_ref, v_ref), kv_s.at[0], 0),
                             ((q_ref, g_ref), qg_s, 1)):
        width = refs[0].shape[1] // 2
        for side, ref in enumerate(refs):
            moves.append((ref.at[:, pl.ds(half * width, width)], held.at[:, pl.ds(side * width, width)]))
    ins = stage(moves, in_sems)
    leaving = []
    for n, src in enumerate((kv_s.at[1], kv_s.at[0], qg_s)):
        wait(ins[2 * n:2 * n + 2])
        leaving.append(pltpu.make_async_copy(src, outs[n], out_sems.at[n]))
        leaving[-1].start()
    wait(leaving)


def pack(keys, values, queries, grads):
    kv, qg = keys.shape, queries.shape
    return call(
        pack_kernel, "pack", [shape(*kv)] * 2 + [shape(*qg)], (keys, values, queries, grads),
        [pltpu.VMEM((2, *kv), BF), pltpu.VMEM(qg, BF),
         pltpu.SemaphoreType.DMA((6,)), pltpu.SemaphoreType.DMA((3,))],
        limit=FIRST_BYTES)


def sum_shards(near_ref, mid_ref, far_ref, straight, crossed, at=0):
    core = lax.rem(lax.axis_index("ctx"), 2)
    tokens = straight.shape[0]
    trim = near_ref.shape[0] - far_ref.shape[0]
    to = slice(at, at + near_ref.shape[1])

    def half(out, shard):
        rows_here = slice(shard * tokens, (shard + 1) * tokens)
        total = near_ref[rows_here, :] + mid_ref[rows_here, :].astype(F32)
        if shard == 0:
            out[:trim, to] = total[:trim, :].astype(BF)
            out[trim:, to] = (total[trim:, :] + far_ref[:tokens - trim, :].astype(F32)).astype(BF)
        else:
            out[:, to] = (total + far_ref[tokens - trim:, :].astype(F32)).astype(BF)

    @pl.when(core == 0)
    def _():
        half(straight, 0)
        half(crossed, 1)

    @pl.when(core == 1)
    def _():
        half(straight, 1)
        half(crossed, 0)


def add_last(near, mid, far):
    tokens, width = near.shape[0] // 2, near.shape[1]
    return call(sum_shards, "add_last", [shape(tokens, width)] * 2, (near, mid, far), [],
                [VMEM] * 3, [VMEM] * 2)


def lay_heads_kernel(blank_last, *refs):
    parts, (out, held, in_sems, out_sems) = refs[:-4], refs[-4:]
    core = lax.rem(lax.axis_index("ctx"), 2)
    moves = []
    for n, part in enumerate(parts):
        half = core if n % 2 == 0 else 1 - core
        moves.append((part, held.at[:, cols((n // 2 * HALF + half) * QW, QW)]))
    wait(stage(moves, in_sems))
    if blank_last:
        @pl.when(lax.axis_index("pipe") == lax.axis_size("pipe") - 1)
        def _():
            held[...] = jnp.zeros_like(held)
    wait(stage([(held, out)], out_sems))


def lay_heads(parts, blank_last):
    tokens = parts[0].shape[0]
    return call(
        functools.partial(lay_heads_kernel, blank_last), "lay_heads", [shape(tokens, H * HD)], parts,
        [pltpu.VMEM((tokens, H * HD), BF),
         pltpu.SemaphoreType.DMA((len(parts),)),
         pltpu.SemaphoreType.DMA((1,))])[0]


def lay_kv_kernel(*refs):
    parts, (key_out, value_out, held, in_sems, out_sems) = refs[:-5], refs[-5:]
    core = lax.rem(lax.axis_index("ctx"), 2)
    moves = []
    for n, part in enumerate(parts):
        half = core if n % 2 == 0 else 1 - core
        dst = cols((n // 2 * HALF + half) * HD, HD)
        for side in range(2):
            moves.append((part.at[:, pl.ds(side * HD, HD)], held.at[side, :, dst]))
    wait(stage(moves, in_sems))

    @pl.when(lax.axis_index("pipe") == lax.axis_size("pipe") - 1)
    def _():
        held[...] = jnp.zeros_like(held)

    wait(stage([(held.at[0], key_out), (held.at[1], value_out)], out_sems))


def lay_kv(parts):
    tokens = parts[0].shape[0]
    return call(
        lay_kv_kernel, "lay_kv", [shape(tokens, KVH * HD)] * 2, parts,
        [pltpu.VMEM((2, tokens, KVH * HD), BF),
         pltpu.SemaphoreType.DMA((2 * KVH,)),
         pltpu.SemaphoreType.DMA((2,))])


def fold8(op, value):
    return op(value.reshape(value.shape[0] // 8, 8, value.shape[1]), axis=0)


def core_kernel(tokens, doc_ref, qg_own, qg_pair, *rest):
    (kv_refs, (o_own, o_pair, dq_own, dq_pair, far_out, mid_out, near_out,
               q_s, g_s, kv_s, kvt_s, acc_s, s_s, p_s, e_s, d_s, o_s, dq_s, sems, out_sems)) = rest[:6], rest[6:]
    me = lax.axis_index("ctx")
    chip, core = lax.div(me, 2), lax.rem(me, 2)
    near_at = 4 * tokens
    mine, other = rows(core * tokens, tokens), rows((1 - core) * tokens, tokens)
    moves = []
    for ref, at in ((qg_own, mine), (qg_pair, other)):
        for side, to in enumerate((q_s, g_s)):
            moves.append((ref.at[:, cols((side * HALF + core) * QW, QW)], to.at[at, :]))
    for n in range(3):
        for m, shard in ((0, core), (1, 1 - core)):
            at = rows((4 - 2 * n + shard) * tokens, tokens)
            for side in range(2):
                moves.append((kv_refs[2 * n + m].at[:, cols((side * HALF + core) * HD, HD)],
                              kv_s.at[at, pl.ds(side * HD, HD)]))
    copies = [pltpu.make_async_copy(src, dst, sems.at[n]) for n, (src, dst) in enumerate(moves)]
    for copy in copies:
        copy.start()
    acc_s[...] = jnp.zeros_like(acc_s)
    for copy in copies:
        copy.wait()
    blocks = kv_s.shape[0] // BLK
    for at in range(blocks):
        kvt_s[:, at * BLK:(at + 1) * BLK] = kv_s[at * BLK:(at + 1) * BLK, :].T

    def attend(block, at, many, seen):
        span = many * BLK
        base = (block + MOST_BLK + 1 - many) * BLK
        window = rows(base, span)
        tok = rows(block * BLK, BLK)
        key_cols = slice(at * KV2, at * KV2 + HD)
        value_cols = slice(at * KV2 + HD, (at + 1) * KV2)
        q_here, g_here = q_s[tok, at * QW:(at + 1) * QW], g_s[tok, at * QW:(at + 1) * QW]
        qt = jnp.concatenate([q_here[:, n * HD:(n + 1) * HD].T for n in range(GROUP)], axis=1)
        gt = jnp.concatenate([g_here[:, n * HD:(n + 1) * HD].T for n in range(GROUP)], axis=1)
        part = 2 * BLK
        ts = [slice(n * part, (n + 1) * part) for n in range(GROUP * BLK // part)]
        scale_rows = []
        edge = jnp.where(seen < many, F32(-1e30), F32(0.0))
        causal = (lax.broadcasted_iota(jnp.int32, (BLK, BLK), 0)
                  <= lax.broadcasted_iota(jnp.int32, (BLK, BLK), 1))
        causal = jnp.concatenate([causal] * (part // BLK), axis=1)
        keys, values = kv_s[window, key_cols], kv_s[window, value_cols]
        here = [slice(kb * BLK, (kb + 1) * BLK) for kb in range(many)]
        tops = []
        for t in ts:
            s_all = jnp.dot(keys, qt[:, t], preferred_element_type=F32)
            most = None
            for kb in range(many):
                s = s_all[here[kb], :]
                if kb == 0:
                    s = s + edge
                if kb == many - 1:
                    s = jnp.where(causal, s, F32(-1e30))
                s_s[here[kb], t] = s
                top = fold8(jnp.max, s)
                most = top if most is None else jnp.maximum(most, top)
            tops.append(jnp.max(most, axis=0, keepdims=True) * F32(SCALE * LOG2E))
        for t in ts:
            p_s[:span, t] = jnp.dot(values, gt[:, t], preferred_element_type=F32)
        for t, top in zip(ts, tops):
            sums = None
            for kb in range(many):
                e = jnp.exp2(s_s[here[kb], t] * F32(SCALE * LOG2E) - top)
                e_s[here[kb], t] = e.astype(BF)
                total = fold8(jnp.sum, e)
                sums = total if sums is None else sums + total
            scale_rows.append(1.0 / jnp.sum(sums, axis=0, keepdims=True))
        dots = []
        for t, inv in zip(ts, scale_rows):
            ot = jnp.dot(kvt_s[value_cols, cols(base, span)], e_s[:span, t],
                         preferred_element_type=F32) * inv
            ot_low = ot.astype(BF)
            dots.append(jnp.sum(gt[:, t].astype(F32) * ot_low.astype(F32), axis=0, keepdims=True))
            for n in range(part // BLK):
                where = slice(at * QW + t.start + n * BLK, at * QW + t.start + (n + 1) * BLK)
                o_s[tok, where] = ot_low[:, n * BLK:(n + 1) * BLK].T
        for t, inv, dot in zip(ts, scale_rows, dots):
            for kb in range(many):
                d_s[here[kb], t] = e_s[here[kb], t] * (p_s[here[kb], t] - dot).astype(BF)
            dqt = jnp.dot(kvt_s[key_cols, cols(base, span)], d_s[:span, t],
                          preferred_element_type=F32) * (inv * F32(SCALE))
            dqt_low = dqt.astype(BF)
            for n in range(part // BLK):
                where = slice(at * QW + t.start + n * BLK, at * QW + t.start + (n + 1) * BLK)
                dq_s[tok, where] = dqt_low[:, n * BLK:(n + 1) * BLK].T
        inv = jnp.concatenate(scale_rows, axis=1)
        gt_low = (gt.astype(F32) * inv).astype(BF)
        qt_low = (qt.astype(F32) * (inv * F32(SCALE))).astype(BF)
        last = (((1,), (1,)), ((), ()))
        acc_s[window, value_cols] += lax.dot_general(e_s[:span, :], gt_low, last, preferred_element_type=F32)
        acc_s[window, key_cols] += lax.dot_general(d_s[:span, :], qt_low, last, preferred_element_type=F32)

    def step(block, carry):
        place = chip * (2 * tokens // BLK) + block
        doc = doc_ref[0, place]
        seen = jnp.int32(0)
        for back in range(MOST_BLK):
            there = place - back
            same = (there >= 0) & (doc_ref[0, jnp.maximum(there, 0)] == doc)
            seen += same.astype(jnp.int32)
        for many in range(2, MOST_BLK + 1, 2):
            @pl.when((seen == many) | (seen == many - 1))
            def _():
                attend(block, 0, many, seen)
        return carry

    lax.fori_loop(0, 2 * tokens // BLK, step, 0)
    far_out[...] = acc_s[BLK:2 * tokens, :].astype(BF)
    mid_out[...] = acc_s[2 * tokens:near_at, :].astype(BF)
    near_out[...] = acc_s[near_at:, :]
    leaving = [(o_s, o_own, mine), (o_s, o_pair, other), (dq_s, dq_own, mine), (dq_s, dq_pair, other)]
    copies = [pltpu.make_async_copy(src.at[at, :], dst, out_sems.at[n])
              for n, (src, dst, at) in enumerate(leaving)]
    for copy in copies:
        copy.start()
    for copy in copies:
        copy.wait()


def attend_half(docs, qg_own, qg_pair, kvs):
    tokens = qg_own.shape[0]
    all_rows = 6 * tokens
    most = MOST_BLK * BLK
    return call(
        functools.partial(core_kernel, tokens),
        "attend",
        [shape(tokens, QW)] * 4 + [
            shape(2 * tokens - BLK, KV2),
            shape(2 * tokens, KV2),
            shape(2 * tokens, KV2, F32),
        ],
        (docs, qg_own, qg_pair, *kvs),
        [
            pltpu.VMEM((2 * tokens, QW), BF),
            pltpu.VMEM((2 * tokens, QW), BF),
            pltpu.VMEM((all_rows, KV2), BF),
            pltpu.VMEM((KV2, all_rows), BF),
            pltpu.VMEM((all_rows, KV2), F32),
            pltpu.VMEM((most, QW), F32),
            pltpu.VMEM((most, QW), F32),
            pltpu.VMEM((most, QW), BF),
            pltpu.VMEM((most, QW), BF),
            pltpu.VMEM((2 * tokens, QW), BF),
            pltpu.VMEM((2 * tokens, QW), BF),
            pltpu.SemaphoreType.DMA((16,)),
            pltpu.SemaphoreType.DMA((4,)),
        ],
        [SMEM] + [ANY] * 8,
        [ANY] * 4 + [VMEM] * 3,
        ATTEND_BYTES,
        ATTEND_FLOPS)


def shards(queries, key_rows, value_rows, out_grad, doc_blocks):
    peers = lax.axis_size("ctx")
    sections = lax.axis_size("pipe")

    def move(value, chips, cross):
        pairs = []
        for i in range(peers):
            to = (i // 2 + chips) * 2 + ((i % 2) ^ cross)
            if 0 <= to < peers:
                pairs.append((i, to))
        return lax.ppermute(value, "ctx", pairs)

    def pass_on(value, by, cross):
        pairs = [(p * peers + i, (p + by) % sections * peers + (i ^ cross))
                 for p in range(sections) for i in range(peers)]
        return lax.ppermute(value, ("pipe", "ctx"), pairs)

    q, g, k, v = queries[0], out_grad[0], key_rows[0], value_rows[0]

    def with_pair(value):
        return [value, move(value, 0, 1)]

    def beside(first, second):
        width = first.shape[1] // 2
        return jnp.concatenate([first[:, :width], second[:, :width]], axis=1)

    kv_next, kv_here, qg_next = pack(k, v, q, g)
    kv_next = pass_on(kv_next, -1, 0)
    mid_here = move(kv_here, 1, 0)
    docs_next = pass_on(doc_blocks, -1, 0)
    kv_next, mid_here, docs_next, qg_next, q, g, k, v = lax.optimization_barrier(
        (kv_next, mid_here, docs_next, qg_next, q, g, k, v))
    qg_next = pass_on(qg_next, -1, 0)
    far_here = move(mid_here, 1, 0)
    mid_next = move(kv_next, 1, 0)
    far_here, mid_next = lax.optimization_barrier((far_here, mid_next))
    far_next = move(mid_next, 1, 0)
    kvs = with_pair(beside(k, v)) + with_pair(mid_here) + with_pair(far_here)
    kvs_next = with_pair(kv_next) + with_pair(mid_next) + with_pair(far_next)
    qgs = with_pair(beside(q, g))
    qgs[0], qg_next, docs_next, *kvs_next = lax.optimization_barrier((qgs[0], qg_next, docs_next, *kvs_next))
    o_own, o_pair, dq_own, dq_pair, far, mid, near = attend_half(doc_blocks, *qgs, kvs)
    back = [move(mid, -1, 0), move(far, -2, 0)]
    q_parts = [pass_on(dq_own, -1, 0), pass_on(dq_pair, -1, 1)]
    outs = [o_own, move(o_pair, 0, 1)]
    o_own, o_pair, dq_own, dq_pair, far, mid, near_next = attend_half(
        docs_next, *with_pair(qg_next), kvs_next)
    near, near_next, *q_parts = lax.optimization_barrier((near, near_next, *q_parts))
    back_next = [move(mid, -1, 0), move(far, -2, 0)]
    outs += [pass_on(o_own, 1, 0), pass_on(o_pair, 1, 1)]
    q_parts += [dq_own, move(dq_pair, 0, 1)]
    ours, theirs = add_last(near, *back)
    kv_parts = [pass_on(ours, -1, 0), pass_on(theirs, -1, 1)]
    attn_out = lay_heads(outs, False)
    ours, theirs = add_last(near_next, *back_next)
    kv_parts += [ours, move(theirs, 0, 1)]
    grad_query = lay_heads(q_parts, True)
    grad_key, grad_value = lay_kv(kv_parts)
    return attn_out[None], grad_query[None], grad_key[None], grad_value[None]


def solution(mesh):
    tokens = P("pipe", "ctx", None)
    return jax.shard_map(
        shards,
        mesh=mesh,
        in_specs=(tokens, tokens, tokens, tokens, P("pipe", None)),
        out_specs=(tokens, tokens, tokens, tokens),
        check_vma=False,
    )
```

```python
import functools
import math

import jax
import jax.numpy as jnp
from jax import lax
from jax.experimental import pallas as pl
from jax.experimental.pallas import tpu as pltpu
from jax.sharding import PartitionSpec as P

HD = 128
H = 16
KVH = 4
BLK = 128
MOST_BLK = 8

GROUP = H // KVH
HALF = KVH // 2
QW = GROUP * HD
KV2 = 2 * HD
SCALE = 1.0 / math.sqrt(HD)
LOG2E = math.log2(math.e)
SMALL_BYTES = 4 * 1024 * 1024
FIRST_BYTES = 56 * 1024 * 1024
ATTEND_BYTES = 20 * 1024 * 1024
ATTEND_FLOPS = 1000

BF = jnp.bfloat16
F32 = jnp.float32
ANY = pl.BlockSpec(memory_space=pl.ANY)
VMEM = pl.BlockSpec(memory_space=pltpu.VMEM)
SMEM = pl.BlockSpec(memory_space=pltpu.SMEM)


def shape(rows, cols, dtype=BF):
    return jax.ShapeDtypeStruct((rows, cols), dtype)


def cols(start, size):
    return pl.ds(pl.multiple_of(start, HD), size)


def rows(start, size):
    return pl.ds(pl.multiple_of(start, BLK), size)


def call(kernel, name, outs, args, scratch, in_specs=None, out_specs=None, limit=SMALL_BYTES, flops=1000):
    return pl.pallas_call(
        kernel,
        name=name,
        out_shape=outs,
        in_specs=in_specs or [ANY] * len(args),
        out_specs=out_specs or [ANY] * len(outs),
        scratch_shapes=scratch,
        compiler_params=pltpu.CompilerParams(vmem_limit_bytes=limit),
        cost_estimate=pl.CostEstimate(flops=flops, bytes_accessed=1000, transcendentals=0),
    )(*args)


def stage(moves, sems):
    copies = [pltpu.make_async_copy(src, dst, sems.at[n]) for n, (src, dst) in enumerate(moves)]
    for copy in copies:
        copy.start()
    return copies


def wait(copies):
    for copy in copies:
        copy.wait()


def pack_kernel(k_ref, v_ref, *rest):
    outs, (held, in_sems, out_sems) = rest[:2], rest[2:]
    width = k_ref.shape[1] // 2
    moves = []
    for half in range(2):
        for side, ref in enumerate((k_ref, v_ref)):
            moves.append((ref.at[:, pl.ds(half * width, width)], held.at[half, :, pl.ds(side * width, width)]))
    ins = stage(moves, in_sems)
    leaving = []
    for half, out in enumerate(outs):
        wait(ins[2 * half:2 * half + 2])
        leaving.append(pltpu.make_async_copy(held.at[half], out, out_sems.at[half]))
        leaving[-1].start()
    wait(leaving)


def pack(keys, values):
    return call(
        pack_kernel, "pack", [shape(*keys.shape)] * 2, (keys, values),
        [pltpu.VMEM((2, *keys.shape), BF), pltpu.SemaphoreType.DMA((4,)), pltpu.SemaphoreType.DMA((2,))],
        limit=FIRST_BYTES)


def add_middle_kernel(mid_ref, far_ref, out):
    trim = mid_ref.shape[0] - far_ref.shape[0]
    out[:trim, :] = mid_ref[:trim, :]
    out[trim:, :] = (mid_ref[trim:, :].astype(F32) + far_ref[...].astype(F32)).astype(BF)


def add_middle(mid, far):
    return call(add_middle_kernel, "add_middle", [shape(*mid.shape)], (mid, far), [],
                [VMEM] * 2, [VMEM])[0]


def add_last_kernel(near_ref, got_ref, straight, crossed):
    core = lax.rem(lax.axis_index("ctx"), 2)
    tokens = straight.shape[0]
    for out, shard in ((straight, core), (crossed, 1 - core)):
        at = rows(shard * tokens, tokens)
        out[...] = (near_ref[at, :] + got_ref[at, :].astype(F32)).astype(BF)


def add_last(near, got):
    tokens, width = near.shape[0] // 2, near.shape[1]
    return call(add_last_kernel, "add_last", [shape(tokens, width)] * 2, (near, got), [],
                [VMEM] * 2, [VMEM] * 2)


def lay_heads_kernel(blank_last, *refs):
    parts, (out, held, in_sems, out_sems) = refs[:-4], refs[-4:]
    core = lax.rem(lax.axis_index("ctx"), 2)
    moves = []
    for n, part in enumerate(parts):
        half = core if n % 2 == 0 else 1 - core
        moves.append((part, held.at[:, cols((n // 2 * HALF + half) * QW, QW)]))
    wait(stage(moves, in_sems))
    if blank_last:
        @pl.when(lax.axis_index("pipe") == lax.axis_size("pipe") - 1)
        def _():
            held[...] = jnp.zeros_like(held)
    wait(stage([(held, out)], out_sems))


def lay_heads(parts, blank_last):
    tokens = parts[0].shape[0]
    return call(
        functools.partial(lay_heads_kernel, blank_last), "lay_heads", [shape(tokens, H * HD)], parts,
        [pltpu.VMEM((tokens, H * HD), BF),
         pltpu.SemaphoreType.DMA((len(parts),)),
         pltpu.SemaphoreType.DMA((1,))])[0]


def lay_kv_kernel(*refs):
    parts, (key_out, value_out, held, in_sems, out_sems) = refs[:-5], refs[-5:]
    core = lax.rem(lax.axis_index("ctx"), 2)
    moves = []
    for n, part in enumerate(parts):
        half = core if n % 2 == 0 else 1 - core
        dst = cols((n // 2 * HALF + half) * HD, HD)
        for side in range(2):
            moves.append((part.at[:, pl.ds(side * HD, HD)], held.at[side, :, dst]))
    wait(stage(moves, in_sems))

    @pl.when(lax.axis_index("pipe") == lax.axis_size("pipe") - 1)
    def _():
        held[...] = jnp.zeros_like(held)

    wait(stage([(held.at[0], key_out), (held.at[1], value_out)], out_sems))


def lay_kv(parts):
    tokens = parts[0].shape[0]
    return call(
        lay_kv_kernel, "lay_kv", [shape(tokens, KVH * HD)] * 2, parts,
        [pltpu.VMEM((2, tokens, KVH * HD), BF),
         pltpu.SemaphoreType.DMA((2 * KVH,)),
         pltpu.SemaphoreType.DMA((2,))])


def fold8(op, value):
    return op(value.reshape(value.shape[0] // 8, 8, value.shape[1]), axis=0)


def core_kernel(chunk, tokens, doc_ref, *rest):
    (sources, (o_own, o_pair, dq_own, dq_pair, far_out, mid_out, near_out,
               q_s, g_s, kv_s, kvt_s, acc_s, s_s, p_s, e_s, d_s, o_s, dq_s, sems, out_sems)) = rest[:12], rest[12:]
    q_own, g_own, q_pair, g_pair, k_own, v_own, k_pair, v_pair, mid_own, mid_pair, far_own, far_pair = sources
    me = lax.axis_index("ctx")
    chip, core = lax.div(me, 2), lax.rem(me, 2)
    near_at = 4 * tokens
    first = chunk * HALF

    def part(ref, head, width):
        return ref.at[:, cols((head + core) * width, width)]

    mine, other = rows(core * tokens, tokens), rows((1 - core) * tokens, tokens)
    moves = [
        (part(q_own, 0, QW), q_s.at[mine, :]), (part(q_pair, first, QW), q_s.at[other, :]),
        (part(g_own, 0, QW), g_s.at[mine, :]), (part(g_pair, first, QW), g_s.at[other, :]),
    ]
    kv_sources = (((k_own, 0), (v_own, 0)), ((k_pair, first), (v_pair, first)),
                  ((mid_own, 0), (mid_own, HALF)), ((mid_pair, 0), (mid_pair, HALF)),
                  ((far_own, 0), (far_own, HALF)), ((far_pair, 0), (far_pair, HALF)))
    for n, both in enumerate(kv_sources):
        shard = core if n % 2 == 0 else 1 - core
        at = rows((4 - n // 2 * 2 + shard) * tokens, tokens)
        for side, (ref, head) in enumerate(both):
            moves.append((part(ref, head, HD), kv_s.at[at, pl.ds(side * HD, HD)]))
    copies = [pltpu.make_async_copy(src, dst, sems.at[n]) for n, (src, dst) in enumerate(moves)]
    for copy in copies:
        copy.start()
    acc_s[...] = jnp.zeros_like(acc_s)
    for copy in copies:
        copy.wait()
    blocks = kv_s.shape[0] // BLK
    for at in range(blocks):
        kvt_s[:, at * BLK:(at + 1) * BLK] = kv_s[at * BLK:(at + 1) * BLK, :].T

    def attend(block, at, many, seen):
        span = many * BLK
        base = (block + MOST_BLK + 1 - many) * BLK
        window = rows(base, span)
        tok = rows(block * BLK, BLK)
        key_cols = slice(at * KV2, at * KV2 + HD)
        value_cols = slice(at * KV2 + HD, (at + 1) * KV2)
        q_here, g_here = q_s[tok, at * QW:(at + 1) * QW], g_s[tok, at * QW:(at + 1) * QW]
        qt = jnp.concatenate([q_here[:, n * HD:(n + 1) * HD].T for n in range(GROUP)], axis=1)
        gt = jnp.concatenate([g_here[:, n * HD:(n + 1) * HD].T for n in range(GROUP)], axis=1)
        part = 2 * BLK
        ts = [slice(n * part, (n + 1) * part) for n in range(GROUP * BLK // part)]
        edge = jnp.where(seen < many, F32(-1e30), F32(0.0))
        causal = (lax.broadcasted_iota(jnp.int32, (BLK, BLK), 0)
                  <= lax.broadcasted_iota(jnp.int32, (BLK, BLK), 1))
        causal = jnp.concatenate([causal] * (part // BLK), axis=1)
        keys, values = kv_s[window, key_cols], kv_s[window, value_cols]
        here = [slice(kb * BLK, (kb + 1) * BLK) for kb in range(many)]

        def scores(t):
            s_all = jnp.dot(keys, qt[:, t], preferred_element_type=F32)
            most = None
            for kb in range(many):
                s = s_all[here[kb], :]
                if kb == 0:
                    s = s + edge
                if kb == many - 1:
                    s = jnp.where(causal, s, F32(-1e30))
                s_s[here[kb], t] = s
                top = fold8(jnp.max, s)
                most = top if most is None else jnp.maximum(most, top)
            return jnp.max(most, axis=0, keepdims=True) * F32(SCALE * LOG2E)

        def weights(t, top):
            sums = None
            for kb in range(many):
                e = jnp.exp2(s_s[here[kb], t] * F32(SCALE * LOG2E) - top)
                e_s[here[kb], t] = e.astype(BF)
                total = fold8(jnp.sum, e)
                sums = total if sums is None else sums + total
            return 1.0 / jnp.sum(sums, axis=0, keepdims=True)

        def prob_grads(t):
            p_s[:span, t] = jnp.dot(values, gt[:, t], preferred_element_type=F32)

        def turned(to, t, value):
            low = value.astype(BF)
            for n in range(part // BLK):
                to[tok, t.start + n * BLK:t.start + (n + 1) * BLK] = low[:, n * BLK:(n + 1) * BLK].T
            return low

        def outputs(t, inv):
            ot = jnp.dot(kvt_s[value_cols, cols(base, span)], e_s[:span, t], preferred_element_type=F32) * inv
            ot_low = turned(o_s, t, ot)
            return jnp.sum(gt[:, t].astype(F32) * ot_low.astype(F32), axis=0, keepdims=True)

        def score_grads(t, dots):
            for kb in range(many):
                d_s[here[kb], t] = e_s[here[kb], t] * (p_s[here[kb], t] - dots).astype(BF)

        def query_grads(t, inv):
            turned(dq_s, t, jnp.dot(kvt_s[key_cols, cols(base, span)], d_s[:span, t],
                                    preferred_element_type=F32) * (inv * F32(SCALE)))

        t0, t1 = ts
        top0 = scores(t0)
        top1 = scores(t1)
        inv0 = weights(t0, top0)
        prob_grads(t0)
        dots0 = outputs(t0, inv0)
        inv1 = weights(t1, top1)
        prob_grads(t1)
        score_grads(t0, dots0)
        dots1 = outputs(t1, inv1)
        query_grads(t0, inv0)
        score_grads(t1, dots1)
        query_grads(t1, inv1)
        scale_rows = [inv0, inv1]
        inv = jnp.concatenate(scale_rows, axis=1)
        gt_low = (gt.astype(F32) * inv).astype(BF)
        qt_low = (qt.astype(F32) * (inv * F32(SCALE))).astype(BF)
        last = (((1,), (1,)), ((), ()))
        acc_s[window, value_cols] += lax.dot_general(e_s[:span, :], gt_low, last, preferred_element_type=F32)
        acc_s[window, key_cols] += lax.dot_general(d_s[:span, :], qt_low, last, preferred_element_type=F32)

    def step(block, carry):
        place = chip * (2 * tokens // BLK) + block
        doc = doc_ref[0, place]
        seen = jnp.int32(0)
        for back in range(MOST_BLK):
            there = place - back
            same = (there >= 0) & (doc_ref[0, jnp.maximum(there, 0)] == doc)
            seen += same.astype(jnp.int32)
        for many in range(2, MOST_BLK + 1, 2):
            @pl.when((seen == many) | (seen == many - 1))
            def _():
                attend(block, 0, many, seen)
        return carry

    lax.fori_loop(0, 2 * tokens // BLK, step, 0)
    far_out[...] = acc_s[BLK:2 * tokens, :].astype(BF)
    mid_out[...] = acc_s[2 * tokens:near_at, :].astype(BF)
    near_out[...] = acc_s[near_at:, :]
    leaving = [(o_s, o_own, mine), (o_s, o_pair, other), (dq_s, dq_own, mine), (dq_s, dq_pair, other)]
    copies = [pltpu.make_async_copy(src.at[at, :], dst, out_sems.at[n])
              for n, (src, dst, at) in enumerate(leaving)]
    for copy in copies:
        copy.start()
    for copy in copies:
        copy.wait()


def attend_half(chunk, docs, sources):
    tokens = sources[0].shape[0]
    all_rows = 6 * tokens
    most = MOST_BLK * BLK
    return call(
        functools.partial(core_kernel, chunk, tokens),
        "attend",
        [shape(tokens, QW)] * 4 + [
            shape(2 * tokens - BLK, KV2),
            shape(2 * tokens, KV2),
            shape(2 * tokens, KV2, F32),
        ],
        (docs, *sources),
        [
            pltpu.VMEM((2 * tokens, QW), BF),
            pltpu.VMEM((2 * tokens, QW), BF),
            pltpu.VMEM((all_rows, KV2), BF),
            pltpu.VMEM((KV2, all_rows), BF),
            pltpu.VMEM((all_rows, KV2), F32),
            pltpu.VMEM((most, QW), F32),
            pltpu.VMEM((most, QW), F32),
            pltpu.VMEM((most, QW), BF),
            pltpu.VMEM((most, QW), BF),
            pltpu.VMEM((2 * tokens, QW), BF),
            pltpu.VMEM((2 * tokens, QW), BF),
            pltpu.SemaphoreType.DMA((16,)),
            pltpu.SemaphoreType.DMA((4,)),
        ],
        [SMEM] + [ANY] * 12,
        [ANY] * 4 + [VMEM] * 3,
        ATTEND_BYTES,
        ATTEND_FLOPS)


def shards(queries, key_rows, value_rows, out_grad, doc_blocks):
    peers = lax.axis_size("ctx")
    sections = lax.axis_size("pipe")

    def move(value, chips, cross):
        pairs = [(i, (i // 2 + chips) % (peers // 2) * 2 + ((i % 2) ^ cross)) for i in range(peers)]
        return lax.ppermute(value, "ctx", pairs)

    def pass_back(value, cross):
        pairs = [(p * peers + i, (p - 1) % sections * peers + (i ^ cross))
                 for p in range(sections) for i in range(peers)]
        return lax.ppermute(value, ("pipe", "ctx"), pairs)

    q, g, k, v = queries[0], out_grad[0], key_rows[0], value_rows[0]

    def with_pair(value):
        return [value, move(value, 0, 1)]

    def half_of(value, half):
        width = value.shape[1] // 2
        return value[:, half * width:(half + 1) * width]

    near = pack(k, v)
    mid = [move(kv, 1, 0) for kv in near]
    pairs = [move(value, 0, 1) for value in (q, g, k, v)]
    own = [half_of(value, half) for half in range(2) for value in (q, g, k, v)]
    mid[0], *own = lax.optimization_barrier((mid[0], *own))
    far = [move(kv, 1, 0) for kv in mid]

    def attend(chunk):
        here = own[4 * chunk:4 * chunk + 4]
        return attend_half(chunk, doc_blocks, [
            *here[:2], *pairs[:2], *here[2:], *pairs[2:], *with_pair(mid[chunk]), *with_pair(far[chunk])])

    mid[1], far[0] = lax.optimization_barrier((mid[1], far[0]))
    o_own, o_pair, dq_own, dq_pair, far_part, mid_part, near_part = attend(0)
    mid_before, far_got = mid_part, move(far_part, -1, 0)
    q_parts = [pass_back(dq_own, 0), pass_back(dq_pair, 1)]
    outs = [o_own, move(o_pair, 0, 1)]
    far[1], near_part = lax.optimization_barrier((far[1], near_part))
    o_own, o_pair, dq_own, dq_pair, far_part, mid_part, near_last = attend(1)
    mid_before, near_last, mid_part, *q_parts = lax.optimization_barrier(
        (mid_before, near_last, mid_part, *q_parts))
    far_part, far_got = lax.optimization_barrier((far_part, far_got))
    back = move(add_middle(mid_before, far_got), -1, 0)
    back_last = move(add_middle(mid_part, move(far_part, -1, 0)), -1, 0)
    q_parts += [pass_back(dq_own, 0), pass_back(dq_pair, 1)]
    outs += [o_own, move(o_pair, 0, 1)]
    ours, theirs = add_last(near_part, back)
    kv_parts = [pass_back(ours, 0), pass_back(theirs, 1)]
    near_last, *q_parts = lax.optimization_barrier((near_last, *q_parts))
    ours, theirs = add_last(near_last, back_last)
    kv_parts += [pass_back(ours, 0), pass_back(theirs, 1)]
    attn_out = lay_heads(outs, False)
    grad_query = lay_heads(q_parts, True)
    grad_key, grad_value = lay_kv(kv_parts)
    return attn_out[None], grad_query[None], grad_key[None], grad_value[None]


def solution(mesh):
    tokens = P("pipe", "ctx", None)
    return jax.shard_map(
        shards,
        mesh=mesh,
        in_specs=(tokens, tokens, tokens, tokens, P("pipe", None)),
        out_specs=(tokens, tokens, tokens, tokens),
        check_vma=False,
    )
```

```python
import functools
import math

import jax
import jax.numpy as jnp
from jax import lax
from jax.experimental import pallas as pl
from jax.experimental.pallas import tpu as pltpu
from jax.sharding import PartitionSpec as P

HD = 128
H = 16
KVH = 4
BLK = 128
MOST_BLK = 8

GROUP = H // KVH
HALF = KVH // 2
QW = GROUP * HD
KV2 = 2 * HD
SCALE = 1.0 / math.sqrt(HD)
LOG2E = math.log2(math.e)
SMALL_BYTES = 4 * 1024 * 1024
FIRST_BYTES = 56 * 1024 * 1024
ATTEND_BYTES = 20 * 1024 * 1024
ATTEND_FLOPS = 1000

BF = jnp.bfloat16
F32 = jnp.float32
ANY = pl.BlockSpec(memory_space=pl.ANY)
VMEM = pl.BlockSpec(memory_space=pltpu.VMEM)
SMEM = pl.BlockSpec(memory_space=pltpu.SMEM)


def shape(rows, cols, dtype=BF):
    return jax.ShapeDtypeStruct((rows, cols), dtype)


def cols(start, size):
    return pl.ds(pl.multiple_of(start, HD), size)


def rows(start, size):
    return pl.ds(pl.multiple_of(start, BLK), size)


def call(kernel, name, outs, args, scratch, in_specs=None, out_specs=None, limit=SMALL_BYTES, flops=1000):
    return pl.pallas_call(
        kernel,
        name=name,
        out_shape=outs,
        in_specs=in_specs or [ANY] * len(args),
        out_specs=out_specs or [ANY] * len(outs),
        scratch_shapes=scratch,
        compiler_params=pltpu.CompilerParams(vmem_limit_bytes=limit),
        cost_estimate=pl.CostEstimate(flops=flops, bytes_accessed=1000, transcendentals=0),
    )(*args)


def stage(moves, sems):
    copies = [pltpu.make_async_copy(src, dst, sems.at[n]) for n, (src, dst) in enumerate(moves)]
    for copy in copies:
        copy.start()
    return copies


def wait(copies):
    for copy in copies:
        copy.wait()


def pack_kernel(k_ref, v_ref, *rest):
    outs, (held, in_sems, out_sems) = rest[:2], rest[2:]
    width = k_ref.shape[1] // 2
    moves = []
    for half in range(2):
        for side, ref in enumerate((k_ref, v_ref)):
            moves.append((ref.at[:, pl.ds(half * width, width)], held.at[half, :, pl.ds(side * width, width)]))
    ins = stage(moves, in_sems)
    leaving = []
    for half, out in enumerate(outs):
        wait(ins[2 * half:2 * half + 2])
        leaving.append(pltpu.make_async_copy(held.at[half], out, out_sems.at[half]))
        leaving[-1].start()
    wait(leaving)


def pack(keys, values):
    return call(
        pack_kernel, "pack", [shape(*keys.shape)] * 2, (keys, values),
        [pltpu.VMEM((2, *keys.shape), BF), pltpu.SemaphoreType.DMA((4,)), pltpu.SemaphoreType.DMA((2,))],
        limit=FIRST_BYTES)


def add_middle_kernel(mid_ref, far_ref, out):
    trim = mid_ref.shape[0] - far_ref.shape[0]
    out[:trim, :] = mid_ref[:trim, :]
    out[trim:, :] = (mid_ref[trim:, :].astype(F32) + far_ref[...].astype(F32)).astype(BF)


def add_middle(mid, far):
    return call(add_middle_kernel, "add_middle", [shape(*mid.shape)], (mid, far), [],
                [VMEM] * 2, [VMEM])[0]


def add_last_kernel(near_ref, got_ref, straight, crossed):
    core = lax.rem(lax.axis_index("ctx"), 2)
    tokens = straight.shape[0]
    for out, shard in ((straight, core), (crossed, 1 - core)):
        at = rows(shard * tokens, tokens)
        out[...] = (near_ref[at, :] + got_ref[at, :].astype(F32)).astype(BF)


def add_last(near, got):
    tokens, width = near.shape[0] // 2, near.shape[1]
    return call(add_last_kernel, "add_last", [shape(tokens, width)] * 2, (near, got), [],
                [VMEM] * 2, [VMEM] * 2)


def lay_heads_kernel(blank_last, *refs):
    parts, (out, held, in_sems, out_sems) = refs[:-4], refs[-4:]
    core = lax.rem(lax.axis_index("ctx"), 2)
    moves = []
    for n, part in enumerate(parts):
        half = core if n % 2 == 0 else 1 - core
        moves.append((part, held.at[:, cols((n // 2 * HALF + half) * QW, QW)]))
    wait(stage(moves, in_sems))
    if blank_last:
        @pl.when(lax.axis_index("pipe") == lax.axis_size("pipe") - 1)
        def _():
            held[...] = jnp.zeros_like(held)
    wait(stage([(held, out)], out_sems))


def lay_heads(parts, blank_last):
    tokens = parts[0].shape[0]
    return call(
        functools.partial(lay_heads_kernel, blank_last), "lay_heads", [shape(tokens, H * HD)], parts,
        [pltpu.VMEM((tokens, H * HD), BF),
         pltpu.SemaphoreType.DMA((len(parts),)),
         pltpu.SemaphoreType.DMA((1,))])[0]


def lay_kv_kernel(*refs):
    parts, (key_out, value_out, held, in_sems, out_sems) = refs[:-5], refs[-5:]
    core = lax.rem(lax.axis_index("ctx"), 2)
    moves = []
    for n, part in enumerate(parts):
        half = core if n % 2 == 0 else 1 - core
        dst = cols((n // 2 * HALF + half) * HD, HD)
        for side in range(2):
            moves.append((part.at[:, pl.ds(side * HD, HD)], held.at[side, :, dst]))
    wait(stage(moves, in_sems))

    @pl.when(lax.axis_index("pipe") == lax.axis_size("pipe") - 1)
    def _():
        held[...] = jnp.zeros_like(held)

    wait(stage([(held.at[0], key_out), (held.at[1], value_out)], out_sems))


def lay_kv(parts):
    tokens = parts[0].shape[0]
    return call(
        lay_kv_kernel, "lay_kv", [shape(tokens, KVH * HD)] * 2, parts,
        [pltpu.VMEM((2, tokens, KVH * HD), BF),
         pltpu.SemaphoreType.DMA((2 * KVH,)),
         pltpu.SemaphoreType.DMA((2,))])


def fold8(op, value):
    return op(value.reshape(value.shape[0] // 8, 8, value.shape[1]), axis=0)


def core_kernel(chunk, tokens, doc_ref, *rest):
    (sources, (o_own, o_pair, dq_own, dq_pair, far_out, mid_out, near_out,
               q_s, g_s, kv_s, kvt_s, acc_s, s_s, p_s, e_s, d_s, o_s, dq_s, sems, out_sems)) = rest[:12], rest[12:]
    q_own, g_own, q_pair, g_pair, k_own, v_own, k_pair, v_pair, mid_own, mid_pair, far_own, far_pair = sources
    me = lax.axis_index("ctx")
    chip, core = lax.div(me, 2), lax.rem(me, 2)
    near_at = 4 * tokens
    first = chunk * HALF

    def part(ref, head, width):
        return ref.at[:, cols((head + core) * width, width)]

    mine, other = rows(core * tokens, tokens), rows((1 - core) * tokens, tokens)
    moves = []
    kv_sources = (((k_own, 0), (v_own, 0)), ((k_pair, first), (v_pair, first)),
                  ((mid_own, 0), (mid_own, HALF)), ((mid_pair, 0), (mid_pair, HALF)),
                  ((far_own, 0), (far_own, HALF)), ((far_pair, 0), (far_pair, HALF)))
    for n, both in enumerate(kv_sources):
        shard = core if n % 2 == 0 else 1 - core
        at = rows((4 - n // 2 * 2 + shard) * tokens, tokens)
        for side, (ref, head) in enumerate(both):
            moves.append((part(ref, head, HD), kv_s.at[at, pl.ds(side * HD, HD)]))
    kv_moves = len(moves)
    moves += [
        (part(q_own, 0, QW), q_s.at[mine, :]), (part(q_pair, first, QW), q_s.at[other, :]),
        (part(g_own, 0, QW), g_s.at[mine, :]), (part(g_pair, first, QW), g_s.at[other, :]),
    ]
    copies = stage(moves, sems)
    acc_s[...] = jnp.zeros_like(acc_s)
    wait(copies[:kv_moves])
    blocks = kv_s.shape[0] // BLK
    for at in range(1, blocks):
        kvt_s[:, at * BLK:(at + 1) * BLK] = kv_s[at * BLK:(at + 1) * BLK, :].T
    wait(copies[kv_moves:])

    def attend(block, at, many, seen):
        span = many * BLK
        base = (block + MOST_BLK + 1 - many) * BLK
        window = rows(base, span)
        tok = rows(block * BLK, BLK)
        key_cols = slice(at * KV2, at * KV2 + HD)
        value_cols = slice(at * KV2 + HD, (at + 1) * KV2)
        q_here, g_here = q_s[tok, at * QW:(at + 1) * QW], g_s[tok, at * QW:(at + 1) * QW]
        qt = jnp.concatenate([q_here[:, n * HD:(n + 1) * HD].T for n in range(GROUP)], axis=1)
        gt = jnp.concatenate([g_here[:, n * HD:(n + 1) * HD].T for n in range(GROUP)], axis=1)
        part = 2 * BLK
        ts = [slice(n * part, (n + 1) * part) for n in range(GROUP * BLK // part)]
        edge = jnp.where(seen < many, F32(-1e30), F32(0.0))
        causal = (lax.broadcasted_iota(jnp.int32, (BLK, BLK), 0)
                  <= lax.broadcasted_iota(jnp.int32, (BLK, BLK), 1))
        causal = jnp.concatenate([causal] * (part // BLK), axis=1)
        keys, values = kv_s[window, key_cols], kv_s[window, value_cols]
        here = [slice(kb * BLK, (kb + 1) * BLK) for kb in range(many)]

        def scores(t):
            s_all = jnp.dot(keys, qt[:, t], preferred_element_type=F32)
            most = None
            for kb in range(many):
                s = s_all[here[kb], :]
                if kb == 0:
                    s = s + edge
                if kb == many - 1:
                    s = jnp.where(causal, s, F32(-1e30))
                s_s[here[kb], t] = s
                top = fold8(jnp.max, s)
                most = top if most is None else jnp.maximum(most, top)
            return jnp.max(most, axis=0, keepdims=True) * F32(SCALE * LOG2E)

        def weights(t, top):
            sums = None
            for kb in range(many):
                e = jnp.exp2(s_s[here[kb], t] * F32(SCALE * LOG2E) - top)
                e_s[here[kb], t] = e.astype(BF)
                total = fold8(jnp.sum, e)
                sums = total if sums is None else sums + total
            return 1.0 / jnp.sum(sums, axis=0, keepdims=True)

        def prob_grads(t):
            p_s[:span, t] = jnp.dot(values, gt[:, t], preferred_element_type=F32)

        def turned(to, t, value):
            low = value.astype(BF)
            for n in range(part // BLK):
                to[tok, t.start + n * BLK:t.start + (n + 1) * BLK] = low[:, n * BLK:(n + 1) * BLK].T
            return low

        def outputs(t, inv):
            ot = jnp.dot(kvt_s[value_cols, cols(base, span)], e_s[:span, t], preferred_element_type=F32) * inv
            ot_low = turned(o_s, t, ot)
            return jnp.sum(gt[:, t].astype(F32) * ot_low.astype(F32), axis=0, keepdims=True)

        def score_grads(t, dots):
            for kb in range(many):
                d_s[here[kb], t] = e_s[here[kb], t] * (p_s[here[kb], t] - dots).astype(BF)

        def query_grads(t, inv):
            turned(dq_s, t, jnp.dot(kvt_s[key_cols, cols(base, span)], d_s[:span, t],
                                    preferred_element_type=F32) * (inv * F32(SCALE)))

        t0, t1 = ts
        top0 = scores(t0)
        top1 = scores(t1)
        inv0 = weights(t0, top0)
        prob_grads(t0)
        dots0 = outputs(t0, inv0)
        inv1 = weights(t1, top1)
        prob_grads(t1)
        score_grads(t0, dots0)
        dots1 = outputs(t1, inv1)
        query_grads(t0, inv0)
        score_grads(t1, dots1)
        query_grads(t1, inv1)
        scale_rows = [inv0, inv1]
        inv = jnp.concatenate(scale_rows, axis=1)
        gt_low = (gt.astype(F32) * inv).astype(BF)
        qt_low = (qt.astype(F32) * (inv * F32(SCALE))).astype(BF)
        last = (((1,), (1,)), ((), ()))
        acc_s[window, value_cols] += lax.dot_general(e_s[:span, :], gt_low, last, preferred_element_type=F32)
        acc_s[window, key_cols] += lax.dot_general(d_s[:span, :], qt_low, last, preferred_element_type=F32)

    def step(block, carry):
        place = chip * (2 * tokens // BLK) + block
        doc = doc_ref[0, place]
        seen = jnp.int32(0)
        for back in range(MOST_BLK):
            there = place - back
            same = (there >= 0) & (doc_ref[0, jnp.maximum(there, 0)] == doc)
            seen += same.astype(jnp.int32)
        for many in range(2, MOST_BLK + 1, 2):
            @pl.when((seen == many) | (seen == many - 1))
            def _():
                attend(block, 0, many, seen)
        return carry

    lax.fori_loop(0, 2 * tokens // BLK, step, 0)
    copies = stage([
        (acc_s.at[pl.ds(near_at, 2 * tokens), :], near_out),
        (o_s.at[mine, :], o_own), (o_s.at[other, :], o_pair),
        (dq_s.at[mine, :], dq_own), (dq_s.at[other, :], dq_pair)], sems)
    kv_s[BLK:near_at, :] = acc_s[BLK:near_at, :].astype(BF)
    copies += stage([
        (kv_s.at[pl.ds(BLK, 2 * tokens - BLK), :], far_out),
        (kv_s.at[pl.ds(2 * tokens, 2 * tokens), :], mid_out)], out_sems)
    wait(copies)


def attend_half(chunk, docs, sources):
    tokens = sources[0].shape[0]
    all_rows = 6 * tokens
    most = MOST_BLK * BLK
    return call(
        functools.partial(core_kernel, chunk, tokens),
        "attend",
        [shape(tokens, QW)] * 4 + [
            shape(2 * tokens - BLK, KV2),
            shape(2 * tokens, KV2),
            shape(2 * tokens, KV2, F32),
        ],
        (docs, *sources),
        [
            pltpu.VMEM((2 * tokens, QW), BF),
            pltpu.VMEM((2 * tokens, QW), BF),
            pltpu.VMEM((all_rows, KV2), BF),
            pltpu.VMEM((KV2, all_rows), BF),
            pltpu.VMEM((all_rows, KV2), F32),
            pltpu.VMEM((most, QW), F32),
            pltpu.VMEM((most, QW), F32),
            pltpu.VMEM((most, QW), BF),
            pltpu.VMEM((most, QW), BF),
            pltpu.VMEM((2 * tokens, QW), BF),
            pltpu.VMEM((2 * tokens, QW), BF),
            pltpu.SemaphoreType.DMA((16,)),
            pltpu.SemaphoreType.DMA((2,)),
        ],
        [SMEM] + [ANY] * 12,
        [ANY] * 7,
        ATTEND_BYTES,
        ATTEND_FLOPS)


def shards(queries, key_rows, value_rows, out_grad, doc_blocks):
    peers = lax.axis_size("ctx")
    sections = lax.axis_size("pipe")

    def move(value, chips, cross):
        pairs = [(i, (i // 2 + chips) % (peers // 2) * 2 + ((i % 2) ^ cross)) for i in range(peers)]
        return lax.ppermute(value, "ctx", pairs)

    def pass_back(value, cross):
        pairs = [(p * peers + i, (p - 1) % sections * peers + (i ^ cross))
                 for p in range(sections) for i in range(peers)]
        return lax.ppermute(value, ("pipe", "ctx"), pairs)

    q, g, k, v = queries[0], out_grad[0], key_rows[0], value_rows[0]

    def with_pair(value):
        return [value, move(value, 0, 1)]

    def half_of(value, half):
        width = value.shape[1] // 2
        return value[:, half * width:(half + 1) * width]

    near = pack(k, v)
    mid = [move(kv, 1, 0) for kv in near]
    pairs = [move(value, 0, 1) for value in (q, g, k, v)]
    own = [half_of(value, half) for half in range(2) for value in (q, g, k, v)]
    mid[0], *own = lax.optimization_barrier((mid[0], *own))
    far = [move(kv, 1, 0) for kv in mid]

    def attend(chunk):
        here = own[4 * chunk:4 * chunk + 4]
        return attend_half(chunk, doc_blocks, [
            *here[:2], *pairs[:2], *here[2:], *pairs[2:], *with_pair(mid[chunk]), *with_pair(far[chunk])])

    mid[1], far[0] = lax.optimization_barrier((mid[1], far[0]))
    o_own, o_pair, dq_own, dq_pair, far_part, mid_part, near_part = attend(0)
    mid_before, far_got = mid_part, move(far_part, -1, 0)
    q_parts = [pass_back(dq_own, 0), pass_back(dq_pair, 1)]
    outs = [o_own, move(o_pair, 0, 1)]
    far[1], near_part = lax.optimization_barrier((far[1], near_part))
    o_own, o_pair, dq_own, dq_pair, far_part, mid_part, near_last = attend(1)
    mid_before, near_last, mid_part, *q_parts = lax.optimization_barrier(
        (mid_before, near_last, mid_part, *q_parts))
    far_part, far_got = lax.optimization_barrier((far_part, far_got))
    back = move(add_middle(mid_before, far_got), -1, 0)
    back_last = move(add_middle(mid_part, move(far_part, -1, 0)), -1, 0)
    q_parts += [pass_back(dq_own, 0), pass_back(dq_pair, 1)]
    outs += [o_own, move(o_pair, 0, 1)]
    ours, theirs = add_last(near_part, back)
    kv_parts = [pass_back(ours, 0), pass_back(theirs, 1)]
    near_last, kv_parts[0], *q_parts = lax.optimization_barrier((near_last, kv_parts[0], *q_parts))
    ours, theirs = add_last(near_last, back_last)
    kv_parts += [pass_back(ours, 0), pass_back(theirs, 1)]
    attn_out = lay_heads(outs, False)
    grad_query = lay_heads(q_parts, True)
    grad_key, grad_value = lay_kv(kv_parts)
    return attn_out[None], grad_query[None], grad_key[None], grad_value[None]


def solution(mesh):
    tokens = P("pipe", "ctx", None)
    return jax.shard_map(
        shards,
        mesh=mesh,
        in_specs=(tokens, tokens, tokens, tokens, P("pipe", None)),
        out_specs=(tokens, tokens, tokens, tokens),
        check_vma=False,
    )
```

```python
import functools
import math

import jax
import jax.numpy as jnp
from jax import lax
from jax.experimental import pallas as pl
from jax.experimental.pallas import tpu as pltpu
from jax.sharding import PartitionSpec as P

HD = 128
H = 16
KVH = 4
BLK = 128
MOST_BLK = 8

GROUP = H // KVH
HALF = KVH // 2
QW = GROUP * HD
KV2 = 2 * HD
SCALE = 1.0 / math.sqrt(HD)
LOG2E = math.log2(math.e)
SMALL_BYTES = 4 * 1024 * 1024
FIRST_BYTES = 56 * 1024 * 1024
ATTEND_BYTES = 20 * 1024 * 1024
ATTEND_FLOPS = 1000

BF = jnp.bfloat16
F32 = jnp.float32
ANY = pl.BlockSpec(memory_space=pl.ANY)
VMEM = pl.BlockSpec(memory_space=pltpu.VMEM)
SMEM = pl.BlockSpec(memory_space=pltpu.SMEM)


def shape(rows, cols, dtype=BF):
    return jax.ShapeDtypeStruct((rows, cols), dtype)


def cols(start, size):
    return pl.ds(pl.multiple_of(start, HD), size)


def rows(start, size):
    return pl.ds(pl.multiple_of(start, BLK), size)


def call(kernel, name, outs, args, scratch, in_specs=None, out_specs=None, limit=SMALL_BYTES, flops=1000):
    return pl.pallas_call(
        kernel,
        name=name,
        out_shape=outs,
        in_specs=in_specs or [ANY] * len(args),
        out_specs=out_specs or [ANY] * len(outs),
        scratch_shapes=scratch,
        compiler_params=pltpu.CompilerParams(vmem_limit_bytes=limit),
        cost_estimate=pl.CostEstimate(flops=flops, bytes_accessed=1000, transcendentals=0),
    )(*args)


def stage(moves, sems):
    copies = [pltpu.make_async_copy(src, dst, sems.at[n]) for n, (src, dst) in enumerate(moves)]
    for copy in copies:
        copy.start()
    return copies


def wait(copies):
    for copy in copies:
        copy.wait()


def pack_kernel(k_ref, v_ref, *rest):
    outs, (held, in_sems, out_sems) = rest[:2], rest[2:]
    width = k_ref.shape[1] // 2
    moves = []
    for half in range(2):
        for side, ref in enumerate((k_ref, v_ref)):
            moves.append((ref.at[:, pl.ds(half * width, width)], held.at[half, :, pl.ds(side * width, width)]))
    ins = stage(moves, in_sems)
    leaving = []
    for half, out in enumerate(outs):
        wait(ins[2 * half:2 * half + 2])
        leaving.append(pltpu.make_async_copy(held.at[half], out, out_sems.at[half]))
        leaving[-1].start()
    wait(leaving)


def pack(keys, values):
    return call(
        pack_kernel, "pack", [shape(*keys.shape)] * 2, (keys, values),
        [pltpu.VMEM((2, *keys.shape), BF), pltpu.SemaphoreType.DMA((4,)), pltpu.SemaphoreType.DMA((2,))],
        limit=FIRST_BYTES)


def add_middle_kernel(mid_ref, far_ref, out):
    trim = mid_ref.shape[0] - far_ref.shape[0]
    out[:trim, :] = mid_ref[:trim, :]
    out[trim:, :] = (mid_ref[trim:, :].astype(F32) + far_ref[...].astype(F32)).astype(BF)


def add_middle(mid, far):
    return call(add_middle_kernel, "add_middle", [shape(*mid.shape)], (mid, far), [],
                [VMEM] * 2, [VMEM])[0]


def add_last_kernel(near_ref, got_ref, straight, crossed):
    core = lax.rem(lax.axis_index("ctx"), 2)
    tokens = straight.shape[0]
    for out, shard in ((straight, core), (crossed, 1 - core)):
        at = rows(shard * tokens, tokens)
        out[...] = (near_ref[at, :] + got_ref[at, :].astype(F32)).astype(BF)


def add_last(near, got):
    tokens, width = near.shape[0] // 2, near.shape[1]
    return call(add_last_kernel, "add_last", [shape(tokens, width)] * 2, (near, got), [],
                [VMEM] * 2, [VMEM] * 2)


def lay_heads_kernel(blank_last, *refs):
    parts, (out, held, in_sems, out_sems) = refs[:-4], refs[-4:]
    core = lax.rem(lax.axis_index("ctx"), 2)
    moves = []
    for n, part in enumerate(parts):
        half = core if n % 2 == 0 else 1 - core
        moves.append((part, held.at[:, cols((n // 2 * HALF + half) * QW, QW)]))
    wait(stage(moves, in_sems))
    if blank_last:
        @pl.when(lax.axis_index("pipe") == lax.axis_size("pipe") - 1)
        def _():
            held[...] = jnp.zeros_like(held)
    wait(stage([(held, out)], out_sems))


def lay_heads(parts, blank_last):
    tokens = parts[0].shape[0]
    return call(
        functools.partial(lay_heads_kernel, blank_last), "lay_heads", [shape(tokens, H * HD)], parts,
        [pltpu.VMEM((tokens, H * HD), BF),
         pltpu.SemaphoreType.DMA((len(parts),)),
         pltpu.SemaphoreType.DMA((1,))])[0]


def lay_kv_kernel(*refs):
    parts, (key_out, value_out, held, in_sems, out_sems) = refs[:-5], refs[-5:]
    core = lax.rem(lax.axis_index("ctx"), 2)
    moves = []
    for n, part in enumerate(parts):
        half = core if n % 2 == 0 else 1 - core
        dst = cols((n // 2 * HALF + half) * HD, HD)
        for side in range(2):
            moves.append((part.at[:, pl.ds(side * HD, HD)], held.at[side, :, dst]))
    wait(stage(moves, in_sems))

    @pl.when(lax.axis_index("pipe") == lax.axis_size("pipe") - 1)
    def _():
        held[...] = jnp.zeros_like(held)

    wait(stage([(held.at[0], key_out), (held.at[1], value_out)], out_sems))


def lay_kv(parts):
    tokens = parts[0].shape[0]
    return call(
        lay_kv_kernel, "lay_kv", [shape(tokens, KVH * HD)] * 2, parts,
        [pltpu.VMEM((2, tokens, KVH * HD), BF),
         pltpu.SemaphoreType.DMA((2 * KVH,)),
         pltpu.SemaphoreType.DMA((2,))])


def fold8(op, value):
    return op(value.reshape(value.shape[0] // 8, 8, value.shape[1]), axis=0)


def core_kernel(chunk, tokens, doc_ref, *rest):
    (sources, (o_own, o_pair, dq_own, dq_pair, far_out, mid_out, near_out,
               q_s, g_s, kv_s, kvt_s, acc_s, s_s, p_s, e_s, d_s, o_s, dq_s, sems, out_sems)) = rest[:12], rest[12:]
    q_own, g_own, q_pair, g_pair, k_own, v_own, k_pair, v_pair, mid_own, mid_pair, far_own, far_pair = sources
    me = lax.axis_index("ctx")
    chip, core = lax.div(me, 2), lax.rem(me, 2)
    near_at = 4 * tokens
    first = chunk * HALF

    def part(ref, head, width):
        return ref.at[:, cols((head + core) * width, width)]

    mine, other = rows(core * tokens, tokens), rows((1 - core) * tokens, tokens)
    moves = [
        (part(q_own, 0, QW), q_s.at[mine, :]), (part(q_pair, first, QW), q_s.at[other, :]),
        (part(g_own, 0, QW), g_s.at[mine, :]), (part(g_pair, first, QW), g_s.at[other, :]),
    ]
    kv_sources = (((k_own, 0), (v_own, 0)), ((k_pair, first), (v_pair, first)),
                  ((mid_own, 0), (mid_own, HALF)), ((mid_pair, 0), (mid_pair, HALF)),
                  ((far_own, 0), (far_own, HALF)), ((far_pair, 0), (far_pair, HALF)))
    for n, both in enumerate(kv_sources):
        shard = core if n % 2 == 0 else 1 - core
        at = rows((4 - n // 2 * 2 + shard) * tokens, tokens)
        for side, (ref, head) in enumerate(both):
            moves.append((part(ref, head, HD), kv_s.at[at, pl.ds(side * HD, HD)]))
    copies = [pltpu.make_async_copy(src, dst, sems.at[n]) for n, (src, dst) in enumerate(moves)]
    for copy in copies:
        copy.start()
    acc_s[...] = jnp.zeros_like(acc_s)
    for copy in copies:
        copy.wait()
    blocks = kv_s.shape[0] // BLK
    for at in range(blocks):
        kvt_s[:, at * BLK:(at + 1) * BLK] = kv_s[at * BLK:(at + 1) * BLK, :].T

    def attend(block, at, many, seen):
        span = many * BLK
        base = (block + MOST_BLK + 1 - many) * BLK
        window = rows(base, span)
        tok = rows(block * BLK, BLK)
        key_cols = slice(at * KV2, at * KV2 + HD)
        value_cols = slice(at * KV2 + HD, (at + 1) * KV2)
        q_here, g_here = q_s[tok, at * QW:(at + 1) * QW], g_s[tok, at * QW:(at + 1) * QW]
        qt = jnp.concatenate([q_here[:, n * HD:(n + 1) * HD].T for n in range(GROUP)], axis=1)
        gt = jnp.concatenate([g_here[:, n * HD:(n + 1) * HD].T for n in range(GROUP)], axis=1)
        part = 2 * BLK
        ts = [slice(n * part, (n + 1) * part) for n in range(GROUP * BLK // part)]
        edge = jnp.where(seen < many, F32(-1e30), F32(0.0))
        causal = (lax.broadcasted_iota(jnp.int32, (BLK, BLK), 0)
                  <= lax.broadcasted_iota(jnp.int32, (BLK, BLK), 1))
        causal = jnp.concatenate([causal] * (part // BLK), axis=1)
        keys, values = kv_s[window, key_cols], kv_s[window, value_cols]
        here = [slice(kb * BLK, (kb + 1) * BLK) for kb in range(many)]

        def scores(t):
            s_all = jnp.dot(keys, qt[:, t], preferred_element_type=F32)
            most = None
            for kb in range(many):
                s = s_all[here[kb], :]
                if kb == 0:
                    s = s + edge
                if kb == many - 1:
                    s = jnp.where(causal, s, F32(-1e30))
                s_s[here[kb], t] = s
                top = fold8(jnp.max, s)
                most = top if most is None else jnp.maximum(most, top)
            return jnp.max(most, axis=0, keepdims=True) * F32(SCALE * LOG2E)

        def weights(t, top):
            sums = None
            for kb in range(many):
                e = jnp.exp2(s_s[here[kb], t] * F32(SCALE * LOG2E) - top)
                e_s[here[kb], t] = e.astype(BF)
                total = fold8(jnp.sum, e)
                sums = total if sums is None else sums + total
            return 1.0 / jnp.sum(sums, axis=0, keepdims=True)

        def prob_grads(t):
            p_s[:span, t] = jnp.dot(values, gt[:, t], preferred_element_type=F32)

        def turned(to, t, value):
            low = value.astype(BF)
            for n in range(part // BLK):
                to[tok, t.start + n * BLK:t.start + (n + 1) * BLK] = low[:, n * BLK:(n + 1) * BLK].T
            return low

        def outputs(t, inv):
            ot = jnp.dot(kvt_s[value_cols, cols(base, span)], e_s[:span, t], preferred_element_type=F32) * inv
            ot_low = turned(o_s, t, ot)
            return jnp.sum(gt[:, t].astype(F32) * ot_low.astype(F32), axis=0, keepdims=True)

        def score_grads(t, dots):
            for kb in range(many):
                d_s[here[kb], t] = e_s[here[kb], t] * (p_s[here[kb], t] - dots).astype(BF)

        def query_grads(t, inv):
            turned(dq_s, t, jnp.dot(kvt_s[key_cols, cols(base, span)], d_s[:span, t],
                                    preferred_element_type=F32) * (inv * F32(SCALE)))

        t0, t1 = ts
        top0 = scores(t0)
        top1 = scores(t1)
        inv0 = weights(t0, top0)
        prob_grads(t0)
        dots0 = outputs(t0, inv0)
        inv1 = weights(t1, top1)
        prob_grads(t1)
        score_grads(t0, dots0)
        dots1 = outputs(t1, inv1)
        query_grads(t0, inv0)
        score_grads(t1, dots1)
        query_grads(t1, inv1)
        scale_rows = [inv0, inv1]
        inv = jnp.concatenate(scale_rows, axis=1)
        gt_low = (gt.astype(F32) * inv).astype(BF)
        qt_low = (qt.astype(F32) * (inv * F32(SCALE))).astype(BF)
        last = (((1,), (1,)), ((), ()))
        acc_s[window, value_cols] += lax.dot_general(e_s[:span, :], gt_low, last, preferred_element_type=F32)
        acc_s[window, key_cols] += lax.dot_general(d_s[:span, :], qt_low, last, preferred_element_type=F32)

    def step(block, carry):
        place = chip * (2 * tokens // BLK) + block
        doc = doc_ref[0, place]
        seen = jnp.int32(0)
        for back in range(MOST_BLK):
            there = place - back
            same = (there >= 0) & (doc_ref[0, jnp.maximum(there, 0)] == doc)
            seen += same.astype(jnp.int32)
        for many in range(2, MOST_BLK + 1, 2):
            @pl.when((seen == many) | (seen == many - 1))
            def _():
                attend(block, 0, many, seen)
        return carry

    lax.fori_loop(0, 2 * tokens // BLK, step, 0)
    far_out[...] = acc_s[BLK:2 * tokens, :].astype(BF)
    mid_out[...] = acc_s[2 * tokens:near_at, :].astype(BF)
    near_out[...] = acc_s[near_at:, :]
    leaving = [(o_s, o_own, mine), (o_s, o_pair, other), (dq_s, dq_own, mine), (dq_s, dq_pair, other)]
    copies = [pltpu.make_async_copy(src.at[at, :], dst, out_sems.at[n])
              for n, (src, dst, at) in enumerate(leaving)]
    for copy in copies:
        copy.start()
    for copy in copies:
        copy.wait()


def attend_half(chunk, docs, sources):
    tokens = sources[0].shape[0]
    all_rows = 6 * tokens
    most = MOST_BLK * BLK
    return call(
        functools.partial(core_kernel, chunk, tokens),
        "attend",
        [shape(tokens, QW)] * 4 + [
            shape(2 * tokens - BLK, KV2),
            shape(2 * tokens, KV2),
            shape(2 * tokens, KV2, F32),
        ],
        (docs, *sources),
        [
            pltpu.VMEM((2 * tokens, QW), BF),
            pltpu.VMEM((2 * tokens, QW), BF),
            pltpu.VMEM((all_rows, KV2), BF),
            pltpu.VMEM((KV2, all_rows), BF),
            pltpu.VMEM((all_rows, KV2), F32),
            pltpu.VMEM((most, QW), F32),
            pltpu.VMEM((most, QW), F32),
            pltpu.VMEM((most, QW), BF),
            pltpu.VMEM((most, QW), BF),
            pltpu.VMEM((2 * tokens, QW), BF),
            pltpu.VMEM((2 * tokens, QW), BF),
            pltpu.SemaphoreType.DMA((16,)),
            pltpu.SemaphoreType.DMA((4,)),
        ],
        [SMEM] + [ANY] * 12,
        [ANY] * 4 + [VMEM] * 3,
        ATTEND_BYTES,
        ATTEND_FLOPS)


def shards(queries, key_rows, value_rows, out_grad, doc_blocks):
    peers = lax.axis_size("ctx")
    sections = lax.axis_size("pipe")

    def move(value, chips, cross):
        pairs = [(i, (i // 2 + chips) % (peers // 2) * 2 + ((i % 2) ^ cross)) for i in range(peers)]
        return lax.ppermute(value, "ctx", pairs)

    def pass_back(value, cross):
        pairs = [(p * peers + i, (p - 1) % sections * peers + (i ^ cross))
                 for p in range(sections) for i in range(peers)]
        return lax.ppermute(value, ("pipe", "ctx"), pairs)

    q, g, k, v = queries[0], out_grad[0], key_rows[0], value_rows[0]

    def with_pair(value):
        return [value, move(value, 0, 1)]

    def half_of(value, half):
        width = value.shape[1] // 2
        return value[:, half * width:(half + 1) * width]

    near = pack(k, v)
    mid = [move(kv, 1, 0) for kv in near]
    pairs = [move(value, 0, 1) for value in (q, g, k, v)]
    own = [half_of(value, half) for half in range(2) for value in (q, g, k, v)]
    mid[0], *own = lax.optimization_barrier((mid[0], *own))
    far = [move(kv, 1, 0) for kv in mid]

    def attend(chunk):
        here = own[4 * chunk:4 * chunk + 4]
        return attend_half(chunk, doc_blocks, [
            *here[:2], *pairs[:2], *here[2:], *pairs[2:], *with_pair(mid[chunk]), *with_pair(far[chunk])])

    mid[1], far[0] = lax.optimization_barrier((mid[1], far[0]))
    o_own, o_pair, dq_own, dq_pair, far_part, mid_part, near_part = attend(0)
    mid_before, far_got = mid_part, move(far_part, -1, 0)
    q_parts = [pass_back(dq_own, 0), pass_back(dq_pair, 1)]
    outs = [o_own, move(o_pair, 0, 1)]
    far[1], near_part = lax.optimization_barrier((far[1], near_part))
    o_own, o_pair, dq_own, dq_pair, far_part, mid_part, near_last = attend(1)
    q_parts += [pass_back(dq_own, 0), pass_back(dq_pair, 1)]
    mid_before, near_last, q_parts[0], q_parts[1] = lax.optimization_barrier(
        (mid_before, near_last, q_parts[0], q_parts[1]))
    mid_part, q_parts[2], q_parts[3] = lax.optimization_barrier((mid_part, q_parts[2], q_parts[3]))
    far_part, far_got = lax.optimization_barrier((far_part, far_got))
    back = move(add_middle(mid_before, far_got), -1, 0)
    back_last = move(add_middle(mid_part, move(far_part, -1, 0)), -1, 0)
    outs += [o_own, move(o_pair, 0, 1)]
    ours, theirs = add_last(near_part, back)
    kv_parts = [pass_back(ours, 0), pass_back(theirs, 1)]
    near_last, kv_parts[0] = lax.optimization_barrier((near_last, kv_parts[0]))
    ours, theirs = add_last(near_last, back_last)
    kv_parts += [pass_back(ours, 0), pass_back(theirs, 1)]
    attn_out = lay_heads(outs, False)
    grad_query = lay_heads(q_parts, True)
    grad_key, grad_value = lay_kv(kv_parts)
    return attn_out[None], grad_query[None], grad_key[None], grad_value[None]


def solution(mesh):
    tokens = P("pipe", "ctx", None)
    return jax.shard_map(
        shards,
        mesh=mesh,
        in_specs=(tokens, tokens, tokens, tokens, P("pipe", None)),
        out_specs=(tokens, tokens, tokens, tokens),
        check_vma=False,
    )
```

```python
import functools
import math

import jax
import jax.numpy as jnp
from jax import lax
from jax.experimental import pallas as pl
from jax.experimental.pallas import tpu as pltpu
from jax.sharding import PartitionSpec as P

HD = 128
H = 16
KVH = 4
BLK = 128
MOST_BLK = 8

GROUP = H // KVH
HALF = KVH // 2
QW = GROUP * HD
KV2 = 2 * HD
SCALE = 1.0 / math.sqrt(HD)
LOG2E = math.log2(math.e)
SMALL_BYTES = 4 * 1024 * 1024
FIRST_BYTES = 56 * 1024 * 1024
ATTEND_BYTES = 20 * 1024 * 1024
ATTEND_FLOPS = 1000

BF = jnp.bfloat16
F32 = jnp.float32
ANY = pl.BlockSpec(memory_space=pl.ANY)
VMEM = pl.BlockSpec(memory_space=pltpu.VMEM)
SMEM = pl.BlockSpec(memory_space=pltpu.SMEM)


def shape(rows, cols, dtype=BF):
    return jax.ShapeDtypeStruct((rows, cols), dtype)


def cols(start, size):
    return pl.ds(pl.multiple_of(start, HD), size)


def rows(start, size):
    return pl.ds(pl.multiple_of(start, BLK), size)


def call(kernel, name, outs, args, scratch, in_specs=None, out_specs=None, limit=SMALL_BYTES, flops=1000):
    return pl.pallas_call(
        kernel,
        name=name,
        out_shape=outs,
        in_specs=in_specs or [ANY] * len(args),
        out_specs=out_specs or [ANY] * len(outs),
        scratch_shapes=scratch,
        compiler_params=pltpu.CompilerParams(vmem_limit_bytes=limit),
        cost_estimate=pl.CostEstimate(flops=flops, bytes_accessed=1000, transcendentals=0),
    )(*args)


def stage(moves, sems):
    copies = [pltpu.make_async_copy(src, dst, sems.at[n]) for n, (src, dst) in enumerate(moves)]
    for copy in copies:
        copy.start()
    return copies


def wait(copies):
    for copy in copies:
        copy.wait()


def pack_kernel(k_ref, v_ref, *rest):
    outs, (held, in_sems, out_sems) = rest[:2], rest[2:]
    width = k_ref.shape[1] // 2
    moves = []
    for half in range(2):
        for side, ref in enumerate((k_ref, v_ref)):
            moves.append((ref.at[:, pl.ds(half * width, width)], held.at[half, :, pl.ds(side * width, width)]))
    ins = stage(moves, in_sems)
    leaving = []
    for half, out in enumerate(outs):
        wait(ins[2 * half:2 * half + 2])
        leaving.append(pltpu.make_async_copy(held.at[half], out, out_sems.at[half]))
        leaving[-1].start()
    wait(leaving)


def pack(keys, values):
    return call(
        pack_kernel, "pack", [shape(*keys.shape)] * 2, (keys, values),
        [pltpu.VMEM((2, *keys.shape), BF), pltpu.SemaphoreType.DMA((4,)), pltpu.SemaphoreType.DMA((2,))],
        limit=FIRST_BYTES)


def add_middle_kernel(mid_ref, far_ref, out):
    trim = mid_ref.shape[0] - far_ref.shape[0]
    out[:trim, :] = mid_ref[:trim, :]
    out[trim:, :] = (mid_ref[trim:, :].astype(F32) + far_ref[...].astype(F32)).astype(BF)


def add_middle(mid, far):
    return call(add_middle_kernel, "add_middle", [shape(*mid.shape)], (mid, far), [],
                [VMEM] * 2, [VMEM])[0]


def add_last_kernel(near_ref, got_ref, straight, crossed):
    core = lax.rem(lax.axis_index("ctx"), 2)
    tokens = straight.shape[0]
    for out, shard in ((straight, core), (crossed, 1 - core)):
        at = rows(shard * tokens, tokens)
        out[...] = (near_ref[at, :].astype(F32) + got_ref[at, :].astype(F32)).astype(BF)


def add_last(near, got):
    tokens, width = near.shape[0] // 2, near.shape[1]
    return call(add_last_kernel, "add_last", [shape(tokens, width)] * 2, (near, got), [],
                [VMEM] * 2, [VMEM] * 2)


def lay_heads_kernel(blank_last, *refs):
    parts, (out, held, in_sems, out_sems) = refs[:-4], refs[-4:]
    core = lax.rem(lax.axis_index("ctx"), 2)
    moves = []
    for n, part in enumerate(parts):
        half = core if n % 2 == 0 else 1 - core
        moves.append((part, held.at[:, cols((n // 2 * HALF + half) * QW, QW)]))
    wait(stage(moves, in_sems))
    if blank_last:
        @pl.when(lax.axis_index("pipe") == lax.axis_size("pipe") - 1)
        def _():
            held[...] = jnp.zeros_like(held)
    wait(stage([(held, out)], out_sems))


def lay_heads(parts, blank_last):
    tokens = parts[0].shape[0]
    return call(
        functools.partial(lay_heads_kernel, blank_last), "lay_heads", [shape(tokens, H * HD)], parts,
        [pltpu.VMEM((tokens, H * HD), BF),
         pltpu.SemaphoreType.DMA((len(parts),)),
         pltpu.SemaphoreType.DMA((1,))])[0]


def lay_kv_kernel(*refs):
    parts, (key_out, value_out, held, in_sems, out_sems) = refs[:-5], refs[-5:]
    core = lax.rem(lax.axis_index("ctx"), 2)
    moves = []
    for n, part in enumerate(parts):
        half = core if n % 2 == 0 else 1 - core
        dst = cols((n // 2 * HALF + half) * HD, HD)
        for side in range(2):
            moves.append((part.at[:, pl.ds(side * HD, HD)], held.at[side, :, dst]))
    wait(stage(moves, in_sems))

    @pl.when(lax.axis_index("pipe") == lax.axis_size("pipe") - 1)
    def _():
        held[...] = jnp.zeros_like(held)

    wait(stage([(held.at[0], key_out), (held.at[1], value_out)], out_sems))


def lay_kv(parts):
    tokens = parts[0].shape[0]
    return call(
        lay_kv_kernel, "lay_kv", [shape(tokens, KVH * HD)] * 2, parts,
        [pltpu.VMEM((2, tokens, KVH * HD), BF),
         pltpu.SemaphoreType.DMA((2 * KVH,)),
         pltpu.SemaphoreType.DMA((2,))])


def fold8(op, value):
    return op(value.reshape(value.shape[0] // 8, 8, value.shape[1]), axis=0)


def core_kernel(chunk, tokens, doc_ref, *rest):
    (sources, (o_own, o_pair, dq_own, dq_pair, far_out, mid_out, near_out,
               q_s, g_s, kv_s, kvt_s, acc_s, s_s, p_s, e_s, d_s, o_s, dq_s, sems, out_sems)) = rest[:12], rest[12:]
    q_own, g_own, q_pair, g_pair, k_own, v_own, k_pair, v_pair, mid_own, mid_pair, far_own, far_pair = sources
    me = lax.axis_index("ctx")
    chip, core = lax.div(me, 2), lax.rem(me, 2)
    near_at = 4 * tokens
    first = chunk * HALF

    def part(ref, head, width):
        return ref.at[:, cols((head + core) * width, width)]

    mine, other = rows(core * tokens, tokens), rows((1 - core) * tokens, tokens)
    moves = [
        (part(q_own, 0, QW), q_s.at[mine, :]), (part(q_pair, first, QW), q_s.at[other, :]),
        (part(g_own, 0, QW), g_s.at[mine, :]), (part(g_pair, first, QW), g_s.at[other, :]),
    ]
    kv_sources = (((k_own, 0), (v_own, 0)), ((k_pair, first), (v_pair, first)),
                  ((mid_own, 0), (mid_own, HALF)), ((mid_pair, 0), (mid_pair, HALF)),
                  ((far_own, 0), (far_own, HALF)), ((far_pair, 0), (far_pair, HALF)))
    for n, both in enumerate(kv_sources):
        shard = core if n % 2 == 0 else 1 - core
        at = rows((4 - n // 2 * 2 + shard) * tokens, tokens)
        for side, (ref, head) in enumerate(both):
            moves.append((part(ref, head, HD), kv_s.at[at, pl.ds(side * HD, HD)]))
    copies = [pltpu.make_async_copy(src, dst, sems.at[n]) for n, (src, dst) in enumerate(moves)]
    for copy in copies:
        copy.start()
    acc_s[...] = jnp.zeros_like(acc_s)
    for copy in copies:
        copy.wait()
    blocks = kv_s.shape[0] // BLK
    for at in range(blocks):
        kvt_s[:, at * BLK:(at + 1) * BLK] = kv_s[at * BLK:(at + 1) * BLK, :].T

    def attend(block, at, many, seen):
        span = many * BLK
        base = (block + MOST_BLK + 1 - many) * BLK
        window = rows(base, span)
        tok = rows(block * BLK, BLK)
        key_cols = slice(at * KV2, at * KV2 + HD)
        value_cols = slice(at * KV2 + HD, (at + 1) * KV2)
        q_here, g_here = q_s[tok, at * QW:(at + 1) * QW], g_s[tok, at * QW:(at + 1) * QW]
        qt = jnp.concatenate([q_here[:, n * HD:(n + 1) * HD].T for n in range(GROUP)], axis=1)
        gt = jnp.concatenate([g_here[:, n * HD:(n + 1) * HD].T for n in range(GROUP)], axis=1)
        part = 2 * BLK
        ts = [slice(n * part, (n + 1) * part) for n in range(GROUP * BLK // part)]
        edge = jnp.where(seen < many, F32(-1e30), F32(0.0))
        causal = (lax.broadcasted_iota(jnp.int32, (BLK, BLK), 0)
                  <= lax.broadcasted_iota(jnp.int32, (BLK, BLK), 1))
        causal = jnp.concatenate([causal] * (part // BLK), axis=1)
        keys, values = kv_s[window, key_cols], kv_s[window, value_cols]
        here = [slice(kb * BLK, (kb + 1) * BLK) for kb in range(many)]

        def scores(t):
            s_all = jnp.dot(keys, qt[:, t], preferred_element_type=F32)
            most = None
            for kb in range(many):
                s = s_all[here[kb], :]
                if kb == 0:
                    s = s + edge
                if kb == many - 1:
                    s = jnp.where(causal, s, F32(-1e30))
                s_s[here[kb], t] = s
                top = fold8(jnp.max, s)
                most = top if most is None else jnp.maximum(most, top)
            return jnp.max(most, axis=0, keepdims=True) * F32(SCALE * LOG2E)

        def weights(t, top):
            sums = None
            for kb in range(many):
                e = jnp.exp2(s_s[here[kb], t] * F32(SCALE * LOG2E) - top)
                e_s[here[kb], t] = e.astype(BF)
                total = fold8(jnp.sum, e)
                sums = total if sums is None else sums + total
            return 1.0 / jnp.sum(sums, axis=0, keepdims=True)

        def prob_grads(t):
            p_s[:span, t] = jnp.dot(values, gt[:, t], preferred_element_type=F32)

        def turned(to, t, value):
            low = value.astype(BF)
            for n in range(part // BLK):
                to[tok, t.start + n * BLK:t.start + (n + 1) * BLK] = low[:, n * BLK:(n + 1) * BLK].T
            return low

        def outputs(t, inv):
            ot = jnp.dot(kvt_s[value_cols, cols(base, span)], e_s[:span, t], preferred_element_type=F32) * inv
            ot_low = turned(o_s, t, ot)
            return jnp.sum(gt[:, t].astype(F32) * ot_low.astype(F32), axis=0, keepdims=True)

        def score_grads(t, dots):
            for kb in range(many):
                d_s[here[kb], t] = e_s[here[kb], t] * (p_s[here[kb], t] - dots).astype(BF)

        def query_grads(t, inv):
            turned(dq_s, t, jnp.dot(kvt_s[key_cols, cols(base, span)], d_s[:span, t],
                                    preferred_element_type=F32) * (inv * F32(SCALE)))

        t0, t1 = ts
        top0 = scores(t0)
        top1 = scores(t1)
        inv0 = weights(t0, top0)
        prob_grads(t0)
        dots0 = outputs(t0, inv0)
        inv1 = weights(t1, top1)
        prob_grads(t1)
        dots1 = outputs(t1, inv1)
        inv = jnp.concatenate([inv0, inv1], axis=1)
        gt_low = (gt.astype(F32) * inv).astype(BF)
        qt_low = (qt.astype(F32) * (inv * F32(SCALE))).astype(BF)
        last = (((1,), (1,)), ((), ()))
        acc_s[window, value_cols] += lax.dot_general(e_s[:span, :], gt_low, last, preferred_element_type=F32)
        score_grads(t0, dots0)
        query_grads(t0, inv0)
        score_grads(t1, dots1)
        query_grads(t1, inv1)
        acc_s[window, key_cols] += lax.dot_general(d_s[:span, :], qt_low, last, preferred_element_type=F32)

    def step(block, carry):
        place = chip * (2 * tokens // BLK) + block
        doc = doc_ref[0, place]
        seen = jnp.int32(0)
        for back in range(MOST_BLK):
            there = place - back
            same = (there >= 0) & (doc_ref[0, jnp.maximum(there, 0)] == doc)
            seen += same.astype(jnp.int32)
        for many in range(2, MOST_BLK + 1, 2):
            @pl.when((seen == many) | (seen == many - 1))
            def _():
                attend(block, 0, many, seen)
        return carry

    lax.fori_loop(0, 2 * tokens // BLK, step, 0)
    far_out[...] = acc_s[BLK:2 * tokens, :].astype(BF)
    mid_out[...] = acc_s[2 * tokens:near_at, :].astype(BF)
    near_out[...] = acc_s[near_at:, :].astype(BF)
    leaving = [(o_s, o_own, mine), (o_s, o_pair, other), (dq_s, dq_own, mine), (dq_s, dq_pair, other)]
    copies = [pltpu.make_async_copy(src.at[at, :], dst, out_sems.at[n])
              for n, (src, dst, at) in enumerate(leaving)]
    for copy in copies:
        copy.start()
    for copy in copies:
        copy.wait()


def attend_half(chunk, docs, sources):
    tokens = sources[0].shape[0]
    all_rows = 6 * tokens
    most = MOST_BLK * BLK
    return call(
        functools.partial(core_kernel, chunk, tokens),
        "attend",
        [shape(tokens, QW)] * 4 + [
            shape(2 * tokens - BLK, KV2),
            shape(2 * tokens, KV2),
            shape(2 * tokens, KV2),
        ],
        (docs, *sources),
        [
            pltpu.VMEM((2 * tokens, QW), BF),
            pltpu.VMEM((2 * tokens, QW), BF),
            pltpu.VMEM((all_rows, KV2), BF),
            pltpu.VMEM((KV2, all_rows), BF),
            pltpu.VMEM((all_rows, KV2), F32),
            pltpu.VMEM((most, QW), F32),
            pltpu.VMEM((most, QW), F32),
            pltpu.VMEM((most, QW), BF),
            pltpu.VMEM((most, QW), BF),
            pltpu.VMEM((2 * tokens, QW), BF),
            pltpu.VMEM((2 * tokens, QW), BF),
            pltpu.SemaphoreType.DMA((16,)),
            pltpu.SemaphoreType.DMA((4,)),
        ],
        [SMEM] + [ANY] * 12,
        [ANY] * 4 + [VMEM] * 3,
        ATTEND_BYTES,
        ATTEND_FLOPS)


def shards(queries, key_rows, value_rows, out_grad, doc_blocks):
    peers = lax.axis_size("ctx")
    sections = lax.axis_size("pipe")

    def move(value, chips, cross):
        pairs = [(i, (i // 2 + chips) % (peers // 2) * 2 + ((i % 2) ^ cross)) for i in range(peers)]
        return lax.ppermute(value, "ctx", pairs)

    def pass_back(value, cross):
        pairs = [(p * peers + i, (p - 1) % sections * peers + (i ^ cross))
                 for p in range(sections) for i in range(peers)]
        return lax.ppermute(value, ("pipe", "ctx"), pairs)

    q, g, k, v = queries[0], out_grad[0], key_rows[0], value_rows[0]

    def with_pair(value):
        return [value, move(value, 0, 1)]

    def half_of(value, half):
        width = value.shape[1] // 2
        return value[:, half * width:(half + 1) * width]

    near = pack(k, v)
    mid = [move(kv, 1, 0) for kv in near]
    pairs = [move(value, 0, 1) for value in (q, g, k, v)]
    own = [half_of(value, half) for half in range(2) for value in (q, g, k, v)]
    mid[0], *own = lax.optimization_barrier((mid[0], *own))
    far = [move(kv, 1, 0) for kv in mid]

    def attend(chunk):
        here = own[4 * chunk:4 * chunk + 4]
        return attend_half(chunk, doc_blocks, [
            *here[:2], *pairs[:2], *here[2:], *pairs[2:], *with_pair(mid[chunk]), *with_pair(far[chunk])])

    mid[1], far[0] = lax.optimization_barrier((mid[1], far[0]))
    o_own, o_pair, dq_own, dq_pair, far_part, mid_part, near_part = attend(0)
    mid_before, far_got = mid_part, move(far_part, -1, 0)
    q_parts = [pass_back(dq_own, 0), pass_back(dq_pair, 1)]
    outs = [o_own, move(o_pair, 0, 1)]
    far[1], near_part = lax.optimization_barrier((far[1], near_part))
    o_own, o_pair, dq_own, dq_pair, far_part, mid_part, near_last = attend(1)
    q_parts += [pass_back(dq_own, 0), pass_back(dq_pair, 1)]
    mid_before, near_last, q_parts[0], q_parts[1] = lax.optimization_barrier(
        (mid_before, near_last, q_parts[0], q_parts[1]))
    mid_part, q_parts[2] = lax.optimization_barrier((mid_part, q_parts[2]))
    far_part, far_got = lax.optimization_barrier((far_part, far_got))
    back = move(add_middle(mid_before, far_got), -1, 0)
    back_last = move(add_middle(mid_part, move(far_part, -1, 0)), -1, 0)
    outs += [o_own, move(o_pair, 0, 1)]
    ours, theirs = add_last(near_part, back)
    kv_parts = [pass_back(ours, 0), pass_back(theirs, 1)]
    ours, theirs = add_last(near_last, back_last)
    ours, theirs, kv_parts[0] = lax.optimization_barrier((ours, theirs, kv_parts[0]))
    kv_parts += [pass_back(ours, 0), pass_back(theirs, 1)]
    attn_out = lay_heads(outs, False)
    grad_query = lay_heads(q_parts, True)
    grad_key, grad_value = lay_kv(kv_parts)
    return attn_out[None], grad_query[None], grad_key[None], grad_value[None]


def solution(mesh):
    tokens = P("pipe", "ctx", None)
    return jax.shard_map(
        shards,
        mesh=mesh,
        in_specs=(tokens, tokens, tokens, tokens, P("pipe", None)),
        out_specs=(tokens, tokens, tokens, tokens),
        check_vma=False,
    )
```

```python
import functools
import math

import jax
import jax.numpy as jnp
from jax import lax
from jax.experimental import pallas as pl
from jax.experimental.pallas import tpu as pltpu
from jax.sharding import PartitionSpec as P

HD = 128
H = 16
KVH = 4
BLK = 128
MOST_BLK = 8

GROUP = H // KVH
HALF = KVH // 2
QW = GROUP * HD
KV2 = 2 * HD
SCALE = 1.0 / math.sqrt(HD)
LOG2E = math.log2(math.e)
SMALL_BYTES = 4 * 1024 * 1024
FIRST_BYTES = 56 * 1024 * 1024
ATTEND_BYTES = 20 * 1024 * 1024
ATTEND_FLOPS = 1000

BF = jnp.bfloat16
F32 = jnp.float32
ANY = pl.BlockSpec(memory_space=pl.ANY)
VMEM = pl.BlockSpec(memory_space=pltpu.VMEM)
SMEM = pl.BlockSpec(memory_space=pltpu.SMEM)


def shape(rows, cols, dtype=BF):
    return jax.ShapeDtypeStruct((rows, cols), dtype)


def cols(start, size):
    return pl.ds(pl.multiple_of(start, HD), size)


def rows(start, size):
    return pl.ds(pl.multiple_of(start, BLK), size)


def call(kernel, name, outs, args, scratch, in_specs=None, out_specs=None, limit=SMALL_BYTES, flops=1000):
    return pl.pallas_call(
        kernel,
        name=name,
        out_shape=outs,
        in_specs=in_specs or [ANY] * len(args),
        out_specs=out_specs or [ANY] * len(outs),
        scratch_shapes=scratch,
        compiler_params=pltpu.CompilerParams(vmem_limit_bytes=limit),
        cost_estimate=pl.CostEstimate(flops=flops, bytes_accessed=1000, transcendentals=0),
    )(*args)


def stage(moves, sems):
    copies = [pltpu.make_async_copy(src, dst, sems.at[n]) for n, (src, dst) in enumerate(moves)]
    for copy in copies:
        copy.start()
    return copies


def wait(copies):
    for copy in copies:
        copy.wait()


def pack_kernel(k_ref, v_ref, *rest):
    outs, (held, in_sems, out_sems) = rest[:2], rest[2:]
    width = k_ref.shape[1] // 2
    moves = []
    for half in range(2):
        for side, ref in enumerate((k_ref, v_ref)):
            moves.append((ref.at[:, pl.ds(half * width, width)], held.at[half, :, pl.ds(side * width, width)]))
    ins = stage(moves, in_sems)
    leaving = []
    for half, out in enumerate(outs):
        wait(ins[2 * half:2 * half + 2])
        leaving.append(pltpu.make_async_copy(held.at[half], out, out_sems.at[half]))
        leaving[-1].start()
    wait(leaving)


def pack(keys, values):
    return call(
        pack_kernel, "pack", [shape(*keys.shape)] * 2, (keys, values),
        [pltpu.VMEM((2, *keys.shape), BF), pltpu.SemaphoreType.DMA((4,)), pltpu.SemaphoreType.DMA((2,))],
        limit=FIRST_BYTES)


def add_middle_kernel(mid_ref, far_ref, out):
    trim = mid_ref.shape[0] - far_ref.shape[0]
    out[:trim, :] = mid_ref[:trim, :]
    out[trim:, :] = (mid_ref[trim:, :].astype(F32) + far_ref[...].astype(F32)).astype(BF)


def add_middle(mid, far):
    return call(add_middle_kernel, "add_middle", [shape(*mid.shape)], (mid, far), [],
                [VMEM] * 2, [VMEM])[0]


def add_last_kernel(near_ref, got_ref, straight, crossed):
    core = lax.rem(lax.axis_index("ctx"), 2)
    tokens = straight.shape[0]
    for out, shard in ((straight, core), (crossed, 1 - core)):
        at = rows(shard * tokens, tokens)
        out[...] = (near_ref[at, :].astype(F32) + got_ref[at, :].astype(F32)).astype(BF)


def add_last(near, got):
    tokens, width = near.shape[0] // 2, near.shape[1]
    return call(add_last_kernel, "add_last", [shape(tokens, width)] * 2, (near, got), [],
                [VMEM] * 2, [VMEM] * 2)


def lay_heads_kernel(blank_last, *refs):
    parts, (out, held, in_sems, out_sems) = refs[:-4], refs[-4:]
    core = lax.rem(lax.axis_index("ctx"), 2)
    moves = []
    for n, part in enumerate(parts):
        half = core if n % 2 == 0 else 1 - core
        moves.append((part, held.at[:, cols((n // 2 * HALF + half) * QW, QW)]))
    wait(stage(moves, in_sems))
    if blank_last:
        @pl.when(lax.axis_index("pipe") == lax.axis_size("pipe") - 1)
        def _():
            held[...] = jnp.zeros_like(held)
    wait(stage([(held, out)], out_sems))


def lay_heads(parts, blank_last):
    tokens = parts[0].shape[0]
    return call(
        functools.partial(lay_heads_kernel, blank_last), "lay_heads", [shape(tokens, H * HD)], parts,
        [pltpu.VMEM((tokens, H * HD), BF),
         pltpu.SemaphoreType.DMA((len(parts),)),
         pltpu.SemaphoreType.DMA((1,))])[0]


def lay_kv_kernel(*refs):
    parts, (key_out, value_out, held, in_sems, out_sems) = refs[:-5], refs[-5:]
    core = lax.rem(lax.axis_index("ctx"), 2)
    moves = []
    for n, part in enumerate(parts):
        half = core if n % 2 == 0 else 1 - core
        dst = cols((n // 2 * HALF + half) * HD, HD)
        for side in range(2):
            moves.append((part.at[:, pl.ds(side * HD, HD)], held.at[side, :, dst]))
    wait(stage(moves, in_sems))

    @pl.when(lax.axis_index("pipe") == lax.axis_size("pipe") - 1)
    def _():
        held[...] = jnp.zeros_like(held)

    wait(stage([(held.at[0], key_out), (held.at[1], value_out)], out_sems))


def lay_kv(parts):
    tokens = parts[0].shape[0]
    return call(
        lay_kv_kernel, "lay_kv", [shape(tokens, KVH * HD)] * 2, parts,
        [pltpu.VMEM((2, tokens, KVH * HD), BF),
         pltpu.SemaphoreType.DMA((2 * KVH,)),
         pltpu.SemaphoreType.DMA((2,))])


def fold8(op, value):
    return op(value.reshape(value.shape[0] // 8, 8, value.shape[1]), axis=0)


def core_kernel(second, tokens, doc_ref, *rest):
    (sources, (o_own, o_pair, dq_own, dq_pair, far_out, mid_out, near_out,
               q_s, g_s, kv_s, kvt_s, acc_s, s_s, p_s, e_s, d_s, o_s, dq_s, sems, out_sems)) = rest[:12], rest[12:]
    q_own, g_own, q_pair, g_pair, k_own, v_own, k_pair, v_pair, mid_own, mid_pair, far_own, far_pair = sources
    me = lax.axis_index("ctx")
    chip, core = lax.div(me, 2), lax.rem(me, 2)
    near_at = 4 * tokens

    def part(ref, head, width):
        return ref.at[:, cols((head + core) * width, width)]

    mine, other = rows(core * tokens, tokens), rows((1 - core) * tokens, tokens)
    moves = [
        (part(q_own, 0, QW), q_s.at[mine, :]), (part(q_pair, 0, QW), q_s.at[other, :]),
        (part(g_own, second, QW), g_s.at[mine, :]), (part(g_pair, second, QW), g_s.at[other, :]),
    ]
    kv_sources = (((k_own, 0), (v_own, second)), ((k_pair, 0), (v_pair, second)),
                  ((mid_own, 0), (mid_own, HALF)), ((mid_pair, 0), (mid_pair, HALF)),
                  ((far_own, 0), (far_own, HALF)), ((far_pair, 0), (far_pair, HALF)))
    for n, both in enumerate(kv_sources):
        shard = core if n % 2 == 0 else 1 - core
        at = rows((4 - n // 2 * 2 + shard) * tokens, tokens)
        for side, (ref, head) in enumerate(both):
            moves.append((part(ref, head, HD), kv_s.at[at, pl.ds(side * HD, HD)]))
    copies = [pltpu.make_async_copy(src, dst, sems.at[n]) for n, (src, dst) in enumerate(moves)]
    for copy in copies:
        copy.start()
    acc_s[...] = jnp.zeros_like(acc_s)
    for copy in copies:
        copy.wait()
    blocks = kv_s.shape[0] // BLK
    for at in range(blocks):
        kvt_s[:, at * BLK:(at + 1) * BLK] = kv_s[at * BLK:(at + 1) * BLK, :].T

    def attend(block, at, many, seen):
        span = many * BLK
        base = (block + MOST_BLK + 1 - many) * BLK
        window = rows(base, span)
        tok = rows(block * BLK, BLK)
        key_cols = slice(at * KV2, at * KV2 + HD)
        value_cols = slice(at * KV2 + HD, (at + 1) * KV2)
        q_here, g_here = q_s[tok, at * QW:(at + 1) * QW], g_s[tok, at * QW:(at + 1) * QW]
        qt = jnp.concatenate([q_here[:, n * HD:(n + 1) * HD].T for n in range(GROUP)], axis=1)
        gt = jnp.concatenate([g_here[:, n * HD:(n + 1) * HD].T for n in range(GROUP)], axis=1)
        part = 2 * BLK
        ts = [slice(n * part, (n + 1) * part) for n in range(GROUP * BLK // part)]
        edge = jnp.where(seen < many, F32(-1e30), F32(0.0))
        causal = (lax.broadcasted_iota(jnp.int32, (BLK, BLK), 0)
                  <= lax.broadcasted_iota(jnp.int32, (BLK, BLK), 1))
        causal = jnp.concatenate([causal] * (part // BLK), axis=1)
        keys, values = kv_s[window, key_cols], kv_s[window, value_cols]
        here = [slice(kb * BLK, (kb + 1) * BLK) for kb in range(many)]

        def scores(t):
            s_all = jnp.dot(keys, qt[:, t], preferred_element_type=F32)
            most = None
            for kb in range(many):
                s = s_all[here[kb], :]
                if kb == 0:
                    s = s + edge
                if kb == many - 1:
                    s = jnp.where(causal, s, F32(-1e30))
                s_s[here[kb], t] = s
                top = fold8(jnp.max, s)
                most = top if most is None else jnp.maximum(most, top)
            return jnp.max(most, axis=0, keepdims=True) * F32(SCALE * LOG2E)

        def weights(t, top):
            sums = None
            for kb in range(many):
                e = jnp.exp2(s_s[here[kb], t] * F32(SCALE * LOG2E) - top)
                e_s[here[kb], t] = e.astype(BF)
                total = fold8(jnp.sum, e)
                sums = total if sums is None else sums + total
            return 1.0 / jnp.sum(sums, axis=0, keepdims=True)

        def prob_grads(t):
            p_s[:span, t] = jnp.dot(values, gt[:, t], preferred_element_type=F32)

        def turned(to, t, value):
            low = value.astype(BF)
            for n in range(part // BLK):
                to[tok, t.start + n * BLK:t.start + (n + 1) * BLK] = low[:, n * BLK:(n + 1) * BLK].T
            return low

        def outputs(t, inv):
            ot = jnp.dot(kvt_s[value_cols, cols(base, span)], e_s[:span, t], preferred_element_type=F32) * inv
            ot_low = turned(o_s, t, ot)
            return jnp.sum(gt[:, t].astype(F32) * ot_low.astype(F32), axis=0, keepdims=True)

        def score_grads(t, dots):
            for kb in range(many):
                d_s[here[kb], t] = e_s[here[kb], t] * (p_s[here[kb], t] - dots).astype(BF)

        def query_grads(t, inv):
            turned(dq_s, t, jnp.dot(kvt_s[key_cols, cols(base, span)], d_s[:span, t],
                                    preferred_element_type=F32) * (inv * F32(SCALE)))

        t0, t1 = ts
        top0 = scores(t0)
        top1 = scores(t1)
        inv0 = weights(t0, top0)
        prob_grads(t0)
        dots0 = outputs(t0, inv0)
        inv1 = weights(t1, top1)
        prob_grads(t1)
        dots1 = outputs(t1, inv1)
        inv = jnp.concatenate([inv0, inv1], axis=1)
        gt_low = (gt.astype(F32) * inv).astype(BF)
        qt_low = (qt.astype(F32) * (inv * F32(SCALE))).astype(BF)
        last = (((1,), (1,)), ((), ()))
        acc_s[window, value_cols] += lax.dot_general(e_s[:span, :], gt_low, last, preferred_element_type=F32)
        score_grads(t0, dots0)
        query_grads(t0, inv0)
        score_grads(t1, dots1)
        query_grads(t1, inv1)
        acc_s[window, key_cols] += lax.dot_general(d_s[:span, :], qt_low, last, preferred_element_type=F32)

    def step(block, carry):
        place = chip * (2 * tokens // BLK) + block
        doc = doc_ref[0, place]
        seen = jnp.int32(0)
        for back in range(MOST_BLK):
            there = place - back
            same = (there >= 0) & (doc_ref[0, jnp.maximum(there, 0)] == doc)
            seen += same.astype(jnp.int32)
        for many in range(2, MOST_BLK + 1, 2):
            @pl.when((seen == many) | (seen == many - 1))
            def _():
                attend(block, 0, many, seen)
        return carry

    lax.fori_loop(0, 2 * tokens // BLK, step, 0)
    far_out[...] = acc_s[BLK:2 * tokens, :].astype(BF)
    mid_out[...] = acc_s[2 * tokens:near_at, :].astype(BF)
    near_out[...] = acc_s[near_at:, :].astype(BF)
    leaving = [(o_s, o_own, mine), (o_s, o_pair, other), (dq_s, dq_own, mine), (dq_s, dq_pair, other)]
    copies = [pltpu.make_async_copy(src.at[at, :], dst, out_sems.at[n])
              for n, (src, dst, at) in enumerate(leaving)]
    for copy in copies:
        copy.start()
    for copy in copies:
        copy.wait()


def attend_half(second, docs, sources):
    tokens = sources[0].shape[0]
    all_rows = 6 * tokens
    most = MOST_BLK * BLK
    return call(
        functools.partial(core_kernel, second, tokens),
        "attend",
        [shape(tokens, QW)] * 4 + [
            shape(2 * tokens - BLK, KV2),
            shape(2 * tokens, KV2),
            shape(2 * tokens, KV2),
        ],
        (docs, *sources),
        [
            pltpu.VMEM((2 * tokens, QW), BF),
            pltpu.VMEM((2 * tokens, QW), BF),
            pltpu.VMEM((all_rows, KV2), BF),
            pltpu.VMEM((KV2, all_rows), BF),
            pltpu.VMEM((all_rows, KV2), F32),
            pltpu.VMEM((most, QW), F32),
            pltpu.VMEM((most, QW), F32),
            pltpu.VMEM((most, QW), BF),
            pltpu.VMEM((most, QW), BF),
            pltpu.VMEM((2 * tokens, QW), BF),
            pltpu.VMEM((2 * tokens, QW), BF),
            pltpu.SemaphoreType.DMA((16,)),
            pltpu.SemaphoreType.DMA((4,)),
        ],
        [SMEM] + [ANY] * 12,
        [ANY] * 4 + [VMEM] * 3,
        ATTEND_BYTES,
        ATTEND_FLOPS)


def shards(queries, key_rows, value_rows, out_grad, doc_blocks):
    peers = lax.axis_size("ctx")
    sections = lax.axis_size("pipe")

    def move(value, chips, cross):
        pairs = [(i, (i // 2 + chips) % (peers // 2) * 2 + ((i % 2) ^ cross)) for i in range(peers)]
        return lax.ppermute(value, "ctx", pairs)

    def pass_on(value, by, cross):
        pairs = [(p * peers + i, (p + by) % sections * peers + (i ^ cross))
                 for p in range(sections) for i in range(peers)]
        return lax.ppermute(value, ("pipe", "ctx"), pairs)

    q, g, k, v = queries[0], out_grad[0], key_rows[0], value_rows[0]

    def with_pair(value):
        return [value, move(value, 0, 1)]

    def half_of(value, half):
        width = value.shape[1] // 2
        return value[:, half * width:(half + 1) * width]

    kv_here, kv_next = pack(k, v)
    mid_here = move(kv_here, 1, 0)
    kv_next = pass_on(kv_next, -1, 0)
    docs_next = pass_on(doc_blocks, -1, 0)
    pairs = [move(value, 0, 1) for value in (q, g, k, v)]
    q_here, g_here, k_here, v_here = [half_of(value, 0) for value in (q, g, k, v)]
    qg_next = jnp.concatenate([half_of(q, 1), half_of(g, 1)], axis=1)
    mid_here, docs_next, qg_next, q_here, g_here, k_here, v_here = lax.optimization_barrier(
        (mid_here, docs_next, qg_next, q_here, g_here, k_here, v_here))
    qg_next = pass_on(qg_next, -1, 0)
    far_here = move(mid_here, 1, 0)
    mid_next = move(kv_next, 1, 0)
    far_next = move(mid_next, 1, 0)
    mid_next, far_here = lax.optimization_barrier((mid_next, far_here))
    o_own, o_pair, dq_own, dq_pair, far_part, mid_part, near_part = attend_half(0, doc_blocks, [
        q_here, g_here, *pairs[:2], k_here, v_here, *pairs[2:], *with_pair(mid_here), *with_pair(far_here)])
    mid_before, far_got = mid_part, move(far_part, -1, 0)
    q_parts = [pass_on(dq_own, -1, 0), pass_on(dq_pair, -1, 1)]
    outs = [o_own, move(o_pair, 0, 1)]
    far_next, qg_next, near_part = lax.optimization_barrier((far_next, qg_next, near_part))
    kv_pair, qg_pair = move(kv_next, 0, 1), move(qg_next, 0, 1)
    o_own, o_pair, dq_own, dq_pair, far_part, mid_part, near_last = attend_half(HALF, docs_next, [
        qg_next, qg_next, qg_pair, qg_pair, kv_next, kv_next, kv_pair, kv_pair,
        *with_pair(mid_next), *with_pair(far_next)])
    mid_before, near_last, *q_parts = lax.optimization_barrier((mid_before, near_last, *q_parts))
    far_part, far_got = lax.optimization_barrier((far_part, far_got))
    back = move(add_middle(mid_before, far_got), -1, 0)
    back_last = move(add_middle(mid_part, move(far_part, -1, 0)), -1, 0)
    outs += [pass_on(o_own, 1, 0), pass_on(o_pair, 1, 1)]
    q_parts += [dq_own, move(dq_pair, 0, 1)]
    ours, theirs = add_last(near_part, back)
    kv_parts = [pass_on(ours, -1, 0), pass_on(theirs, -1, 1)]
    near_last, kv_parts[0], outs[2], outs[3] = lax.optimization_barrier(
        (near_last, kv_parts[0], outs[2], outs[3]))
    ours, theirs = add_last(near_last, back_last)
    kv_parts += [ours, move(theirs, 0, 1)]
    attn_out = lay_heads(outs, False)
    grad_query = lay_heads(q_parts, True)
    grad_key, grad_value = lay_kv(kv_parts)
    return attn_out[None], grad_query[None], grad_key[None], grad_value[None]


def solution(mesh):
    tokens = P("pipe", "ctx", None)
    return jax.shard_map(
        shards,
        mesh=mesh,
        in_specs=(tokens, tokens, tokens, tokens, P("pipe", None)),
        out_specs=(tokens, tokens, tokens, tokens),
        check_vma=False,
    )
```

```python
import functools
import math

import jax
import jax.numpy as jnp
from jax import lax
from jax.experimental import pallas as pl
from jax.experimental.pallas import tpu as pltpu
from jax.sharding import PartitionSpec as P

HD = 128
H = 16
KVH = 4
BLK = 128
MOST_BLK = 8

GROUP = H // KVH
HALF = KVH // 2
QW = GROUP * HD
KV2 = 2 * HD
SCALE = 1.0 / math.sqrt(HD)
LOG2E = math.log2(math.e)
SMALL_BYTES = 4 * 1024 * 1024
FIRST_BYTES = 56 * 1024 * 1024
ATTEND_BYTES = 20 * 1024 * 1024
ATTEND_FLOPS = 1000

BF = jnp.bfloat16
F32 = jnp.float32
ANY = pl.BlockSpec(memory_space=pl.ANY)
VMEM = pl.BlockSpec(memory_space=pltpu.VMEM)
SMEM = pl.BlockSpec(memory_space=pltpu.SMEM)


def shape(rows, cols, dtype=BF):
    return jax.ShapeDtypeStruct((rows, cols), dtype)


def cols(start, size):
    return pl.ds(pl.multiple_of(start, HD), size)


def rows(start, size):
    return pl.ds(pl.multiple_of(start, BLK), size)


def call(kernel, name, outs, args, scratch, in_specs=None, out_specs=None, limit=SMALL_BYTES, flops=1000):
    return pl.pallas_call(
        kernel,
        name=name,
        out_shape=outs,
        in_specs=in_specs or [ANY] * len(args),
        out_specs=out_specs or [ANY] * len(outs),
        scratch_shapes=scratch,
        compiler_params=pltpu.CompilerParams(vmem_limit_bytes=limit),
        cost_estimate=pl.CostEstimate(flops=flops, bytes_accessed=1000, transcendentals=0),
    )(*args)


def stage(moves, sems):
    copies = [pltpu.make_async_copy(src, dst, sems.at[n]) for n, (src, dst) in enumerate(moves)]
    for copy in copies:
        copy.start()
    return copies


def wait(copies):
    for copy in copies:
        copy.wait()


def pack_kernel(k_ref, v_ref, *rest):
    outs, (held, in_sems, out_sems) = rest[:2], rest[2:]
    width = k_ref.shape[1] // 2
    moves = []
    for half in range(2):
        for side, ref in enumerate((k_ref, v_ref)):
            moves.append((ref.at[:, pl.ds(half * width, width)], held.at[half, :, pl.ds(side * width, width)]))
    ins = stage(moves, in_sems)
    leaving = []
    for half, out in enumerate(outs):
        wait(ins[2 * half:2 * half + 2])
        leaving.append(pltpu.make_async_copy(held.at[half], out, out_sems.at[half]))
        leaving[-1].start()
    wait(leaving)


def pack(keys, values):
    return call(
        pack_kernel, "pack", [shape(*keys.shape)] * 2, (keys, values),
        [pltpu.VMEM((2, *keys.shape), BF), pltpu.SemaphoreType.DMA((4,)), pltpu.SemaphoreType.DMA((2,))],
        limit=FIRST_BYTES)


def add_middle_kernel(mid_ref, far_ref, out):
    trim = mid_ref.shape[0] - far_ref.shape[0]
    out[:trim, :] = mid_ref[:trim, :]
    out[trim:, :] = (mid_ref[trim:, :].astype(F32) + far_ref[...].astype(F32)).astype(BF)


def add_middle(mid, far):
    return call(add_middle_kernel, "add_middle", [shape(*mid.shape)], (mid, far), [],
                [VMEM] * 2, [VMEM])[0]


def add_last_kernel(near_ref, got_ref, straight, crossed):
    core = lax.rem(lax.axis_index("ctx"), 2)
    tokens = straight.shape[0]
    for out, shard in ((straight, core), (crossed, 1 - core)):
        at = rows(shard * tokens, tokens)
        out[...] = (near_ref[at, :].astype(F32) + got_ref[at, :].astype(F32)).astype(BF)


def add_last(near, got):
    tokens, width = near.shape[0] // 2, near.shape[1]
    return call(add_last_kernel, "add_last", [shape(tokens, width)] * 2, (near, got), [],
                [VMEM] * 2, [VMEM] * 2)


def lay_heads_kernel(blank_last, *refs):
    parts, (out, held, in_sems, out_sems) = refs[:-4], refs[-4:]
    core = lax.rem(lax.axis_index("ctx"), 2)
    moves = []
    for n, part in enumerate(parts):
        half = core if n % 2 == 0 else 1 - core
        moves.append((part, held.at[:, cols((n // 2 * HALF + half) * QW, QW)]))
    wait(stage(moves, in_sems))
    if blank_last:
        @pl.when(lax.axis_index("pipe") == lax.axis_size("pipe") - 1)
        def _():
            held[...] = jnp.zeros_like(held)
    wait(stage([(held, out)], out_sems))


def lay_heads(parts, blank_last):
    tokens = parts[0].shape[0]
    return call(
        functools.partial(lay_heads_kernel, blank_last), "lay_heads", [shape(tokens, H * HD)], parts,
        [pltpu.VMEM((tokens, H * HD), BF),
         pltpu.SemaphoreType.DMA((len(parts),)),
         pltpu.SemaphoreType.DMA((1,))])[0]


def lay_kv_kernel(*refs):
    parts, (key_out, value_out, held, in_sems, out_sems) = refs[:-5], refs[-5:]
    core = lax.rem(lax.axis_index("ctx"), 2)
    moves = []
    for n, part in enumerate(parts):
        half = core if n % 2 == 0 else 1 - core
        dst = cols((n // 2 * HALF + half) * HD, HD)
        for side in range(2):
            moves.append((part.at[:, pl.ds(side * HD, HD)], held.at[side, :, dst]))
    wait(stage(moves, in_sems))

    @pl.when(lax.axis_index("pipe") == lax.axis_size("pipe") - 1)
    def _():
        held[...] = jnp.zeros_like(held)

    wait(stage([(held.at[0], key_out), (held.at[1], value_out)], out_sems))


def lay_kv(parts):
    tokens = parts[0].shape[0]
    return call(
        lay_kv_kernel, "lay_kv", [shape(tokens, KVH * HD)] * 2, parts,
        [pltpu.VMEM((2, tokens, KVH * HD), BF),
         pltpu.SemaphoreType.DMA((2 * KVH,)),
         pltpu.SemaphoreType.DMA((2,))])


def fold8(op, value):
    return op(value.reshape(value.shape[0] // 8, 8, value.shape[1]), axis=0)


def core_kernel(chunk, tokens, doc_ref, *rest):
    (sources, (o_own, o_pair, dq_own, dq_pair, far_out, mid_out, near_out,
               q_s, g_s, kv_s, kvt_s, acc_s, s_s, p_s, e_s, d_s, o_s, dq_s, sems, out_sems)) = rest[:12], rest[12:]
    q_own, g_own, q_pair, g_pair, k_own, v_own, k_pair, v_pair, mid_own, mid_pair, far_own, far_pair = sources
    me = lax.axis_index("ctx")
    chip, core = lax.div(me, 2), lax.rem(me, 2)
    near_at = 4 * tokens
    first = chunk * HALF

    def part(ref, head, width):
        return ref.at[:, cols((head + core) * width, width)]

    mine, other = rows(core * tokens, tokens), rows((1 - core) * tokens, tokens)
    moves = [
        (part(q_own, 0, QW), q_s.at[mine, :]), (part(q_pair, first, QW), q_s.at[other, :]),
        (part(g_own, 0, QW), g_s.at[mine, :]), (part(g_pair, first, QW), g_s.at[other, :]),
    ]
    kv_sources = (((k_own, 0), (v_own, 0)), ((k_pair, first), (v_pair, first)),
                  ((mid_own, 0), (mid_own, HALF)), ((mid_pair, 0), (mid_pair, HALF)),
                  ((far_own, 0), (far_own, HALF)), ((far_pair, 0), (far_pair, HALF)))
    for n, both in enumerate(kv_sources):
        shard = core if n % 2 == 0 else 1 - core
        at = rows((4 - n // 2 * 2 + shard) * tokens, tokens)
        for side, (ref, head) in enumerate(both):
            moves.append((part(ref, head, HD), kv_s.at[at, pl.ds(side * HD, HD)]))
    copies = [pltpu.make_async_copy(src, dst, sems.at[n]) for n, (src, dst) in enumerate(moves)]
    for copy in copies:
        copy.start()
    acc_s[...] = jnp.zeros_like(acc_s)
    for copy in copies:
        copy.wait()
    blocks = kv_s.shape[0] // BLK
    for at in range(blocks):
        kvt_s[:, at * BLK:(at + 1) * BLK] = kv_s[at * BLK:(at + 1) * BLK, :].T

    def attend(block, at, many, seen):
        span = many * BLK
        base = (block + MOST_BLK + 1 - many) * BLK
        window = rows(base, span)
        tok = rows(block * BLK, BLK)
        key_cols = slice(at * KV2, at * KV2 + HD)
        value_cols = slice(at * KV2 + HD, (at + 1) * KV2)
        q_here, g_here = q_s[tok, at * QW:(at + 1) * QW], g_s[tok, at * QW:(at + 1) * QW]
        qt = jnp.concatenate([q_here[:, n * HD:(n + 1) * HD].T for n in range(GROUP)], axis=1)
        gt = jnp.concatenate([g_here[:, n * HD:(n + 1) * HD].T for n in range(GROUP)], axis=1)
        part = 2 * BLK
        ts = [slice(n * part, (n + 1) * part) for n in range(GROUP * BLK // part)]
        edge = jnp.where(seen < many, F32(-1e30), F32(0.0))
        causal = (lax.broadcasted_iota(jnp.int32, (BLK, BLK), 0)
                  <= lax.broadcasted_iota(jnp.int32, (BLK, BLK), 1))
        causal = jnp.concatenate([causal] * (part // BLK), axis=1)
        keys, values = kv_s[window, key_cols], kv_s[window, value_cols]
        here = [slice(kb * BLK, (kb + 1) * BLK) for kb in range(many)]

        def scores(t):
            s_all = jnp.dot(keys, qt[:, t], preferred_element_type=F32)
            most = None
            for kb in range(many):
                s = s_all[here[kb], :]
                if kb == 0:
                    s = s + edge
                if kb == many - 1:
                    s = jnp.where(causal, s, F32(-1e30))
                s_s[here[kb], t] = s
                top = fold8(jnp.max, s)
                most = top if most is None else jnp.maximum(most, top)
            return jnp.max(most, axis=0, keepdims=True) * F32(SCALE * LOG2E)

        def weights(t, top):
            sums = None
            for kb in range(many):
                e = jnp.exp2(s_s[here[kb], t] * F32(SCALE * LOG2E) - top)
                e_s[here[kb], t] = e.astype(BF)
                total = fold8(jnp.sum, e)
                sums = total if sums is None else sums + total
            return 1.0 / jnp.sum(sums, axis=0, keepdims=True)

        def prob_grads(t):
            p_s[:span, t] = jnp.dot(values, gt[:, t], preferred_element_type=F32)

        def turned(to, t, value):
            low = value.astype(BF)
            for n in range(part // BLK):
                to[tok, t.start + n * BLK:t.start + (n + 1) * BLK] = low[:, n * BLK:(n + 1) * BLK].T
            return low

        def outputs(t, inv):
            ot = jnp.dot(kvt_s[value_cols, cols(base, span)], e_s[:span, t], preferred_element_type=F32) * inv
            ot_low = turned(o_s, t, ot)
            return jnp.sum(gt[:, t].astype(F32) * ot_low.astype(F32), axis=0, keepdims=True)

        def score_grads(t, dots):
            for kb in range(many):
                d_s[here[kb], t] = e_s[here[kb], t] * (p_s[here[kb], t] - dots).astype(BF)

        def query_grads(t, inv):
            turned(dq_s, t, jnp.dot(kvt_s[key_cols, cols(base, span)], d_s[:span, t],
                                    preferred_element_type=F32) * (inv * F32(SCALE)))

        t0, t1 = ts
        top0 = scores(t0)
        top1 = scores(t1)
        inv0 = weights(t0, top0)
        prob_grads(t0)
        dots0 = outputs(t0, inv0)
        inv1 = weights(t1, top1)
        prob_grads(t1)
        dots1 = outputs(t1, inv1)
        inv = jnp.concatenate([inv0, inv1], axis=1)
        gt_low = (gt.astype(F32) * inv).astype(BF)
        qt_low = (qt.astype(F32) * (inv * F32(SCALE))).astype(BF)
        last = (((1,), (1,)), ((), ()))
        acc_s[window, value_cols] += lax.dot_general(e_s[:span, :], gt_low, last, preferred_element_type=F32)
        score_grads(t0, dots0)
        query_grads(t0, inv0)
        score_grads(t1, dots1)
        query_grads(t1, inv1)
        acc_s[window, key_cols] += lax.dot_general(d_s[:span, :], qt_low, last, preferred_element_type=F32)

    def step(block, carry):
        place = chip * (2 * tokens // BLK) + block
        doc = doc_ref[0, place]
        seen = jnp.int32(0)
        for back in range(MOST_BLK):
            there = place - back
            same = (there >= 0) & (doc_ref[0, jnp.maximum(there, 0)] == doc)
            seen += same.astype(jnp.int32)
        for many in range(2, MOST_BLK + 1, 2):
            @pl.when((seen == many) | (seen == many - 1))
            def _():
                attend(block, 0, many, seen)
        return carry

    lax.fori_loop(0, 2 * tokens // BLK, step, 0)
    far_out[...] = acc_s[BLK:2 * tokens, :].astype(BF)
    mid_out[...] = acc_s[2 * tokens:near_at, :].astype(BF)
    near_out[...] = acc_s[near_at:, :].astype(BF)
    leaving = [(o_s, o_own, mine), (o_s, o_pair, other), (dq_s, dq_own, mine), (dq_s, dq_pair, other)]
    copies = [pltpu.make_async_copy(src.at[at, :], dst, out_sems.at[n])
              for n, (src, dst, at) in enumerate(leaving)]
    for copy in copies:
        copy.start()
    for copy in copies:
        copy.wait()


def attend_half(chunk, docs, sources):
    tokens = sources[0].shape[0]
    all_rows = 6 * tokens
    most = MOST_BLK * BLK
    return call(
        functools.partial(core_kernel, chunk, tokens),
        "attend",
        [shape(tokens, QW)] * 4 + [
            shape(2 * tokens - BLK, KV2),
            shape(2 * tokens, KV2),
            shape(2 * tokens, KV2),
        ],
        (docs, *sources),
        [
            pltpu.VMEM((2 * tokens, QW), BF),
            pltpu.VMEM((2 * tokens, QW), BF),
            pltpu.VMEM((all_rows, KV2), BF),
            pltpu.VMEM((KV2, all_rows), BF),
            pltpu.VMEM((all_rows, KV2), F32),
            pltpu.VMEM((most, QW), F32),
            pltpu.VMEM((most, QW), F32),
            pltpu.VMEM((most, QW), BF),
            pltpu.VMEM((most, QW), BF),
            pltpu.VMEM((2 * tokens, QW), BF),
            pltpu.VMEM((2 * tokens, QW), BF),
            pltpu.SemaphoreType.DMA((16,)),
            pltpu.SemaphoreType.DMA((4,)),
        ],
        [SMEM] + [ANY] * 12,
        [ANY] * 4 + [VMEM] * 3,
        ATTEND_BYTES,
        ATTEND_FLOPS)


def shards(queries, key_rows, value_rows, out_grad, doc_blocks):
    peers = lax.axis_size("ctx")
    sections = lax.axis_size("pipe")

    def move(value, chips, cross):
        pairs = [(i, (i // 2 + chips) % (peers // 2) * 2 + ((i % 2) ^ cross)) for i in range(peers)]
        return lax.ppermute(value, "ctx", pairs)

    def pass_back(value, cross):
        pairs = [(p * peers + i, (p - 1) % sections * peers + (i ^ cross))
                 for p in range(sections) for i in range(peers)]
        return lax.ppermute(value, ("pipe", "ctx"), pairs)

    q, g, k, v = queries[0], out_grad[0], key_rows[0], value_rows[0]

    def with_pair(value):
        return [value, move(value, 0, 1)]

    def half_of(value, half):
        width = value.shape[1] // 2
        return value[:, half * width:(half + 1) * width]

    near = pack(k, v)
    mid = [move(kv, 1, 0) for kv in near]
    pairs = [move(value, 0, 1) for value in (q, g, k, v)]
    own = [half_of(value, half) for half in range(2) for value in (q, g, k, v)]
    mid[0], *own = lax.optimization_barrier((mid[0], *own))
    far = [move(kv, 1, 0) for kv in mid]

    def attend(chunk):
        here = own[4 * chunk:4 * chunk + 4]
        return attend_half(chunk, doc_blocks, [
            *here[:2], *pairs[:2], *here[2:], *pairs[2:], *with_pair(mid[chunk]), *with_pair(far[chunk])])

    mid[1], far[0] = lax.optimization_barrier((mid[1], far[0]))
    o_own, o_pair, dq_own, dq_pair, far_part, mid_part, near_part = attend(0)
    mid_before, far_got = mid_part, move(far_part, -1, 0)
    q_parts = [pass_back(dq_own, 0), pass_back(dq_pair, 1)]
    outs = [o_own, move(o_pair, 0, 1)]
    far[1], near_part = lax.optimization_barrier((far[1], near_part))
    o_own, o_pair, dq_own, dq_pair, far_part, mid_part, near_last = attend(1)
    mid_before, near_last, mid_part, *q_parts = lax.optimization_barrier(
        (mid_before, near_last, mid_part, *q_parts))
    far_part, far_got = lax.optimization_barrier((far_part, far_got))
    back = move(add_middle(mid_before, far_got), -1, 0)
    back_last = move(add_middle(mid_part, move(far_part, -1, 0)), -1, 0)
    q_parts += [pass_back(dq_own, 0), pass_back(dq_pair, 1)]
    outs += [o_own, move(o_pair, 0, 1)]
    ours, theirs = add_last(near_part, back)
    kv_parts = [pass_back(ours, 0), pass_back(theirs, 1)]
    near_last, *q_parts = lax.optimization_barrier((near_last, *q_parts))
    ours, theirs = add_last(near_last, back_last)
    ours, theirs, kv_parts[0] = lax.optimization_barrier((ours, theirs, kv_parts[0]))
    kv_parts += [pass_back(ours, 0), pass_back(theirs, 1)]
    attn_out = lay_heads(outs, False)
    grad_query = lay_heads(q_parts, True)
    grad_key, grad_value = lay_kv(kv_parts)
    return attn_out[None], grad_query[None], grad_key[None], grad_value[None]


def solution(mesh):
    tokens = P("pipe", "ctx", None)
    return jax.shard_map(
        shards,
        mesh=mesh,
        in_specs=(tokens, tokens, tokens, tokens, P("pipe", None)),
        out_specs=(tokens, tokens, tokens, tokens),
        check_vma=False,
    )
```

```python
import functools
import math

import jax
import jax.numpy as jnp
from jax import lax
from jax.experimental import pallas as pl
from jax.experimental.pallas import tpu as pltpu
from jax.sharding import PartitionSpec as P

HD = 128
H = 16
KVH = 4
BLK = 128
MOST_BLK = 8

GROUP = H // KVH
HALF = KVH // 2
QW = GROUP * HD
KV2 = 2 * HD
SCALE = 1.0 / math.sqrt(HD)
LOG2E = math.log2(math.e)
SMALL_BYTES = 4 * 1024 * 1024
FIRST_BYTES = 56 * 1024 * 1024
ATTEND_BYTES = 20 * 1024 * 1024
ATTEND_FLOPS = 1000

BF = jnp.bfloat16
F32 = jnp.float32
ANY = pl.BlockSpec(memory_space=pl.ANY)
VMEM = pl.BlockSpec(memory_space=pltpu.VMEM)
SMEM = pl.BlockSpec(memory_space=pltpu.SMEM)


def shape(rows, cols, dtype=BF):
    return jax.ShapeDtypeStruct((rows, cols), dtype)


def cols(start, size):
    return pl.ds(pl.multiple_of(start, HD), size)


def rows(start, size):
    return pl.ds(pl.multiple_of(start, BLK), size)


def call(kernel, name, outs, args, scratch, in_specs=None, out_specs=None, limit=SMALL_BYTES, flops=1000):
    return pl.pallas_call(
        kernel,
        name=name,
        out_shape=outs,
        in_specs=in_specs or [ANY] * len(args),
        out_specs=out_specs or [ANY] * len(outs),
        scratch_shapes=scratch,
        compiler_params=pltpu.CompilerParams(vmem_limit_bytes=limit),
        cost_estimate=pl.CostEstimate(flops=flops, bytes_accessed=1000, transcendentals=0),
    )(*args)


def stage(moves, sems):
    copies = [pltpu.make_async_copy(src, dst, sems.at[n]) for n, (src, dst) in enumerate(moves)]
    for copy in copies:
        copy.start()
    return copies


def wait(copies):
    for copy in copies:
        copy.wait()


def pack_kernel(k_ref, v_ref, *rest):
    outs, (held, in_sems, out_sems) = rest[:2], rest[2:]
    width = k_ref.shape[1] // 2
    moves = []
    for half in range(2):
        for side, ref in enumerate((k_ref, v_ref)):
            moves.append((ref.at[:, pl.ds(half * width, width)], held.at[half, :, pl.ds(side * width, width)]))
    ins = stage(moves, in_sems)
    leaving = []
    for half, out in enumerate(outs):
        wait(ins[2 * half:2 * half + 2])
        leaving.append(pltpu.make_async_copy(held.at[half], out, out_sems.at[half]))
        leaving[-1].start()
    wait(leaving)


def pack(keys, values):
    return call(
        pack_kernel, "pack", [shape(*keys.shape)] * 2, (keys, values),
        [pltpu.VMEM((2, *keys.shape), BF), pltpu.SemaphoreType.DMA((4,)), pltpu.SemaphoreType.DMA((2,))],
        limit=FIRST_BYTES)


def add_middle_kernel(mid_ref, far_ref, out):
    trim = mid_ref.shape[0] - far_ref.shape[0]
    out[:trim, :] = mid_ref[:trim, :]
    out[trim:, :] = (mid_ref[trim:, :].astype(F32) + far_ref[...].astype(F32)).astype(BF)


def add_middle(mid, far):
    return call(add_middle_kernel, "add_middle", [shape(*mid.shape)], (mid, far), [],
                [VMEM] * 2, [VMEM])[0]


def add_last_kernel(near_ref, got_ref, straight, crossed):
    core = lax.rem(lax.axis_index("ctx"), 2)
    tokens = straight.shape[0]
    for out, shard in ((straight, core), (crossed, 1 - core)):
        at = rows(shard * tokens, tokens)
        out[...] = (near_ref[at, :].astype(F32) + got_ref[at, :].astype(F32)).astype(BF)


def add_last(near, got):
    tokens, width = near.shape[0] // 2, near.shape[1]
    return call(add_last_kernel, "add_last", [shape(tokens, width)] * 2, (near, got), [],
                [VMEM] * 2, [VMEM] * 2)


def lay_heads_kernel(blank_last, *refs):
    parts, (out, held, in_sems, out_sems) = refs[:-4], refs[-4:]
    core = lax.rem(lax.axis_index("ctx"), 2)
    moves = []
    for n, part in enumerate(parts):
        half = core if n % 2 == 0 else 1 - core
        moves.append((part, held.at[:, cols((n // 2 * HALF + half) * QW, QW)]))
    wait(stage(moves, in_sems))
    if blank_last:
        @pl.when(lax.axis_index("pipe") == lax.axis_size("pipe") - 1)
        def _():
            held[...] = jnp.zeros_like(held)
    wait(stage([(held, out)], out_sems))


def lay_heads(parts, blank_last):
    tokens = parts[0].shape[0]
    return call(
        functools.partial(lay_heads_kernel, blank_last), "lay_heads", [shape(tokens, H * HD)], parts,
        [pltpu.VMEM((tokens, H * HD), BF),
         pltpu.SemaphoreType.DMA((len(parts),)),
         pltpu.SemaphoreType.DMA((1,))])[0]


def lay_kv_kernel(*refs):
    parts, (key_out, value_out, held, in_sems, out_sems) = refs[:-5], refs[-5:]
    core = lax.rem(lax.axis_index("ctx"), 2)
    moves = []
    for n, part in enumerate(parts):
        half = core if n % 2 == 0 else 1 - core
        dst = cols((n // 2 * HALF + half) * HD, HD)
        for side in range(2):
            moves.append((part.at[:, pl.ds(side * HD, HD)], held.at[side, :, dst]))
    wait(stage(moves, in_sems))

    @pl.when(lax.axis_index("pipe") == lax.axis_size("pipe") - 1)
    def _():
        held[...] = jnp.zeros_like(held)

    wait(stage([(held.at[0], key_out), (held.at[1], value_out)], out_sems))


def lay_kv(parts):
    tokens = parts[0].shape[0]
    return call(
        lay_kv_kernel, "lay_kv", [shape(tokens, KVH * HD)] * 2, parts,
        [pltpu.VMEM((2, tokens, KVH * HD), BF),
         pltpu.SemaphoreType.DMA((2 * KVH,)),
         pltpu.SemaphoreType.DMA((2,))])


def fold8(op, value):
    return op(value.reshape(value.shape[0] // 8, 8, value.shape[1]), axis=0)


def core_kernel(chunk, tokens, doc_ref, *rest):
    (sources, (o_own, o_pair, dq_own, dq_pair, far_out, mid_out, near_out,
               q_s, g_s, kv_s, kvt_s, acc_s, s_s, p_s, e_s, d_s, o_s, dq_s, sems, out_sems)) = rest[:12], rest[12:]
    q_own, g_own, q_pair, g_pair, k_own, v_own, k_pair, v_pair, mid_own, mid_pair, far_own, far_pair = sources
    me = lax.axis_index("ctx")
    chip, core = lax.div(me, 2), lax.rem(me, 2)
    near_at = 4 * tokens
    first = chunk * HALF

    def part(ref, head, width):
        return ref.at[:, cols((head + core) * width, width)]

    mine, other = rows(core * tokens, tokens), rows((1 - core) * tokens, tokens)
    moves = []
    kv_sources = (((k_own, 0), (v_own, 0)), ((k_pair, first), (v_pair, first)),
                  ((mid_own, 0), (mid_own, HALF)), ((mid_pair, 0), (mid_pair, HALF)),
                  ((far_own, 0), (far_own, HALF)), ((far_pair, 0), (far_pair, HALF)))
    for n, both in enumerate(kv_sources):
        shard = core if n % 2 == 0 else 1 - core
        at = rows((4 - n // 2 * 2 + shard) * tokens, tokens)
        for side, (ref, head) in enumerate(both):
            moves.append((part(ref, head, HD), kv_s.at[at, pl.ds(side * HD, HD)]))
    kv_moves = len(moves)
    moves += [
        (part(q_own, 0, QW), q_s.at[mine, :]), (part(q_pair, first, QW), q_s.at[other, :]),
        (part(g_own, 0, QW), g_s.at[mine, :]), (part(g_pair, first, QW), g_s.at[other, :]),
    ]
    copies = stage(moves, sems)
    acc_s[...] = jnp.zeros_like(acc_s)
    wait(copies[:kv_moves])
    blocks = kv_s.shape[0] // BLK
    for at in range(1, blocks):
        kvt_s[:, at * BLK:(at + 1) * BLK] = kv_s[at * BLK:(at + 1) * BLK, :].T
    wait(copies[kv_moves:])

    def attend(block, at, many, seen):
        span = many * BLK
        base = (block + MOST_BLK + 1 - many) * BLK
        window = rows(base, span)
        tok = rows(block * BLK, BLK)
        key_cols = slice(at * KV2, at * KV2 + HD)
        value_cols = slice(at * KV2 + HD, (at + 1) * KV2)
        q_here, g_here = q_s[tok, at * QW:(at + 1) * QW], g_s[tok, at * QW:(at + 1) * QW]
        qt = jnp.concatenate([q_here[:, n * HD:(n + 1) * HD].T for n in range(GROUP)], axis=1)
        gt = jnp.concatenate([g_here[:, n * HD:(n + 1) * HD].T for n in range(GROUP)], axis=1)
        part = 2 * BLK
        ts = [slice(n * part, (n + 1) * part) for n in range(GROUP * BLK // part)]
        edge = jnp.where(seen < many, F32(-1e30), F32(0.0))
        causal = (lax.broadcasted_iota(jnp.int32, (BLK, BLK), 0)
                  <= lax.broadcasted_iota(jnp.int32, (BLK, BLK), 1))
        causal = jnp.concatenate([causal] * (part // BLK), axis=1)
        keys, values = kv_s[window, key_cols], kv_s[window, value_cols]
        here = [slice(kb * BLK, (kb + 1) * BLK) for kb in range(many)]

        def scores(t):
            s_all = jnp.dot(keys, qt[:, t], preferred_element_type=F32)
            most = None
            for kb in range(many):
                s = s_all[here[kb], :]
                if kb == 0:
                    s = s + edge
                if kb == many - 1:
                    s = jnp.where(causal, s, F32(-1e30))
                s_s[here[kb], t] = s
                top = fold8(jnp.max, s)
                most = top if most is None else jnp.maximum(most, top)
            return jnp.max(most, axis=0, keepdims=True) * F32(SCALE * LOG2E)

        def weights(t, top):
            sums = None
            for kb in range(many):
                e = jnp.exp2(s_s[here[kb], t] * F32(SCALE * LOG2E) - top)
                e_s[here[kb], t] = e.astype(BF)
                total = fold8(jnp.sum, e)
                sums = total if sums is None else sums + total
            return 1.0 / jnp.sum(sums, axis=0, keepdims=True)

        def prob_grads(t):
            p_s[:span, t] = jnp.dot(values, gt[:, t], preferred_element_type=F32)

        def turned(to, t, value):
            low = value.astype(BF)
            for n in range(part // BLK):
                to[tok, t.start + n * BLK:t.start + (n + 1) * BLK] = low[:, n * BLK:(n + 1) * BLK].T
            return low

        def outputs(t, inv):
            ot = jnp.dot(kvt_s[value_cols, cols(base, span)], e_s[:span, t], preferred_element_type=F32) * inv
            ot_low = turned(o_s, t, ot)
            return jnp.sum(gt[:, t].astype(F32) * ot_low.astype(F32), axis=0, keepdims=True)

        def score_grads(t, dots):
            for kb in range(many):
                d_s[here[kb], t] = e_s[here[kb], t] * (p_s[here[kb], t] - dots).astype(BF)

        def query_grads(t, inv):
            turned(dq_s, t, jnp.dot(kvt_s[key_cols, cols(base, span)], d_s[:span, t],
                                    preferred_element_type=F32) * (inv * F32(SCALE)))

        t0, t1 = ts
        top0 = scores(t0)
        top1 = scores(t1)
        inv0 = weights(t0, top0)
        prob_grads(t0)
        dots0 = outputs(t0, inv0)
        inv1 = weights(t1, top1)
        prob_grads(t1)
        dots1 = outputs(t1, inv1)
        inv = jnp.concatenate([inv0, inv1], axis=1)
        gt_low = (gt.astype(F32) * inv).astype(BF)
        qt_low = (qt.astype(F32) * (inv * F32(SCALE))).astype(BF)
        last = (((1,), (1,)), ((), ()))
        acc_s[window, value_cols] += lax.dot_general(e_s[:span, :], gt_low, last, preferred_element_type=F32)
        score_grads(t0, dots0)
        query_grads(t0, inv0)
        score_grads(t1, dots1)
        query_grads(t1, inv1)
        acc_s[window, key_cols] += lax.dot_general(d_s[:span, :], qt_low, last, preferred_element_type=F32)

    def step(block, carry):
        place = chip * (2 * tokens // BLK) + block
        doc = doc_ref[0, place]
        seen = jnp.int32(0)
        for back in range(MOST_BLK):
            there = place - back
            same = (there >= 0) & (doc_ref[0, jnp.maximum(there, 0)] == doc)
            seen += same.astype(jnp.int32)
        for many in range(2, MOST_BLK + 1, 2):
            @pl.when((seen == many) | (seen == many - 1))
            def _():
                attend(block, 0, many, seen)
        return carry

    lax.fori_loop(0, 2 * tokens // BLK, step, 0)
    far_out[...] = acc_s[BLK:2 * tokens, :].astype(BF)
    mid_out[...] = acc_s[2 * tokens:near_at, :].astype(BF)
    near_out[...] = acc_s[near_at:, :].astype(BF)
    leaving = [(o_s, o_own, mine), (o_s, o_pair, other), (dq_s, dq_own, mine), (dq_s, dq_pair, other)]
    copies = [pltpu.make_async_copy(src.at[at, :], dst, out_sems.at[n])
              for n, (src, dst, at) in enumerate(leaving)]
    for copy in copies:
        copy.start()
    for copy in copies:
        copy.wait()


def attend_half(chunk, docs, sources):
    tokens = sources[0].shape[0]
    all_rows = 6 * tokens
    most = MOST_BLK * BLK
    return call(
        functools.partial(core_kernel, chunk, tokens),
        "attend",
        [shape(tokens, QW)] * 4 + [
            shape(2 * tokens - BLK, KV2),
            shape(2 * tokens, KV2),
            shape(2 * tokens, KV2),
        ],
        (docs, *sources),
        [
            pltpu.VMEM((2 * tokens, QW), BF),
            pltpu.VMEM((2 * tokens, QW), BF),
            pltpu.VMEM((all_rows, KV2), BF),
            pltpu.VMEM((KV2, all_rows), BF),
            pltpu.VMEM((all_rows, KV2), F32),
            pltpu.VMEM((most, QW), F32),
            pltpu.VMEM((most, QW), F32),
            pltpu.VMEM((most, QW), BF),
            pltpu.VMEM((most, QW), BF),
            pltpu.VMEM((2 * tokens, QW), BF),
            pltpu.VMEM((2 * tokens, QW), BF),
            pltpu.SemaphoreType.DMA((16,)),
            pltpu.SemaphoreType.DMA((4,)),
        ],
        [SMEM] + [ANY] * 12,
        [ANY] * 4 + [VMEM] * 3,
        ATTEND_BYTES,
        ATTEND_FLOPS)


def shards(queries, key_rows, value_rows, out_grad, doc_blocks):
    peers = lax.axis_size("ctx")
    sections = lax.axis_size("pipe")

    def move(value, chips, cross):
        pairs = [(i, (i // 2 + chips) % (peers // 2) * 2 + ((i % 2) ^ cross)) for i in range(peers)]
        return lax.ppermute(value, "ctx", pairs)

    def pass_back(value, cross):
        pairs = [(p * peers + i, (p - 1) % sections * peers + (i ^ cross))
                 for p in range(sections) for i in range(peers)]
        return lax.ppermute(value, ("pipe", "ctx"), pairs)

    q, g, k, v = queries[0], out_grad[0], key_rows[0], value_rows[0]

    def with_pair(value):
        return [value, move(value, 0, 1)]

    def half_of(value, half):
        width = value.shape[1] // 2
        return value[:, half * width:(half + 1) * width]

    near = pack(k, v)
    mid = [move(kv, 1, 0) for kv in near]
    pairs = [move(value, 0, 1) for value in (q, g, k, v)]
    own = [half_of(value, half) for half in range(2) for value in (q, g, k, v)]
    mid[0], *own = lax.optimization_barrier((mid[0], *own))
    far = [move(kv, 1, 0) for kv in mid]

    def attend(chunk):
        here = own[4 * chunk:4 * chunk + 4]
        return attend_half(chunk, doc_blocks, [
            *here[:2], *pairs[:2], *here[2:], *pairs[2:], *with_pair(mid[chunk]), *with_pair(far[chunk])])

    mid[1], far[0] = lax.optimization_barrier((mid[1], far[0]))
    o_own, o_pair, dq_own, dq_pair, far_part, mid_part, near_part = attend(0)
    mid_before, far_got = mid_part, move(far_part, -1, 0)
    q_parts = [pass_back(dq_own, 0), pass_back(dq_pair, 1)]
    outs = [o_own, move(o_pair, 0, 1)]
    far[1], near_part = lax.optimization_barrier((far[1], near_part))
    o_own, o_pair, dq_own, dq_pair, far_part, mid_part, near_last = attend(1)
    mid_before, near_last, mid_part, *q_parts = lax.optimization_barrier(
        (mid_before, near_last, mid_part, *q_parts))
    far_part, far_got = lax.optimization_barrier((far_part, far_got))
    back = move(add_middle(mid_before, far_got), -1, 0)
    back_last = move(add_middle(mid_part, move(far_part, -1, 0)), -1, 0)
    q_parts += [pass_back(dq_own, 0), pass_back(dq_pair, 1)]
    outs += [o_own, move(o_pair, 0, 1)]
    ours, theirs = add_last(near_part, back)
    kv_parts = [pass_back(ours, 0), pass_back(theirs, 1)]
    near_last, *q_parts = lax.optimization_barrier((near_last, *q_parts))
    ours, theirs = add_last(near_last, back_last)
    ours, theirs, kv_parts[0] = lax.optimization_barrier((ours, theirs, kv_parts[0]))
    kv_parts += [pass_back(ours, 0), pass_back(theirs, 1)]
    attn_out = lay_heads(outs, False)
    grad_query = lay_heads(q_parts, True)
    grad_key, grad_value = lay_kv(kv_parts)
    return attn_out[None], grad_query[None], grad_key[None], grad_value[None]


def solution(mesh):
    tokens = P("pipe", "ctx", None)
    return jax.shard_map(
        shards,
        mesh=mesh,
        in_specs=(tokens, tokens, tokens, tokens, P("pipe", None)),
        out_specs=(tokens, tokens, tokens, tokens),
        check_vma=False,
    )
```
